512 devices in a mesh: band: 8 (over z), grid: 64 (over y, x, core).
Axes of the slice: x: 4, y: 8, z: 8, core: 2. Of those that a mesh axis runs over, the one named last changes fastest.
Arguments:
- psi_g: float32 [2, 16, 3072, 128], P(None, 'band', 'grid'), may hold values from -6 to 6
- col_index: int32 [3072], P('grid'), may hold values from 0 to 16383, as said below
- v_local: float32 [128, 128, 128], P('grid'), may hold values from -4 to 4
- proj_values: float32 [16384, 18, 128], P('grid'), may hold values from -0.15625 to 0.15625
- pair_atom: int32 [16384], P('grid'), may hold values from 0 to 512, as said below
- pair_row: int32 [16384], P('grid'), may hold values from 0 to 16383, as said below
- d_matrices: float32 [512, 18, 18], P('grid'), may hold values from -1.5 to 1.5
- occupations: float32 [16], P('band'), may hold values from 0.2 to 2
Outputs:
- h_psi: float32 [2, 16, 3072, 128], P(None, 'band', 'grid')
- density: float32 [128, 128, 128], P('grid')
The draws below stay inside these ranges and needn't reach their ends.
Inputs may be any that keep to these rules, and one draw needn't show every extreme that they name: `col_index`: distinct positions; the set is the 3072 positions of smallest fy^2 + fz^2, ties broken by the seed, dealt to the devices in a random order. `pair_atom`: an atom, or 512 for an empty slot. On each grid device the live slots come first; their number is an eighth, a quarter or all of its 256 slots, and some device has all slots live. The live slots of one atom lie on at most three devices of grid that follow one another cyclically (the last device is followed by the first). `pair_row`: the row lies in the planes of the device that holds the slot: device i of grid holds x from i * 2 to (i + 1) * 2 - 1. Rows may repeat.
All inputs are finite; a program needn't handle non-finite values.
Results may differ from the reference program's by a relative error of at most 0.0001.
Values sent between devices are 32-bit elements; how exact they have to be, the bound alone decides.
A program may use at most 64 MiB of HBM per device.

```python
import jax
import jax.numpy as jnp
from jax import lax

N = 128
NPROJ = 18
ATOM_DEV = 8
PAIRS_DEV = 256
BANDS = 16
COLS = 3072
ATOMS = 512
PAIRS = 16384
PLANES = 2
N_GRID = 64


def pair_layout(key):
    positions = jnp.arange(PAIRS, dtype=jnp.int32)
    holder = positions // PAIRS_DEV
    slot_pos = positions % PAIRS_DEV
    sub_keys = jax.random.split(key, 6)
    level_table = jnp.array([1, 2, 8], dtype=jnp.int32)
    levels = level_table[jax.random.randint(sub_keys[0], (N_GRID,), 0, 3)]
    full_device = jax.random.randint(sub_keys[1], (), 0, N_GRID)
    levels = jnp.where(jnp.arange(N_GRID, dtype=jnp.int32) == full_device, 8, levels)
    live_mask = slot_pos < PAIRS_DEV * levels[holder] // 8
    neighbour = (holder + jax.random.randint(sub_keys[2], (PAIRS,), -1, 2) + N_GRID) % N_GRID
    member = jax.random.randint(sub_keys[3], (PAIRS,), 0, ATOM_DEV)
    labels = jax.random.permutation(sub_keys[4], ATOMS)
    atom_ids = jnp.where(live_mask, labels[neighbour * ATOM_DEV + member], ATOMS)
    row_ids = holder * PLANES * N + jax.random.randint(sub_keys[5], (PAIRS,), 0, PLANES * N)
    return (atom_ids.astype(jnp.int32), row_ids.astype(jnp.int32))


def draw_pair_atom(key, part):
    return pair_layout(key)[0]


def draw_pair_row(key, part):
    return pair_layout(key)[1]


def draw_col_index(key, part):
    key = jax.random.fold_in(key, 11)
    first_key, second_key = jax.random.split(key)
    positions = jnp.arange(N * N, dtype=jnp.int32)
    first_freq = positions // N
    second_freq = positions % N
    first_freq = jnp.where(first_freq >= N // 2, first_freq - N, first_freq)
    second_freq = jnp.where(second_freq >= N // 2, second_freq - N, second_freq)
    radius = first_freq * first_freq + second_freq * second_freq
    tie_break = jax.random.permutation(first_key, N * N)
    score = radius * (N * N) + tie_break
    order = jnp.argsort(score, stable=True)
    chosen = order[:COLS]
    return jax.random.permutation(second_key, chosen).astype(jnp.int32)


def block_scale(rng, dims, cuts, low, largest):
    def one(position, shards_of):
        heights = jax.random.uniform(jax.random.fold_in(jax.random.fold_in(rng, 6), position), (shards_of,), jnp.float32, low / len(cuts), largest / len(cuts))
        return jnp.repeat(jnp.exp(heights), dims[position] // shards_of).reshape((-1,) + (1,) * (len(dims) - position - 1))

    loudness = one(*cuts[0])
    for cut in cuts[1:]:
        loudness = loudness * one(*cut)
    return loudness


def normal_values(stream_key, dims, deviation, reach, pieces=(), kind=jnp.bfloat16):
    values = jax.random.normal(stream_key, dims, jnp.float32) * deviation
    if len(pieces) > 0:
        values = block_scale(stream_key, dims, pieces, -0.22, 0.18) * values
    return jnp.clip(values, min=-reach, max=reach).astype(kind)


def setup_inputs(seed: int = 0) -> dict:
    streams_of = jax.random.split(jax.random.key(seed), 9)
    return {
        "psi_g": normal_values(streams_of[0], (2, BANDS, COLS, N), 1.0, 6.0, ((1, 8), (2, 64)), jnp.float32),
        "col_index": draw_col_index(jax.random.fold_in(streams_of[8], 71), 0),
        "v_local": normal_values(streams_of[2], (N, N, N), 1.0, 4.0, ((0, 64),), jnp.float32),
        "proj_values": normal_values(streams_of[3], (PAIRS, NPROJ, N), (10 * N) ** -0.5, 0.15625, ((0, 64),), jnp.float32),
        "pair_atom": draw_pair_atom(jax.random.fold_in(streams_of[8], 71), 0),
        "pair_row": draw_pair_row(jax.random.fold_in(streams_of[8], 71), 0),
        "d_matrices": normal_values(streams_of[6], (ATOMS, NPROJ, NPROJ), NPROJ ** -0.5, 1.5, ((0, 64),), jnp.float32),
        "occupations": jnp.clip(0.2 + 1.8 * jax.random.uniform(streams_of[7], (BANDS,), jnp.float32) ** block_scale(streams_of[7], (BANDS,), ((0, 8),), -0.2, 0.2), 0.2, 2.0),
    }


KINETIC = 0.0005


def signed_freq(index):
    return jnp.where(index >= N // 2, index - N, index)


def reference(psi_g, col_index, v_local, proj_values, pair_atom, pair_row, d_matrices, occupations):
    high = lax.Precision.HIGHEST
    gy_freq = signed_freq(col_index // N)
    gz_freq = signed_freq(col_index % N)
    gx_freq = signed_freq(jnp.arange(N, dtype=jnp.int32))
    square = (gy_freq * gy_freq + gz_freq * gz_freq)[:, None] + (gx_freq * gx_freq)[None, :]
    kinetic = KINETIC * square.astype(jnp.float32)
    v_rows = v_local.reshape(N * N, N)

    def project(rows):
        coeff_pair = jnp.einsum("piz,pz->pi", proj_values, rows[pair_row], precision=high)
        summed = jax.ops.segment_sum(coeff_pair, pair_atom, num_segments=ATOMS + 1)[:ATOMS]
        applied = jnp.einsum("aij,aj->ai", d_matrices, summed, precision=high)
        padded = jnp.concatenate([applied, jnp.zeros((1, NPROJ), applied.dtype)], axis=0)
        added = jnp.einsum("piz,pi->pz", proj_values, padded[pair_atom], precision=high)
        return v_rows * rows + jnp.zeros_like(rows).at[pair_row].add(added)

    def one_band(density, inputs):
        coeffs, occupy = inputs
        values = lax.complex(coeffs[0], coeffs[1])
        box = jnp.zeros((N * N, N), values.dtype).at[col_index].set(values)
        cube = box.reshape(N, N, N).transpose(2, 0, 1)
        field = jnp.fft.ifftn(cube, norm="ortho")
        real_rows = jnp.real(field).reshape(N * N, N)
        imag_rows = jnp.imag(field).reshape(N * N, N)
        density = density + occupy * (real_rows * real_rows + imag_rows * imag_rows).reshape(N, N, N)
        h_field = lax.complex(project(real_rows), project(imag_rows)).reshape(N, N, N)
        spectrum = jnp.fft.fftn(h_field, norm="ortho")
        flat = spectrum.transpose(1, 2, 0).reshape(N * N, N)[col_index]
        result = jnp.stack([jnp.real(flat), jnp.imag(flat)]) + kinetic[None] * coeffs
        return density, result

    start = jnp.zeros((N, N, N), jnp.float32)
    density, outputs = lax.scan(one_band, start, (psi_g.transpose(1, 0, 2, 3), occupations))
    return outputs.transpose(1, 0, 2, 3), density
```

```python
import functools

import jax
import jax.numpy as jnp
import numpy as np
from jax import lax
from jax.experimental import pallas as pl
from jax.experimental.pallas import tpu as pltpu
from jax.sharding import PartitionSpec as P

MESH = pl.DeviceIdType.MESH
F32 = jnp.float32
BF16 = jnp.bfloat16
KINETIC = 0.0005

N = 128
BOX = 64
PLANES = 2
BANDS = 2
COLS = 48
SLOT = 64
PROJ = 18
PAIRS = 256
ATOMS = 8
COMBOS = 4
ROWS = PLANES * N


def split(table):
    high = table.astype(jnp.bfloat16)
    low = (table - high.astype(np.float64)).astype(jnp.bfloat16)
    return np.stack([high, low])


def tables(grid_count):
    scale = 1.0 / np.sqrt(N)
    pos = np.arange(N)
    box = np.arange(BOX)
    freq = np.where(box >= BOX // 2, box - BOX, box)

    def cos_sin(left, right):
        angle = 2.0 * np.pi / N * (np.outer(left, right) % N)
        return np.cos(angle) * scale, np.sin(angle) * scale

    cos_x, sin_x = cos_sin(pos, pos)
    x_table = np.zeros((grid_count, 2, PLANES, 2, N))
    cos_r = cos_x.reshape(grid_count, PLANES, N)
    sin_r = sin_x.reshape(grid_count, PLANES, N)
    x_table[:, 0, :, 0] = cos_r
    x_table[:, 0, :, 1] = -sin_r
    x_table[:, 1, :, 0] = sin_r
    x_table[:, 1, :, 1] = cos_r
    x_table = x_table.reshape(2 * N, 2 * N)
    cos_y, sin_y = cos_sin(freq, pos)
    y_table = np.zeros((BANDS, BOX, 2, BANDS, N))
    for band in range(BANDS):
        y_table[band, :, 0, band] = cos_y
        y_table[band, :, 1, band] = sin_y
    y_back = y_table.transpose(3, 4, 2, 0, 1).reshape(BANDS * N, 2 * BANDS * BOX)
    y_table = y_table.reshape(BANDS * BOX, 2 * BANDS * N)
    cos_z, sin_z = cos_sin(pos, freq)
    z_table = np.block([[cos_z, -sin_z], [sin_z, cos_z]])
    return [split(t) for t in (x_table, y_table, y_back, z_table, z_table.T)]


def halves(value):
    high = value.astype(BF16)
    low = (value - high.astype(F32)).astype(BF16)
    return high, low


def mm(left, right, dims=((1,), (0,))):
    return lax.dot_general(left, right, (dims, ((), ())), preferred_element_type=F32)


NT = ((1,), (1,))
TN = ((0,), (0,))


def iota(shape, dim):
    return lax.broadcasted_iota(jnp.int32, shape, dim)


def make_kernel(grid_count, band_count):
    peers = grid_count - 1
    half = grid_count // 2

    def kernel(
        psi_ref, col_ref, vloc_ref, proj_ref, atom_ref, row_ref, dmat_ref, occ_ref,
        xt_ref, yt_ref, yb_ref, zt_ref, zb_ref,
        out_ref, dens_ref,
        proj_buf, proj_t, psi_pad, msg1, got1, msg2, got2, code_y, code_z, oh_y, box_ref,
        field, tiles, coeff, near_coeff, near_atom, atom_col, vloc_t,
        d_own, d_mate, d_slot, d_send, summed, applied, added, h_ref,
        dens_loc, dens_part, dens_full, work,
        proj_sem, own_sem, s1, r1, s2, r2, sd, rd, sm, rm, sa, ra, sc, rc, sp, rp, sf, rf,
    ):
        me = lax.axis_index("grid")
        band = lax.axis_index("band")
        core = lax.rem(me, 2)
        chip = me // 2

        def to_grid(src, dst, send, recv, target):
            return pltpu.make_async_remote_copy(
                src_ref=src, dst_ref=dst, send_sem=send, recv_sem=recv,
                device_id={"grid": target}, device_id_type=MESH,
            )

        def to_band(src, dst, send, recv, target):
            return pltpu.make_async_remote_copy(
                src_ref=src, dst_ref=dst, send_sem=send, recv_sem=recv,
                device_id={"band": target}, device_id_type=MESH,
            )

        def settle(ref, sem):
            pltpu.make_async_copy(ref, ref, sem).wait()

        barrier = pltpu.get_barrier_semaphore()

        def greet_grid(step, carry):
            pl.semaphore_signal(
                barrier, inc=1, device_id={"grid": lax.rem(me + step, grid_count)},
                device_id_type=MESH,
            )
            return carry

        def greet_band(step, carry):
            pl.semaphore_signal(
                barrier, inc=1, device_id={"band": lax.rem(band + step, band_count)},
                device_id_type=MESH,
            )
            return carry

        proj_copy = pltpu.make_async_copy(proj_ref, proj_buf, proj_sem)
        proj_copy.start()
        lax.fori_loop(1, grid_count, greet_grid, 0)
        if band_count > 1:
            lax.fori_loop(1, band_count, greet_band, 0)

        psi_pad[...] = jnp.zeros_like(psi_pad)
        for member in range(BANDS):
            for part in range(2):
                psi_pad[member * SLOT : member * SLOT + COLS, part * N : (part + 1) * N] = psi_ref[
                    part, member
                ]
        psi_hi, psi_lo = halves(psi_pad[...])
        spread = mm(xt_ref[0], psi_hi, NT) + mm(xt_ref[1], psi_hi, NT) + mm(xt_ref[0], psi_lo, NT)
        work[...] = jnp.zeros_like(work)
        work[0:1, 0:COLS] = col_ref[...].astype(F32)
        codes = jnp.broadcast_to(work[0:1, :], (8, N))
        sub = iota((8, N), 0) % 4
        lane = iota((8, N), 1)
        pattern = jnp.where(
            sub == 0,
            pltpu.roll(codes, 48, 1),
            jnp.where(sub == 1, pltpu.roll(codes, 32, 1), pltpu.roll(codes, 16, 1)),
        )
        pattern = jnp.where((lane >= COLS) & (lane < SLOT) & (sub < 3), pattern, 0.0)
        for pair in range(grid_count // 2):
            both = spread[8 * pair : 8 * pair + 8] + pattern
            msg1[2 * pair] = both[0:4]
            msg1[2 * pair + 1] = both[4:8]
        got1[me] = msg1[me]
        for q in range(3):
            d_send[q] = dmat_ref[q]
        d_own[chip] = d_send[...]

        pl.semaphore_wait(barrier, peers + band_count - 1)

        def send1(step, carry):
            target = lax.rem(me + step, grid_count)
            to_grid(msg1.at[target], got1.at[me], s1, r1, target).start()
            return carry

        lax.fori_loop(1, grid_count, send1, 0)
        near = [lax.rem(me + off + grid_count, grid_count) for off in (1, -1, 2, -2)]
        atom_copies = [
            to_grid(atom_ref, near_atom.at[i], sa.at[i], ra.at[i], near[i]) for i in range(4)
        ]
        for copy in atom_copies:
            copy.start()

        def send_d(step, carry):
            other = lax.rem(chip + step, half)
            to_grid(d_send, d_own.at[chip], sd, rd, 2 * other + core).start()
            return carry

        lax.fori_loop(1, half, send_d, 0)

        for plane in range(PLANES):
            vloc_t[:, plane * N : (plane + 1) * N] = vloc_ref[plane].T
        atom_row = atom_ref[...].astype(F32)
        for part in range(2):
            atom_col[part * N : (part + 1) * N, :] = jnp.broadcast_to(
                atom_row[:, part * N : (part + 1) * N], (N, N)
            ).T
        proj_copy.wait()
        for i in range(PROJ):
            for part in range(2):
                proj_t[i, :, part * N : (part + 1) * N] = proj_buf[
                    part * N : (part + 1) * N, i, :
                ].T

        settle(got1.at[pl.ds(0, peers)], r1)
        rows = [got1[:, r, :] for r in range(3)]
        wide = iota((grid_count, N), 1)
        low = wide % SLOT
        code = jnp.where(
            low < 16,
            pltpu.roll(rows[0], 80, 1),
            jnp.where(low < 32, pltpu.roll(rows[1], 96, 1), pltpu.roll(rows[2], 112, 1)),
        )
        code = jnp.where(wide < SLOT, code, pltpu.roll(code, SLOT, 1)).astype(jnp.int32)
        valid = low < COLS
        code_y[...] = jnp.where(valid, ((code // N) % BOX) + jnp.where(wide < SLOT, 0, BOX), -1)
        code_z[...] = jnp.where(valid, code % BOX, -1)

        box_ref[...] = jnp.zeros_like(box_ref)
        row_id = iota((BANDS * BOX, N), 0)
        z_id = iota((BOX, N), 0)

        def fill(chunk, carry):
            base = pl.multiple_of(chunk * 8, 8)
            ys = code_y[pl.ds(base, 8), :]
            zs = code_z[pl.ds(base, 8), :]
            total = jnp.zeros((2 * PLANES * BOX, BANDS * BOX), F32)
            for pair in range(4):
                picks, highs, lows = [], [], []
                for j in (2 * pair, 2 * pair + 1):
                    picker = jnp.where(row_id == ys[j : j + 1], 1.0, 0.0).astype(BF16)
                    oh_y[base + j] = picker
                    picks.append(picker)
                    data = got1[base + j]
                    high = data.astype(BF16).astype(F32)
                    rest = data - high
                    at = z_id == zs[j : j + 1]
                    highs.append(
                        jnp.concatenate(
                            [jnp.where(at, high[r : r + 1], 0.0) for r in range(4)], axis=0
                        ).astype(BF16)
                    )
                    lows.append(
                        jnp.concatenate(
                            [jnp.where(at, rest[r : r + 1], 0.0) for r in range(4)], axis=0
                        ).astype(BF16)
                    )
                pick = jnp.concatenate(picks, axis=1)
                total += mm(jnp.concatenate(highs, axis=1), pick, NT)
                total += mm(jnp.concatenate(lows, axis=1), pick, NT)
            box_ref[...] += total
            return carry

        lax.fori_loop(0, grid_count // 8, fill, 0)

        box_hi, box_lo = halves(box_ref[...])
        turned = mm(box_hi, yt_ref[0]) + mm(box_lo, yt_ref[0]) + mm(box_hi, yt_ref[1])
        mid, end = PLANES * BOX, BANDS * N
        part_re = turned[:mid, :end] - turned[mid:, end:]
        part_im = turned[:mid, end:] + turned[mid:, :end]
        for plane in range(PLANES):
            here = slice(plane * BOX, (plane + 1) * BOX)
            value = jnp.concatenate([part_re[here], part_im[here]], axis=0)
            v_hi, v_lo = halves(value)
            wave = mm(zt_ref[0], v_hi) + mm(zt_ref[1], v_hi) + mm(zt_ref[0], v_lo)
            for part in range(2):
                for member in range(BANDS):
                    first = (part * BANDS + member) * N
                    field[first : first + N, plane * N : (plane + 1) * N] = wave[
                        part * N : (part + 1) * N, member * N : (member + 1) * N
                    ]

        dens_t = jnp.zeros((N, ROWS), F32)
        for member in range(BANDS):
            real = field[member * N : (member + 1) * N, :]
            imag = field[(BANDS + member) * N : (BANDS + member + 1) * N, :]
            dens_t += occ_ref[0, member] * (real * real + imag * imag)
        for plane in range(PLANES):
            dens_loc[plane * N : (plane + 1) * N, :] = dens_t[:, plane * N : (plane + 1) * N].T
        share = ROWS // band_count

        def send_part(step, carry):
            target = lax.rem(band + step, band_count)
            first = pl.multiple_of(target * share, share)
            to_band(dens_loc.at[pl.ds(first, share)], dens_part.at[band], sp, rp, target).start()
            return carry

        if band_count > 1:
            lax.fori_loop(1, band_count, send_part, 0)

        local_row = row_ref[...] - me * ROWS
        row_pick = jnp.where(iota((ROWS, PAIRS), 0) == local_row, 1.0, 0.0).astype(BF16)
        f_hi, f_lo = halves(field[...])
        tiles[...] = mm(f_hi, row_pick) + mm(f_lo, row_pick)

        def project(step, carry):
            found = []
            for k in range(2):
                values = proj_t[2 * step + k]
                for combo in range(COMBOS):
                    found.append(
                        jnp.sum(values * tiles[combo * N : (combo + 1) * N, :], axis=0, keepdims=True)
                    )
            coeff[pl.ds(pl.multiple_of(step * 8, 8), 8), :] = jnp.concatenate(found, axis=0)
            return carry

        lax.fori_loop(0, PROJ // 2, project, 0)
        coeff_copies = [
            to_grid(coeff, near_coeff.at[i], sc.at[i], rc.at[i], near[i]) for i in range(4)
        ]
        for copy in coeff_copies:
            copy.start()

        if band_count > 1:
            settle(dens_part.at[pl.ds(0, band_count - 1)], rp)
        mine = pl.ds(pl.multiple_of(band * share, share), share)
        dens_part[band] = dens_loc[mine, :]
        whole = dens_part[0]
        for other in range(1, band_count):
            whole += dens_part[other]
        dens_full[mine, :] = whole

        def send_full(step, carry):
            target = lax.rem(band + step, band_count)
            to_band(dens_full.at[mine], dens_full.at[mine], sf, rf, target).start()
            return carry

        if band_count > 1:
            lax.fori_loop(1, band_count, send_full, 0)

        settle(d_own.at[pl.ds(0, half - 1)], rd)
        mate = to_grid(d_own, d_mate, sm, rm, 2 * chip + 1 - core)
        mate.start()
        place = iota((half * ATOMS, PAIRS), 0)
        atom_base = (place // ATOMS) * (2 * ATOMS) + place % ATOMS
        atoms = atom_ref[...]
        own_pick = jnp.where(atom_base + core * ATOMS == atoms, 1.0, 0.0).astype(BF16)
        mate_pick = jnp.where(atom_base + (1 - core) * ATOMS == atoms, 1.0, 0.0).astype(BF16)
        for q in range(3):
            d_hi, d_lo = halves(d_own[:, q].reshape(half * ATOMS, N))
            d_slot[q * N : (q + 1) * N, :] = mm(d_hi, own_pick, TN) + mm(d_lo, own_pick, TN)
        mate.wait_recv()
        for q in range(3):
            d_hi, d_lo = halves(d_mate[:, q].reshape(half * ATOMS, N))
            d_slot[q * N : (q + 1) * N, :] += mm(d_hi, mate_pick, TN) + mm(d_lo, mate_pick, TN)

        for copy in atom_copies:
            copy.wait_recv()
        column = jnp.concatenate([atom_col[...], atom_col[...]], axis=1)

        def same(other_row):
            return jnp.where(column == other_row.astype(F32), 1.0, 0.0).astype(BF16)

        c_hi, c_lo = halves(coeff[...])
        pick = same(atoms)
        total = mm(c_hi, pick, NT) + mm(c_lo, pick, NT)
        for i in range(4):
            coeff_copies[i].wait_recv()
            c_hi, c_lo = halves(near_coeff[i])
            pick = same(near_atom[i])
            total += mm(c_hi, pick, NT) + mm(c_lo, pick, NT)
        summed[...] = total

        for combo in range(COMBOS):
            value = jnp.zeros((PROJ, PAIRS), F32)
            for j in range(PROJ):
                first = (j // 7) * N + (j % 7) * PROJ
                value += d_slot[first : first + PROJ, :] * summed[
                    j * COMBOS + combo : j * COMBOS + combo + 1, :
                ]
            applied[combo, 0:PROJ, :] = value

        depth = 32

        def spread_back(step, carry):
            first = pl.multiple_of(step * depth, depth)
            totals = [jnp.zeros((depth, PAIRS), F32) for _ in range(COMBOS)]
            for i in range(PROJ):
                values = proj_t[i, pl.ds(first, depth), :]
                for combo in range(COMBOS):
                    totals[combo] += values * applied[combo, i : i + 1, :]
            for combo in range(COMBOS):
                added[pl.ds(pl.multiple_of(combo * N + first, depth), depth), :] = totals[combo]
            return carry

        lax.fori_loop(0, N // depth, spread_back, 0)
        a_hi, a_lo = halves(added[...])
        projected = mm(a_hi, row_pick, NT) + mm(a_lo, row_pick, NT)
        for combo in range(COMBOS):
            here = slice(combo * N, (combo + 1) * N)
            h_ref[here, :] = vloc_t[...] * field[here, :] + projected[here]

        spectra = []
        for plane in range(PLANES):
            lanes = slice(plane * N, (plane + 1) * N)
            value = jnp.concatenate(
                [
                    jnp.concatenate(
                        [
                            h_ref[(part * BANDS + member) * N : (part * BANDS + member + 1) * N, lanes]
                            for member in range(BANDS)
                        ],
                        axis=1,
                    )
                    for part in range(2)
                ],
                axis=0,
            )
            v_hi, v_lo = halves(value)
            spectra.append(mm(zb_ref[0], v_hi) + mm(zb_ref[1], v_hi) + mm(zb_ref[0], v_lo))
        turned = jnp.concatenate(
            [spectra[plane][part * BOX : (part + 1) * BOX] for part in range(2) for plane in range(PLANES)],
            axis=0,
        )
        t_hi, t_lo = halves(turned)
        turned = mm(t_hi, yb_ref[0]) + mm(t_lo, yb_ref[0]) + mm(t_hi, yb_ref[1])
        end = BANDS * BOX
        final = jnp.concatenate(
            [turned[:mid, :end] + turned[mid:, end:], turned[mid:, :end] - turned[:mid, end:]], axis=0
        )
        q_hi, q_lo = halves(final)
        both = jnp.concatenate([q_hi, q_lo], axis=1)

        def take(target):
            picker = oh_y[target]
            found = mm(both, jnp.concatenate([picker, picker], axis=0))
            at = z_id == code_z[pl.ds(target, 1), :]
            msg2[target] = jnp.concatenate(
                [
                    jnp.sum(
                        jnp.where(at, found[r * BOX : (r + 1) * BOX], 0.0), axis=0, keepdims=True
                    )
                    for r in range(4)
                ],
                axis=0,
            )

        def send2(step, carry):
            target = lax.rem(me + step, grid_count)
            take(target)
            to_grid(msg2.at[target], got2.at[me], s2, r2, target).start()
            return carry

        lax.fori_loop(1, grid_count, send2, 0)
        take(me)
        got2[me] = msg2[me]

        if band_count > 1:
            settle(dens_full.at[pl.ds(0, ROWS - share)], rf)
        dens_ref[...] = dens_full[...]
        first_freq = col_ref[...]

        work[...] = jnp.zeros_like(work)
        work[0:1, 0:COLS] = first_freq.astype(F32)
        codes = jnp.broadcast_to(work[0:1, :], (N, N)).T.astype(jnp.int32)[0:COLS]

        def signed(index):
            return jnp.where(index >= N // 2, index - N, index)

        fy, fz, fx = signed(codes // N), signed(codes % N), signed(iota((COLS, N), 1))
        kinetic = KINETIC * (fx * fx + fy * fy + fz * fz).astype(F32)

        settle(got2.at[pl.ds(0, peers)], r2)
        back = got2[...].reshape(grid_count * 4, N).T
        b_hi, b_lo = halves(back)
        result = mm(b_hi, xt_ref[0]) + mm(b_lo, xt_ref[0]) + mm(b_hi, xt_ref[1])
        for part in range(2):
            for member in range(BANDS):
                out_ref[part, member] = (
                    result[member * SLOT : member * SLOT + COLS, part * N : (part + 1) * N]
                    + kinetic * psi_ref[part, member]
                )

        settle(msg1.at[pl.ds(0, peers)], s1)
        settle(msg2.at[pl.ds(0, peers)], s2)
        settle(d_own.at[pl.ds(0, half - 1)], sd)
        mate.wait_send()
        for copy in atom_copies + coeff_copies:
            copy.wait_send()
        if band_count > 1:
            settle(dens_part.at[pl.ds(0, band_count - 1)], sp)
            settle(dens_full.at[pl.ds(0, ROWS - share)], sf)

    return kernel


def solution(mesh):
    grid_count = mesh.shape["grid"]
    band_count = mesh.shape["band"]
    half = grid_count // 2
    constants = tables(grid_count)

    def step(psi_g, col_index, v_local, proj_values, pair_atom, pair_row, d_matrices, occupations):
        d_flat = d_matrices.transpose(0, 2, 1)
        d_flat = jnp.pad(d_flat, ((0, 0), (0, 3), (0, 0))).reshape(ATOMS, 3, 7 * PROJ)
        d_flat = jnp.pad(d_flat, ((0, 0), (0, 0), (0, N - 7 * PROJ))).transpose(1, 0, 2)
        vmem = pl.BlockSpec(memory_space=pltpu.VMEM)
        dma = pltpu.SemaphoreType.DMA
        out, dens = pl.pallas_call(
            make_kernel(grid_count, band_count),
            out_shape=(
                jax.ShapeDtypeStruct(psi_g.shape, F32),
                jax.ShapeDtypeStruct((ROWS, N), F32),
            ),
            in_specs=[
                vmem, vmem, vmem, pl.BlockSpec(memory_space=pl.ANY), vmem, vmem, vmem,
                pl.BlockSpec(memory_space=pltpu.SMEM),
            ]
            + [vmem] * 5,
            out_specs=(vmem, vmem),
            scratch_shapes=[
                pltpu.VMEM((PAIRS, PROJ, N), F32),
                pltpu.VMEM((PROJ, N, PAIRS), F32),
                pltpu.VMEM((BANDS * SLOT, 2 * N), F32),
                pltpu.VMEM((grid_count, 4, N), F32),
                pltpu.VMEM((grid_count, 4, N), F32),
                pltpu.VMEM((grid_count, 4, N), F32),
                pltpu.VMEM((grid_count, 4, N), F32),
                pltpu.VMEM((grid_count, N), jnp.int32),
                pltpu.VMEM((grid_count, N), jnp.int32),
                pltpu.VMEM((grid_count, BANDS * BOX, N), BF16),
                pltpu.VMEM((2 * PLANES * BOX, BANDS * BOX), F32),
                pltpu.VMEM((COMBOS * N, ROWS), F32),
                pltpu.VMEM((COMBOS * N, PAIRS), F32),
                pltpu.VMEM((PROJ * COMBOS, PAIRS), F32),
                pltpu.VMEM((4, PROJ * COMBOS, PAIRS), F32),
                pltpu.VMEM((4, 1, PAIRS), jnp.int32),
                pltpu.VMEM((PAIRS, N), F32),
                pltpu.VMEM((N, ROWS), F32),
                pltpu.VMEM((half, 3, ATOMS, N), F32),
                pltpu.VMEM((half, 3, ATOMS, N), F32),
                pltpu.VMEM((3 * N, PAIRS), F32),
                pltpu.VMEM((3, ATOMS, N), F32),
                pltpu.VMEM((PROJ * COMBOS, PAIRS), F32),
                pltpu.VMEM((COMBOS, 24, PAIRS), F32),
                pltpu.VMEM((COMBOS * N, PAIRS), F32),
                pltpu.VMEM((COMBOS * N, ROWS), F32),
                pltpu.VMEM((ROWS, N), F32),
                pltpu.VMEM((band_count, ROWS // band_count, N), F32),
                pltpu.VMEM((ROWS, N), F32),
                pltpu.VMEM((8, N), F32),
                dma, dma, dma, dma, dma, dma, dma, dma, dma, dma,
                dma((4,)), dma((4,)), dma((4,)), dma((4,)), dma, dma, dma, dma,
            ],
            compiler_params=pltpu.CompilerParams(
                collective_id=0, has_side_effects=True, vmem_limit_bytes=48 << 20
            ),
        )(
            psi_g,
            col_index.reshape(1, COLS),
            v_local,
            proj_values,
            pair_atom.reshape(1, PAIRS),
            pair_row.reshape(1, PAIRS),
            d_flat,
            occupations.reshape(1, BANDS),
            *[jnp.asarray(t) for t in constants],
        )
        return out, dens.reshape(PLANES, N, N)

    return jax.shard_map(
        step,
        mesh=mesh,
        in_specs=(
            P(None, "band", "grid", None),
            P("grid"),
            P("grid", None, None),
            P("grid", None, None),
            P("grid"),
            P("grid"),
            P("grid", None, None),
            P("band"),
        ),
        out_specs=(P(None, "band", "grid", None), P("grid", None, None)),
        check_vma=False,
    )
```

```python
import functools

import jax
import jax.numpy as jnp
import numpy as np
from jax import lax
from jax.experimental import pallas as pl
from jax.experimental.pallas import tpu as pltpu
from jax.sharding import PartitionSpec as P

MESH = pl.DeviceIdType.MESH
F32 = jnp.float32
BF16 = jnp.bfloat16
KINETIC = 0.0005

N = 128
BOX = 64
PLANES = 2
BANDS = 2
COLS = 48
SLOT = 64
PROJ = 18
PAIRS = 256
ATOMS = 8
COMBOS = 4
ROWS = PLANES * N


def split(table):
    high = table.astype(jnp.bfloat16)
    low = (table - high.astype(np.float64)).astype(jnp.bfloat16)
    return np.stack([high, low])


def tables(grid_count):
    scale = 1.0 / np.sqrt(N)
    pos = np.arange(N)
    box = np.arange(BOX)
    freq = np.where(box >= BOX // 2, box - BOX, box)

    def cos_sin(left, right):
        angle = 2.0 * np.pi / N * (np.outer(left, right) % N)
        return np.cos(angle) * scale, np.sin(angle) * scale

    cos_x, sin_x = cos_sin(pos, pos)
    x_table = np.zeros((grid_count, 2, PLANES, 2, N))
    cos_r = cos_x.reshape(grid_count, PLANES, N)
    sin_r = sin_x.reshape(grid_count, PLANES, N)
    x_table[:, 0, :, 0] = cos_r
    x_table[:, 0, :, 1] = -sin_r
    x_table[:, 1, :, 0] = sin_r
    x_table[:, 1, :, 1] = cos_r
    x_table = x_table.reshape(2 * N, 2 * N)
    cos_y, sin_y = cos_sin(freq, pos)
    y_table = np.zeros((BANDS, BOX, 2, BANDS, N))
    for band in range(BANDS):
        y_table[band, :, 0, band] = cos_y
        y_table[band, :, 1, band] = sin_y
    y_back = y_table.transpose(3, 4, 2, 0, 1).reshape(BANDS * N, 2 * BANDS * BOX)
    y_table = y_table.reshape(BANDS * BOX, 2 * BANDS * N)
    cos_z, sin_z = cos_sin(pos, freq)
    z_table = np.block([[cos_z, -sin_z], [sin_z, cos_z]])
    return [split(t) for t in (x_table, y_table, y_back, z_table, z_table.T)]


def halves(value):
    high = value.astype(BF16)
    low = (value - high.astype(F32)).astype(BF16)
    return high, low


def mm(left, right, dims=((1,), (0,))):
    return lax.dot_general(left, right, (dims, ((), ())), preferred_element_type=F32)


NT = ((1,), (1,))
TN = ((0,), (0,))


def iota(shape, dim):
    return lax.broadcasted_iota(jnp.int32, shape, dim)


def make_kernel(grid_count, band_count):
    peers = grid_count - 1
    half = grid_count // 2

    def kernel(
        psi_in, col_in, xt_in, dmat_in, atom_in, vloc_in, proj_in, row_in, yt_in, zt_in, zb_in,
        yb_in, occ_ref,
        out_hbm, dens_hbm,
        psi_ref, col_ref, xt_ref, dmat_ref, atom_ref, vloc_ref, proj_buf, row_ref, yt_ref, zt_ref,
        zb_ref, yb_ref, out_ref, proj_t, psi_pad, msg1, got1, msg2, got2, code_z, oh_y, box_ref,
        field, tiles, coeff, near_coeff, near_atom, atom_col, vloc_t,
        d_own, d_mate, d_slot, d_send, summed, applied, added, h_ref,
        dens_loc, dens_part, dens_full, work,
        in_sem, out_sem, s1, r1, s2, r2, sd, rd, sm, rm, sa, ra, sc, rc, sp, rp, sf, rf,
    ):
        me = lax.axis_index("grid")
        band = lax.axis_index("band")
        core = lax.rem(me, 2)
        chip = me // 2

        def to_grid(src, dst, send, recv, target):
            return pltpu.make_async_remote_copy(
                src_ref=src, dst_ref=dst, send_sem=send, recv_sem=recv,
                device_id={"grid": target}, device_id_type=MESH,
            )

        def to_band(src, dst, send, recv, target):
            return pltpu.make_async_remote_copy(
                src_ref=src, dst_ref=dst, send_sem=send, recv_sem=recv,
                device_id={"band": target}, device_id_type=MESH,
            )

        def settle(ref, sem):
            pltpu.make_async_copy(ref, ref, sem).wait()

        def far(step):
            return half + (1 - 2 * (step % 2)) * ((step + 1) // 2)

        barrier = pltpu.get_barrier_semaphore()

        def greet_grid(step, carry):
            pl.semaphore_signal(
                barrier, inc=1, device_id={"grid": lax.rem(me + step, grid_count)},
                device_id_type=MESH,
            )
            return carry

        def greet_band(step, carry):
            pl.semaphore_signal(
                barrier, inc=1, device_id={"band": lax.rem(band + step, band_count)},
                device_id_type=MESH,
            )
            return carry

        inputs = [
            pltpu.make_async_copy(src, dst, in_sem.at[i])
            for i, (src, dst) in enumerate(
                [
                    (psi_in, psi_ref), (col_in, col_ref), (xt_in, xt_ref), (dmat_in, dmat_ref),
                    (atom_in, atom_ref), (vloc_in, vloc_ref), (proj_in, proj_buf),
                    (row_in, row_ref), (yt_in, yt_ref), (zt_in, zt_ref), (zb_in, zb_ref),
                    (yb_in, yb_ref),
                ]
            )
        ]
        for copy in inputs:
            copy.start()
        lax.fori_loop(1, grid_count, greet_grid, 0)
        if band_count > 1:
            lax.fori_loop(1, band_count, greet_band, 0)

        psi_pad[...] = jnp.zeros_like(psi_pad)
        for copy in inputs[:4]:
            copy.wait()
        for member in range(BANDS):
            for part in range(2):
                psi_pad[member * SLOT : member * SLOT + COLS, part * N : (part + 1) * N] = psi_ref[
                    part, member
                ]
        psi_hi, psi_lo = halves(psi_pad[...])
        spread = mm(xt_ref[0], psi_hi, NT) + mm(xt_ref[1], psi_hi, NT) + mm(xt_ref[0], psi_lo, NT)
        work[...] = jnp.zeros_like(work)
        work[0:1, 0:COLS] = col_ref[...].astype(F32)
        codes = jnp.broadcast_to(work[0:1, :], (8, N))
        sub = iota((8, N), 0) % 4
        lane = iota((8, N), 1)
        pattern = jnp.where(
            sub == 0,
            pltpu.roll(codes, 48, 1),
            jnp.where(sub == 1, pltpu.roll(codes, 32, 1), pltpu.roll(codes, 16, 1)),
        )
        pattern = jnp.where((lane >= COLS) & (lane < SLOT) & (sub < 3), pattern, 0.0)
        for pair in range(grid_count // 2):
            both = spread[8 * pair : 8 * pair + 8] + pattern
            msg1[2 * pair] = both[0:4]
            msg1[2 * pair + 1] = both[4:8]
        own_copy = pltpu.make_async_copy(msg1.at[me], got1.at[me], r1.at[grid_count // 8 - 1])
        own_copy.start()
        d_send[...] = jnp.zeros_like(d_send)
        for i in range(PROJ):
            first = (i % 7) * PROJ
            d_send[i // 7, :, first : first + PROJ] = dmat_ref[i]
        d_own[chip] = d_send[...]

        pl.semaphore_wait(barrier, peers + band_count - 1)

        def send1(step, carry):
            target = lax.rem(me + far(step), grid_count)
            to_grid(msg1.at[target], got1.at[me], s1, r1.at[step // 8], target).start()
            return carry

        lax.fori_loop(0, peers, send1, 0)
        near = [lax.rem(me + off + grid_count, grid_count) for off in (1, -1, 2, -2)]
        inputs[4].wait()
        atom_copies = [
            to_grid(atom_ref, near_atom.at[i], sa.at[i], ra.at[i], near[i]) for i in range(4)
        ]
        for copy in atom_copies:
            copy.start()

        def send_d(step, carry):
            other = lax.rem(chip + step, half)
            to_grid(d_send, d_own.at[chip], sd, rd, 2 * other + core).start()
            return carry

        lax.fori_loop(1, half, send_d, 0)

        inputs[5].wait()
        for plane in range(PLANES):
            vloc_t[:, plane * N : (plane + 1) * N] = vloc_ref[plane].T
        atom_row = atom_ref[...].astype(F32)
        for part in range(2):
            atom_col[part * N : (part + 1) * N, :] = jnp.broadcast_to(
                atom_row[:, part * N : (part + 1) * N], (N, N)
            ).T
        inputs[6].wait()
        for i in range(PROJ):
            for part in range(2):
                proj_t[i, :, part * N : (part + 1) * N] = proj_buf[i, part * N : (part + 1) * N, :].T

        box_ref[...] = jnp.zeros_like(box_ref)
        row_id = iota((BANDS * BOX, N), 0)
        z_id = iota((BOX, N), 0)
        sub = iota((8, N), 0)
        lane = iota((8, N), 1)
        code_place = lane // 16 == (sub + 3) % 8
        lane = iota((1, N), 1)
        filled = lane % SLOT < COLS
        upper = lane >= SLOT

        def fill(step, carry):
            group = grid_count // 8 - 1 - step
            settle(got1.at[pl.ds(0, 8)], r1.at[group])
            total = jnp.zeros((2 * PLANES * BOX, BANDS * BOX), F32)
            for pair in range(4):
                senders = [
                    lax.rem(me + grid_count - far(8 * group + 2 * pair + k), grid_count)
                    for k in range(2)
                ]
                data = [got1[sender] for sender in senders]
                codes = pltpu.roll(jnp.concatenate(data, axis=0), 0, 1, stride=16, stride_axis=0)
                codes = jnp.where(code_place, codes, 0.0)
                picks, highs, lows = [], [], []
                for k in range(2):
                    code = jnp.sum(codes[4 * k : 4 * k + 4], axis=0, keepdims=True)
                    code = jnp.broadcast_to(code, (8, N))
                    turned = [pltpu.roll(code, 80, 1), pltpu.roll(code, 16, 1)]
                    code = jnp.where(upper, turned[1 - k], turned[k])[0:1]
                    code = code.astype(jnp.int32)
                    at_y = jnp.where(filled, (code // N) % BOX + jnp.where(upper, BOX, 0), -1)
                    at_z = jnp.where(filled, code % BOX, -1)
                    code_z[senders[k]] = at_z
                    picker = jnp.where(row_id == at_y, 1.0, 0.0).astype(BF16)
                    oh_y[senders[k]] = picker
                    picks.append(picker)
                    high = data[k].astype(BF16).astype(F32)
                    rest = data[k] - high
                    at = z_id == at_z
                    for value, store in ((high, highs), (rest, lows)):
                        store.append(
                            jnp.concatenate(
                                [jnp.where(at, value[r : r + 1], 0.0) for r in range(4)], axis=0
                            ).astype(BF16)
                        )
                pick = jnp.concatenate(picks, axis=1)
                total += mm(jnp.concatenate(highs, axis=1), pick, NT)
                total += mm(jnp.concatenate(lows, axis=1), pick, NT)
            box_ref[...] += total
            return carry

        lax.fori_loop(0, grid_count // 8, fill, 0)

        for copy in inputs[7:]:
            copy.wait()
        box_hi, box_lo = halves(box_ref[...])
        turned = mm(box_hi, yt_ref[0]) + mm(box_lo, yt_ref[0]) + mm(box_hi, yt_ref[1])
        mid, end = PLANES * BOX, BANDS * N
        part_re = turned[:mid, :end] - turned[mid:, end:]
        part_im = turned[:mid, end:] + turned[mid:, :end]
        for plane in range(PLANES):
            here = slice(plane * BOX, (plane + 1) * BOX)
            value = jnp.concatenate([part_re[here], part_im[here]], axis=0)
            v_hi, v_lo = halves(value)
            wave = mm(zt_ref[0], v_hi) + mm(zt_ref[1], v_hi) + mm(zt_ref[0], v_lo)
            for part in range(2):
                for member in range(BANDS):
                    first = (part * BANDS + member) * N
                    field[first : first + N, plane * N : (plane + 1) * N] = wave[
                        part * N : (part + 1) * N, member * N : (member + 1) * N
                    ]

        dens_t = jnp.zeros((N, ROWS), F32)
        for member in range(BANDS):
            real = field[member * N : (member + 1) * N, :]
            imag = field[(BANDS + member) * N : (BANDS + member + 1) * N, :]
            dens_t += occ_ref[0, member] * (real * real + imag * imag)
        for plane in range(PLANES):
            dens_loc[plane * N : (plane + 1) * N, :] = dens_t[:, plane * N : (plane + 1) * N].T
        share = ROWS // band_count

        def send_part(step, carry):
            target = lax.rem(band + step, band_count)
            first = pl.multiple_of(target * share, share)
            to_band(dens_loc.at[pl.ds(first, share)], dens_part.at[band], sp, rp, target).start()
            return carry

        if band_count > 1:
            lax.fori_loop(1, band_count, send_part, 0)

        local_row = row_ref[...] - me * ROWS
        row_pick = jnp.where(iota((ROWS, PAIRS), 0) == local_row, 1.0, 0.0).astype(BF16)
        f_hi, f_lo = halves(field[...])
        tiles[...] = mm(f_hi, row_pick) + mm(f_lo, row_pick)

        def project(step, carry):
            found = []
            for k in range(2):
                values = proj_t[2 * step + k]
                for combo in range(COMBOS):
                    found.append(
                        jnp.sum(values * tiles[combo * N : (combo + 1) * N, :], axis=0, keepdims=True)
                    )
            coeff[pl.ds(pl.multiple_of(step * 8, 8), 8), :] = jnp.concatenate(found, axis=0)
            return carry

        lax.fori_loop(0, PROJ // 2, project, 0)
        coeff_copies = [
            to_grid(coeff, near_coeff.at[i], sc.at[i], rc.at[i], near[i]) for i in range(4)
        ]
        for copy in coeff_copies:
            copy.start()

        if band_count > 1:
            settle(dens_part.at[pl.ds(0, band_count - 1)], rp)
        mine = pl.ds(pl.multiple_of(band * share, share), share)
        dens_part[band] = dens_loc[mine, :]
        whole = dens_part[0]
        for other in range(1, band_count):
            whole += dens_part[other]
        dens_full[mine, :] = whole

        def send_full(step, carry):
            target = lax.rem(band + step, band_count)
            to_band(dens_full.at[mine], dens_full.at[mine], sf, rf, target).start()
            return carry

        if band_count > 1:
            lax.fori_loop(1, band_count, send_full, 0)

        settle(d_own.at[pl.ds(0, half - 1)], rd)
        mate = to_grid(d_own, d_mate, sm, rm, 2 * chip + 1 - core)
        mate.start()
        place = iota((half * ATOMS, PAIRS), 0)
        atom_base = (place // ATOMS) * (2 * ATOMS) + place % ATOMS
        atoms = atom_ref[...]
        own_pick = jnp.where(atom_base + core * ATOMS == atoms, 1.0, 0.0).astype(BF16)
        mate_pick = jnp.where(atom_base + (1 - core) * ATOMS == atoms, 1.0, 0.0).astype(BF16)
        for q in range(3):
            d_hi, d_lo = halves(d_own[:, q].reshape(half * ATOMS, N))
            slots = mm(d_hi, own_pick, TN) + mm(d_lo, own_pick, TN)
            for lanes in range(2):
                d_slot[lanes, q * N : (q + 1) * N, :] = slots[:, lanes * N : (lanes + 1) * N]
        mate.wait_recv()
        for q in range(3):
            d_hi, d_lo = halves(d_mate[:, q].reshape(half * ATOMS, N))
            slots = mm(d_hi, mate_pick, TN) + mm(d_lo, mate_pick, TN)
            for lanes in range(2):
                d_slot[lanes, q * N : (q + 1) * N, :] += slots[:, lanes * N : (lanes + 1) * N]

        for copy in atom_copies:
            copy.wait_recv()
        column = jnp.concatenate([atom_col[...], atom_col[...]], axis=1)

        def same(other_row):
            return jnp.where(column == other_row.astype(F32), 1.0, 0.0).astype(BF16)

        c_hi, c_lo = halves(coeff[...])
        pick = same(atoms)
        total = mm(c_hi, pick, NT) + mm(c_lo, pick, NT)
        for i in range(4):
            coeff_copies[i].wait_recv()
            c_hi, c_lo = halves(near_coeff[i])
            pick = same(near_atom[i])
            total += mm(c_hi, pick, NT) + mm(c_lo, pick, NT)
        summed[...] = total

        d_slot[:, 3 * N :, :] = jnp.zeros((2, 24, N), F32)
        values = [jnp.zeros((24, PAIRS), F32) for _ in range(COMBOS)]
        for j in range(PROJ):
            part = jnp.concatenate(
                [
                    jnp.concatenate(
                        [d_slot[lanes, pl.ds(q * N + j, 8, stride=PROJ), :] for lanes in range(2)],
                        axis=1,
                    )
                    for q in range(3)
                ],
                axis=0,
            )
            for combo in range(COMBOS):
                row = j * COMBOS + combo
                values[combo] += part * summed[row : row + 1, :]
        for combo in range(COMBOS):
            applied[combo] = values[combo]

        depth = 32

        def spread_back(step, carry):
            first = pl.multiple_of(step * depth, depth)
            totals = [jnp.zeros((depth, PAIRS), F32) for _ in range(COMBOS)]
            for i in range(PROJ):
                values = proj_t[i, pl.ds(first, depth), :]
                for combo in range(COMBOS):
                    totals[combo] += values * applied[combo, 8 * (i // 7) + i % 7 : 8 * (i // 7) + i % 7 + 1, :]
            for combo in range(COMBOS):
                added[pl.ds(pl.multiple_of(combo * N + first, depth), depth), :] = totals[combo]
            return carry

        lax.fori_loop(0, N // depth, spread_back, 0)
        a_hi, a_lo = halves(added[...])
        projected = mm(a_hi, row_pick, NT) + mm(a_lo, row_pick, NT)
        for combo in range(COMBOS):
            here = slice(combo * N, (combo + 1) * N)
            h_ref[here, :] = vloc_t[...] * field[here, :] + projected[here]

        spectra = []
        for plane in range(PLANES):
            lanes = slice(plane * N, (plane + 1) * N)
            value = jnp.concatenate(
                [
                    jnp.concatenate(
                        [
                            h_ref[(part * BANDS + member) * N : (part * BANDS + member + 1) * N, lanes]
                            for member in range(BANDS)
                        ],
                        axis=1,
                    )
                    for part in range(2)
                ],
                axis=0,
            )
            v_hi, v_lo = halves(value)
            spectra.append(mm(zb_ref[0], v_hi) + mm(zb_ref[1], v_hi) + mm(zb_ref[0], v_lo))
        turned = jnp.concatenate(
            [spectra[plane][part * BOX : (part + 1) * BOX] for part in range(2) for plane in range(PLANES)],
            axis=0,
        )
        t_hi, t_lo = halves(turned)
        turned = mm(t_hi, yb_ref[0]) + mm(t_lo, yb_ref[0]) + mm(t_hi, yb_ref[1])
        end = BANDS * BOX
        final = jnp.concatenate(
            [turned[:mid, :end] + turned[mid:, end:], turned[mid:, :end] - turned[:mid, end:]], axis=0
        )
        q_hi, q_lo = halves(final)
        both = jnp.concatenate([q_hi, q_lo], axis=1)

        batch = 4

        def take(targets):
            for first in range(0, batch, 2):
                two = targets[first : first + 2]
                pick = jnp.concatenate([oh_y[target] for target in two], axis=1)
                found = mm(both, jnp.concatenate([pick, pick], axis=0))
                for k, target in enumerate(two):
                    at = z_id == code_z[target]
                    msg2[target] = jnp.concatenate(
                        [
                            jnp.sum(
                                jnp.where(
                                    at, found[r * BOX : (r + 1) * BOX, k * N : (k + 1) * N], 0.0
                                ),
                                axis=0,
                                keepdims=True,
                            )
                            for r in range(4)
                        ],
                        axis=0,
                    )

        def partners(step):
            return [lax.rem(me + far(batch * step + k), grid_count) for k in range(batch)]

        def send2(target):
            to_grid(msg2.at[target], got2.at[me], s2, r2, target).start()

        def take_and_send(step, carry):
            targets = partners(step)
            take(targets)
            for target in targets:
                send2(target)
            return carry

        lax.fori_loop(0, grid_count // batch - 1, take_and_send, 0)
        targets = partners(grid_count // batch - 1)
        take(targets)
        for target in targets[:-1]:
            send2(target)
        got2[me] = msg2[me]

        if band_count > 1:
            settle(dens_full.at[pl.ds(0, ROWS - share)], rf)
        dens_out = pltpu.make_async_copy(dens_full, dens_hbm, out_sem.at[0])
        dens_out.start()

        work[...] = jnp.zeros_like(work)
        work[0:1, 0:COLS] = col_ref[...].astype(F32)
        codes = jnp.broadcast_to(work[0:1, :], (N, N)).T.astype(jnp.int32)[0:COLS]

        def signed(index):
            return jnp.where(index >= N // 2, index - N, index)

        fy, fz, fx = signed(codes // N), signed(codes % N), signed(iota((COLS, N), 1))
        kinetic = KINETIC * (fx * fx + fy * fy + fz * fz).astype(F32)

        settle(got2.at[pl.ds(0, peers)], r2)
        back = got2[...].reshape(grid_count * 4, N).T
        b_hi, b_lo = halves(back)
        result = mm(b_hi, xt_ref[0]) + mm(b_lo, xt_ref[0]) + mm(b_hi, xt_ref[1])
        for part in range(2):
            for member in range(BANDS):
                out_ref[part, member] = (
                    result[member * SLOT : member * SLOT + COLS, part * N : (part + 1) * N]
                    + kinetic * psi_ref[part, member]
                )

        out_copy = pltpu.make_async_copy(out_ref, out_hbm, out_sem.at[1])
        out_copy.start()

        dens_out.wait()
        settle(msg1.at[pl.ds(0, peers)], s1)
        settle(msg2.at[pl.ds(0, peers)], s2)
        settle(d_own.at[pl.ds(0, half - 1)], sd)
        mate.wait_send()
        for copy in atom_copies + coeff_copies:
            copy.wait_send()
        if band_count > 1:
            settle(dens_part.at[pl.ds(0, band_count - 1)], sp)
            settle(dens_full.at[pl.ds(0, ROWS - share)], sf)
        out_copy.wait()

    return kernel


def solution(mesh):
    grid_count = mesh.shape["grid"]
    band_count = mesh.shape["band"]
    half = grid_count // 2
    constants = tables(grid_count)

    def step(psi_g, col_index, v_local, proj_values, pair_atom, pair_row, d_matrices, occupations):
        x_table, y_table, y_back, z_table, z_back = [jnp.asarray(t) for t in constants]
        hbm = pl.BlockSpec(memory_space=pl.ANY)
        dma = pltpu.SemaphoreType.DMA
        out, dens = pl.pallas_call(
            make_kernel(grid_count, band_count),
            out_shape=(
                jax.ShapeDtypeStruct(psi_g.shape, F32),
                jax.ShapeDtypeStruct((ROWS, N), F32),
            ),
            in_specs=[hbm] * 12 + [pl.BlockSpec(memory_space=pltpu.SMEM)],
            out_specs=(hbm, hbm),
            scratch_shapes=[
                pltpu.VMEM((2, BANDS, COLS, N), F32),
                pltpu.VMEM((1, COLS), jnp.int32),
                pltpu.VMEM((2, 2 * N, 2 * N), BF16),
                pltpu.VMEM((PROJ, ATOMS, PROJ), F32),
                pltpu.VMEM((1, PAIRS), jnp.int32),
                pltpu.VMEM((PLANES, N, N), F32),
                pltpu.VMEM((PROJ, PAIRS, N), F32),
                pltpu.VMEM((1, PAIRS), jnp.int32),
                pltpu.VMEM((2, BANDS * BOX, 2 * BANDS * N), BF16),
                pltpu.VMEM((2, 2 * N, 2 * BOX), BF16),
                pltpu.VMEM((2, 2 * BOX, 2 * N), BF16),
                pltpu.VMEM((2, BANDS * N, 2 * BANDS * BOX), BF16),
                pltpu.VMEM((2, BANDS, COLS, N), F32),
                pltpu.VMEM((PROJ, N, PAIRS), F32),
                pltpu.VMEM((BANDS * SLOT, 2 * N), F32),
                pltpu.VMEM((grid_count, 4, N), F32),
                pltpu.VMEM((grid_count, 4, N), F32),
                pltpu.VMEM((grid_count, 4, N), F32),
                pltpu.VMEM((grid_count, 4, N), F32),
                pltpu.VMEM((grid_count, 1, N), jnp.int32),
                pltpu.VMEM((grid_count, BANDS * BOX, N), BF16),
                pltpu.VMEM((2 * PLANES * BOX, BANDS * BOX), F32),
                pltpu.VMEM((COMBOS * N, ROWS), F32),
                pltpu.VMEM((COMBOS * N, PAIRS), F32),
                pltpu.VMEM((PROJ * COMBOS, PAIRS), F32),
                pltpu.VMEM((4, PROJ * COMBOS, PAIRS), F32),
                pltpu.VMEM((4, 1, PAIRS), jnp.int32),
                pltpu.VMEM((PAIRS, N), F32),
                pltpu.VMEM((N, ROWS), F32),
                pltpu.VMEM((half, 3, ATOMS, N), F32),
                pltpu.VMEM((half, 3, ATOMS, N), F32),
                pltpu.VMEM((2, 3 * N + 24, N), F32),
                pltpu.VMEM((3, ATOMS, N), F32),
                pltpu.VMEM((PROJ * COMBOS, PAIRS), F32),
                pltpu.VMEM((COMBOS, 24, PAIRS), F32),
                pltpu.VMEM((COMBOS * N, PAIRS), F32),
                pltpu.VMEM((COMBOS * N, ROWS), F32),
                pltpu.VMEM((ROWS, N), F32),
                pltpu.VMEM((band_count, ROWS // band_count, N), F32),
                pltpu.VMEM((ROWS, N), F32),
                pltpu.VMEM((8, N), F32),
                dma((12,)), dma((2,)), dma, dma((grid_count // 8,)), dma, dma, dma, dma, dma, dma,
                dma((4,)), dma((4,)), dma((4,)), dma((4,)), dma, dma, dma, dma,
            ],
            compiler_params=pltpu.CompilerParams(
                collective_id=0, has_side_effects=True, vmem_limit_bytes=60 << 20
            ),
        )(
            psi_g,
            col_index.reshape(1, COLS),
            x_table,
            d_matrices.transpose(1, 0, 2),
            pair_atom.reshape(1, PAIRS),
            v_local,
            proj_values.transpose(1, 0, 2),
            pair_row.reshape(1, PAIRS),
            y_table,
            z_table,
            z_back,
            y_back,
            occupations.reshape(1, BANDS),
        )
        return out, dens.reshape(PLANES, N, N)

    return jax.shard_map(
        step,
        mesh=mesh,
        in_specs=(
            P(None, "band", "grid", None),
            P("grid"),
            P("grid", None, None),
            P("grid", None, None),
            P("grid"),
            P("grid"),
            P("grid", None, None),
            P("band"),
        ),
        out_specs=(P(None, "band", "grid", None), P("grid", None, None)),
        check_vma=False,
    )
```

```python
import functools

import jax
import jax.numpy as jnp
import numpy as np
from jax import lax
from jax.experimental import pallas as pl
from jax.experimental.pallas import tpu as pltpu
from jax.sharding import PartitionSpec as P

MESH = pl.DeviceIdType.MESH
F32 = jnp.float32
BF16 = jnp.bfloat16
KINETIC = 0.0005

N = 128
BOX = 64
PLANES = 2
BANDS = 2
COLS = 48
SLOT = 64
PROJ = 18
PAIRS = 256
ATOMS = 8
COMBOS = 4
ROWS = PLANES * N


def split(table):
    high = table.astype(jnp.bfloat16)
    low = (table - high.astype(np.float64)).astype(jnp.bfloat16)
    return np.stack([high, low])


def tables(grid_count):
    scale = 1.0 / np.sqrt(N)
    pos = np.arange(N)
    box = np.arange(BOX)
    freq = np.where(box >= BOX // 2, box - BOX, box)

    def cos_sin(left, right):
        angle = 2.0 * np.pi / N * (np.outer(left, right) % N)
        return np.cos(angle) * scale, np.sin(angle) * scale

    cos_x, sin_x = cos_sin(pos, pos)
    x_table = np.zeros((grid_count, 2, PLANES, 2, N))
    cos_r = cos_x.reshape(grid_count, PLANES, N)
    sin_r = sin_x.reshape(grid_count, PLANES, N)
    x_table[:, 0, :, 0] = cos_r
    x_table[:, 0, :, 1] = -sin_r
    x_table[:, 1, :, 0] = sin_r
    x_table[:, 1, :, 1] = cos_r
    x_table = x_table.reshape(2 * N, 2 * N)
    cos_y, sin_y = cos_sin(freq, pos)
    y_table = np.zeros((BANDS, BOX, 2, BANDS, N))
    for band in range(BANDS):
        y_table[band, :, 0, band] = cos_y
        y_table[band, :, 1, band] = sin_y
    y_back = y_table.transpose(3, 4, 2, 0, 1).reshape(BANDS * N, 2 * BANDS * BOX)
    y_table = y_table.reshape(BANDS * BOX, 2 * BANDS * N)
    cos_z, sin_z = cos_sin(pos, freq)
    z_table = np.block([[cos_z, -sin_z], [sin_z, cos_z]])
    return [split(t) for t in (x_table, y_table, y_back, z_table, z_table.T)]


def halves(value):
    high = value.astype(BF16)
    low = (value - high.astype(F32)).astype(BF16)
    return high, low


def mm(left, right, dims=((1,), (0,))):
    return lax.dot_general(left, right, (dims, ((), ())), preferred_element_type=F32)


NT = ((1,), (1,))
TN = ((0,), (0,))


def iota(shape, dim):
    return lax.broadcasted_iota(jnp.int32, shape, dim)


def make_kernel(grid_count, band_count):
    peers = grid_count - 1
    half = grid_count // 2
    width = 4
    height = half // width

    def kernel(
        psi_in, col_in, xt_in, dmat_in, atom_in, vloc_in, proj_in, row_in, yt_in, zt_in, zb_in,
        yb_in, occ_ref,
        got2, dens_hbm,
        psi_ref, col_ref, xt_ref, dmat_ref, atom_ref, vloc_ref, proj_buf, row_ref, yt_ref, zt_ref,
        zb_ref, yb_ref, proj_t, psi_pad, msg1, got1, msg2, code_z, oh_y, box_ref,
        field, tiles, coeff, near_coeff, near_atom, atom_col, vloc_t,
        d_own, d_mate, d_slot, d_send, summed, applied, added, h_ref,
        dens_loc, dens_part, dens_full, work,
        in_sem, out_sem, s1, r1, s2, r2, sd, rd, sx, rx, sm, rm, sa, ra, sc, rc, sp, rp, sf, rf,
    ):
        me = lax.axis_index("grid")
        band = lax.axis_index("band")
        core = lax.rem(me, 2)
        chip = me // 2
        at_x = lax.rem(chip, width)
        at_y = chip // width

        def to_grid(src, dst, send, recv, target):
            return pltpu.make_async_remote_copy(
                src_ref=src, dst_ref=dst, send_sem=send, recv_sem=recv,
                device_id={"grid": target}, device_id_type=MESH,
            )

        def to_band(src, dst, send, recv, target):
            return pltpu.make_async_remote_copy(
                src_ref=src, dst_ref=dst, send_sem=send, recv_sem=recv,
                device_id={"band": target}, device_id_type=MESH,
            )

        def settle(ref, sem):
            pltpu.make_async_copy(ref, ref, sem).wait()

        def far(step):
            return half + (1 - 2 * (step % 2)) * ((step + 1) // 2)

        barrier = pltpu.get_barrier_semaphore()
        def greet_grid(step, carry):
            pl.semaphore_signal(
                barrier, inc=1, device_id={"grid": lax.rem(me + step, grid_count)},
                device_id_type=MESH,
            )
            return carry

        def greet_band(step, carry):
            pl.semaphore_signal(
                barrier, inc=1, device_id={"band": lax.rem(band + step, band_count)},
                device_id_type=MESH,
            )
            return carry

        inputs = [
            pltpu.make_async_copy(src, dst, in_sem.at[i])
            for i, (src, dst) in enumerate(
                [
                    (psi_in, psi_ref), (col_in, col_ref), (xt_in, xt_ref), (dmat_in, dmat_ref),
                    (atom_in, atom_ref), (vloc_in, vloc_ref), (proj_in, proj_buf),
                    (row_in, row_ref), (yt_in, yt_ref), (zt_in, zt_ref), (zb_in, zb_ref),
                    (yb_in, yb_ref),
                ]
            )
        ]
        for copy in inputs[:4]:
            copy.start()
        lax.fori_loop(1, grid_count, greet_grid, 0)
        if band_count > 1:
            lax.fori_loop(1, band_count, greet_band, 0)
        for copy in inputs[4:]:
            copy.start()

        psi_pad[...] = jnp.zeros_like(psi_pad)
        for copy in inputs[:4]:
            copy.wait()
        for member in range(BANDS):
            for part in range(2):
                psi_pad[member * SLOT : member * SLOT + COLS, part * N : (part + 1) * N] = psi_ref[
                    part, member
                ]
        psi_hi, psi_lo = halves(psi_pad[...])
        spread = mm(xt_ref[0], psi_hi, NT) + mm(xt_ref[1], psi_hi, NT) + mm(xt_ref[0], psi_lo, NT)
        work[...] = jnp.zeros_like(work)
        work[0:1, 0:COLS] = col_ref[...].astype(F32)
        codes = jnp.broadcast_to(work[0:1, :], (8, N))
        sub = iota((8, N), 0) % 4
        lane = iota((8, N), 1)
        pattern = jnp.where(
            sub == 0,
            pltpu.roll(codes, 48, 1),
            jnp.where(sub == 1, pltpu.roll(codes, 32, 1), pltpu.roll(codes, 16, 1)),
        )
        pattern = jnp.where((lane >= COLS) & (lane < SLOT) & (sub < 3), pattern, 0.0)
        for pair in range(grid_count // 2):
            both = spread[8 * pair : 8 * pair + 8] + pattern
            msg1[2 * pair] = both[0:4]
            msg1[2 * pair + 1] = both[4:8]
        own_copy = pltpu.make_async_copy(msg1.at[me], got1.at[me], r1.at[grid_count // 16 - 1])
        own_copy.start()
        d_send[...] = jnp.zeros_like(d_send)
        for i in range(PROJ):
            first = (i % 7) * PROJ
            d_send[i // 7, :, first : first + PROJ] = dmat_ref[i]
        d_own[at_x * height + at_y] = d_send[...]

        pl.semaphore_wait(barrier, peers + band_count - 1)

        def send1(step, carry):
            target = lax.rem(me + far(step), grid_count)
            to_grid(msg1.at[target], got1.at[me], s1, r1.at[step // 16], target).start()
            return carry

        lax.fori_loop(0, peers, send1, 0)
        near = [lax.rem(me + off + grid_count, grid_count) for off in (1, -1, 2, -2)]
        inputs[4].wait()
        atom_copies = [
            to_grid(atom_ref, near_atom.at[i], sa.at[i], ra.at[i], near[i]) for i in range(4)
        ]
        for copy in atom_copies:
            copy.start()

        for step in range(1, height):
            other = lax.rem(at_y + step, height) * width + at_x
            to_grid(d_send, d_own.at[at_x * height + at_y], sd, rd, 2 * other + core).start()

        inputs[5].wait()
        for plane in range(PLANES):
            vloc_t[:, plane * N : (plane + 1) * N] = vloc_ref[plane].T
        atom_row = atom_ref[...].astype(F32)
        for part in range(2):
            atom_col[part * N : (part + 1) * N, :] = jnp.broadcast_to(
                atom_row[:, part * N : (part + 1) * N], (N, N)
            ).T
        inputs[6].wait()
        for i in range(PROJ):
            for part in range(2):
                proj_t[i, :, part * N : (part + 1) * N] = proj_buf[i, part * N : (part + 1) * N, :].T

        box_ref[...] = jnp.zeros_like(box_ref)
        row_id = iota((BANDS * BOX, N), 0).astype(F32).astype(BF16)
        z_id = iota((BOX, N), 0)
        z_id16 = z_id.astype(F32).astype(BF16)
        sub = iota((8, N), 0)
        lane = iota((8, N), 1)
        one, zero = jnp.ones((), BF16), jnp.zeros((), BF16)
        code_place = lane // 16 == (sub + 3) % 8
        lane = iota((1, N), 1)
        filled = lane % SLOT < COLS
        upper = lane >= SLOT

        def fill(step, carry):
            group = grid_count // 16 - 1 - step
            settle(got1.at[pl.ds(0, 16)], r1.at[group])
            total = jnp.zeros((BANDS * BOX, 2 * PLANES * BOX), F32)
            for pair in range(8):
                senders = [
                    lax.rem(me + grid_count - far(16 * group + 2 * pair + k), grid_count)
                    for k in range(2)
                ]
                data = [got1[sender] for sender in senders]
                codes = pltpu.roll(jnp.concatenate(data, axis=0), 0, 1, stride=16, stride_axis=0)
                codes = jnp.where(code_place, codes, 0.0)
                picks, highs, lows = [], [], []
                for k in range(2):
                    code = jnp.sum(codes[4 * k : 4 * k + 4], axis=0, keepdims=True)
                    code = jnp.broadcast_to(code, (8, N))
                    turned = [pltpu.roll(code, 80, 1), pltpu.roll(code, 16, 1)]
                    code = jnp.where(upper, turned[1 - k], turned[k])[0:1]
                    code = code.astype(jnp.int32)
                    at_y = jnp.where(filled, (code // N) % BOX + jnp.where(upper, BOX, 0), -1)
                    at_z = jnp.where(filled, code % BOX, -1)
                    code_z[senders[k]] = at_z
                    picker = jnp.where(row_id == at_y.astype(F32).astype(BF16), one, zero)
                    oh_y[senders[k]] = picker
                    picks.append(picker)
                    high, rest = halves(data[k])
                    at = z_id16 == at_z.astype(F32).astype(BF16)
                    for value, store in ((high, highs), (rest, lows)):
                        store.append(
                            jnp.concatenate(
                                [jnp.where(at, value[r : r + 1], zero) for r in range(4)], axis=0
                            )
                        )
                pick = jnp.concatenate(picks, axis=1)
                total += mm(pick, jnp.concatenate(highs, axis=1), NT)
                total += mm(pick, jnp.concatenate(lows, axis=1), NT)
            box_ref[...] += total
            return carry

        lax.fori_loop(0, grid_count // 16, fill, 0)

        settle(d_own.at[pl.ds(0, height - 1)], rd)
        column = pl.ds(at_x * height, height)
        for step in range(1, width):
            other = at_y * width + lax.rem(at_x + step, width)
            to_grid(d_own.at[column], d_own.at[column], sx, rx, 2 * other + core).start()

        for copy in inputs[7:]:
            copy.wait()
        box_hi, box_lo = halves(box_ref[...].T)
        turned = mm(box_hi, yt_ref[0]) + mm(box_lo, yt_ref[0]) + mm(box_hi, yt_ref[1])
        mid, end = PLANES * BOX, BANDS * N
        part_re = turned[:mid, :end] - turned[mid:, end:]
        part_im = turned[:mid, end:] + turned[mid:, :end]
        for plane in range(PLANES):
            here = slice(plane * BOX, (plane + 1) * BOX)
            value = jnp.concatenate([part_re[here], part_im[here]], axis=0)
            v_hi, v_lo = halves(value)
            wave = mm(zt_ref[0], v_hi) + mm(zt_ref[1], v_hi) + mm(zt_ref[0], v_lo)
            for part in range(2):
                for member in range(BANDS):
                    first = (part * BANDS + member) * N
                    field[first : first + N, plane * N : (plane + 1) * N] = wave[
                        part * N : (part + 1) * N, member * N : (member + 1) * N
                    ]

        dens_t = jnp.zeros((N, ROWS), F32)
        for member in range(BANDS):
            real = field[member * N : (member + 1) * N, :]
            imag = field[(BANDS + member) * N : (BANDS + member + 1) * N, :]
            dens_t += occ_ref[0, member] * (real * real + imag * imag)
        for plane in range(PLANES):
            dens_loc[plane * N : (plane + 1) * N, :] = dens_t[:, plane * N : (plane + 1) * N].T
        share = ROWS // band_count

        def send_part(step, carry):
            target = lax.rem(band + step, band_count)
            first = pl.multiple_of(target * share, share)
            to_band(dens_loc.at[pl.ds(first, share)], dens_part.at[band], sp, rp, target).start()
            return carry

        if band_count > 1:
            lax.fori_loop(1, band_count, send_part, 0)

        local_row = row_ref[...] - me * ROWS
        row_pick = jnp.where(iota((ROWS, PAIRS), 0) == local_row, 1.0, 0.0).astype(BF16)
        f_hi, f_lo = halves(field[...])
        tiles[...] = mm(f_hi, row_pick) + mm(f_lo, row_pick)

        def project(step, carry):
            found = []
            for k in range(2):
                values = proj_t[2 * step + k]
                for combo in range(COMBOS):
                    found.append(
                        jnp.sum(values * tiles[combo * N : (combo + 1) * N, :], axis=0, keepdims=True)
                    )
            coeff[pl.ds(pl.multiple_of(step * 8, 8), 8), :] = jnp.concatenate(found, axis=0)
            return carry

        coeff_copies = []
        for part in range(3):
            lax.fori_loop(3 * part, 3 * part + 3, project, 0)
            rows = pl.ds(24 * part, 24)
            coeff_copies.append(
                [
                    to_grid(
                        coeff.at[rows], near_coeff.at[i, rows], sc.at[i, part], rc.at[i, part], near[i]
                    )
                    for i in range(4)
                ]
            )
            for copy in coeff_copies[-1]:
                copy.start()

        settle(d_own.at[pl.ds(0, half - height)], rx)
        mate = to_grid(d_own, d_mate, sm, rm, 2 * chip + 1 - core)
        mate.start()
        place = iota((half * ATOMS, PAIRS), 0)
        slot = place // ATOMS
        atom_base = ((slot % height) * width + slot // height) * (2 * ATOMS) + place % ATOMS
        atoms = atom_ref[...]
        own_pick = jnp.where(atom_base + core * ATOMS == atoms, 1.0, 0.0).astype(BF16)
        mate_pick = jnp.where(atom_base + (1 - core) * ATOMS == atoms, 1.0, 0.0).astype(BF16)
        for q in range(3):
            d_hi, d_lo = halves(d_own[:, q].reshape(half * ATOMS, N))
            slots = mm(d_hi, own_pick, TN) + mm(d_lo, own_pick, TN)
            for lanes in range(2):
                d_slot[lanes, q * N : (q + 1) * N, :] = slots[:, lanes * N : (lanes + 1) * N]
        mate.wait_recv()
        for q in range(3):
            d_hi, d_lo = halves(d_mate[:, q].reshape(half * ATOMS, N))
            slots = mm(d_hi, mate_pick, TN) + mm(d_lo, mate_pick, TN)
            for lanes in range(2):
                d_slot[lanes, q * N : (q + 1) * N, :] += slots[:, lanes * N : (lanes + 1) * N]

        for copy in atom_copies:
            copy.wait_recv()
        column = jnp.concatenate([atom_col[...], atom_col[...]], axis=1)

        def same(other_row):
            return jnp.where(column == other_row.astype(F32), 1.0, 0.0).astype(BF16)

        c_hi, c_lo = halves(coeff[...])
        pick = same(atoms)
        total = mm(c_hi, pick, NT) + mm(c_lo, pick, NT)
        for i in range(4):
            for part in range(3):
                coeff_copies[part][i].wait_recv()
            c_hi, c_lo = halves(near_coeff[i])
            pick = same(near_atom[i])
            total += mm(c_hi, pick, NT) + mm(c_lo, pick, NT)
        summed[...] = total

        d_slot[:, 3 * N :, :] = jnp.zeros((2, 24, N), F32)
        values = [jnp.zeros((24, PAIRS), F32) for _ in range(COMBOS)]
        for j in range(PROJ):
            part = jnp.concatenate(
                [
                    jnp.concatenate(
                        [d_slot[lanes, pl.ds(q * N + j, 8, stride=PROJ), :] for lanes in range(2)],
                        axis=1,
                    )
                    for q in range(3)
                ],
                axis=0,
            )
            for combo in range(COMBOS):
                row = j * COMBOS + combo
                values[combo] += part * summed[row : row + 1, :]
        for combo in range(COMBOS):
            applied[combo] = values[combo]

        depth = 32

        def spread_back(step, carry):
            first = pl.multiple_of(step * depth, depth)
            totals = [jnp.zeros((depth, PAIRS), F32) for _ in range(COMBOS)]
            for i in range(PROJ):
                values = proj_t[i, pl.ds(first, depth), :]
                for combo in range(COMBOS):
                    totals[combo] += values * applied[combo, 8 * (i // 7) + i % 7 : 8 * (i // 7) + i % 7 + 1, :]
            for combo in range(COMBOS):
                added[pl.ds(pl.multiple_of(combo * N + first, depth), depth), :] = totals[combo]
            return carry

        lax.fori_loop(0, N // depth, spread_back, 0)
        a_hi, a_lo = halves(added[...])
        projected = mm(a_hi, row_pick, NT) + mm(a_lo, row_pick, NT)
        for combo in range(COMBOS):
            here = slice(combo * N, (combo + 1) * N)
            h_ref[here, :] = vloc_t[...] * field[here, :] + projected[here]

        if band_count > 1:
            settle(dens_part.at[pl.ds(0, band_count - 1)], rp)
        mine = pl.ds(pl.multiple_of(band * share, share), share)
        dens_part[band] = dens_loc[mine, :]
        whole = dens_part[0]
        for other in range(1, band_count):
            whole += dens_part[other]
        dens_full[mine, :] = whole

        def send_full(step, carry):
            target = lax.rem(band + step, band_count)
            to_band(dens_full.at[mine], dens_full.at[mine], sf, rf, target).start()
            return carry

        if band_count > 1:
            lax.fori_loop(1, band_count, send_full, 0)

        spectra = []
        for plane in range(PLANES):
            lanes = slice(plane * N, (plane + 1) * N)
            value = jnp.concatenate(
                [
                    jnp.concatenate(
                        [
                            h_ref[(part * BANDS + member) * N : (part * BANDS + member + 1) * N, lanes]
                            for member in range(BANDS)
                        ],
                        axis=1,
                    )
                    for part in range(2)
                ],
                axis=0,
            )
            v_hi, v_lo = halves(value)
            spectra.append(mm(zb_ref[0], v_hi) + mm(zb_ref[1], v_hi) + mm(zb_ref[0], v_lo))
        turned = jnp.concatenate(
            [spectra[plane][part * BOX : (part + 1) * BOX] for part in range(2) for plane in range(PLANES)],
            axis=0,
        )
        t_hi, t_lo = halves(turned)
        turned = mm(t_hi, yb_ref[0]) + mm(t_lo, yb_ref[0]) + mm(t_hi, yb_ref[1])
        end = BANDS * BOX
        final = jnp.concatenate(
            [turned[:mid, :end] + turned[mid:, end:], turned[mid:, :end] - turned[:mid, end:]], axis=0
        )
        q_hi, q_lo = halves(final)
        both = jnp.concatenate([q_hi, q_lo], axis=1)

        batch = 16

        def take(targets):
            for first in range(0, batch, 2):
                two = targets[first : first + 2]
                pick = jnp.concatenate([oh_y[target] for target in two], axis=1)
                found = mm(both, jnp.concatenate([pick, pick], axis=0))
                for k, target in enumerate(two):
                    at = z_id == code_z[target]
                    msg2[target] = jnp.concatenate(
                        [
                            jnp.sum(
                                jnp.where(
                                    at, found[r * BOX : (r + 1) * BOX, k * N : (k + 1) * N], 0.0
                                ),
                                axis=0,
                                keepdims=True,
                            )
                            for r in range(4)
                        ],
                        axis=0,
                    )

        def partners(step):
            return [lax.rem(me + far(batch * step + k), grid_count) for k in range(batch)]

        def send2(target):
            to_grid(msg2.at[target], got2.at[me], s2, r2, target).start()

        def take_and_send(step, carry):
            targets = partners(step)
            take(targets)
            for target in targets:
                send2(target)
            return carry

        lax.fori_loop(0, grid_count // batch - 1, take_and_send, 0)
        targets = partners(grid_count // batch - 1)
        take(targets)
        for target in targets[:-1]:
            send2(target)
        own_back = pltpu.make_async_copy(msg2.at[me], got2.at[me], out_sem)
        own_back.start()

        if band_count > 1:
            settle(dens_full.at[pl.ds(0, ROWS - share)], rf)
        dens_out = pltpu.make_async_copy(dens_full, dens_hbm, in_sem.at[0])
        dens_out.start()
        settle(got2.at[pl.ds(0, peers)], r2)
        own_back.wait()

        dens_out.wait()
        settle(msg1.at[pl.ds(0, peers)], s1)
        settle(msg2.at[pl.ds(0, peers)], s2)
        settle(d_own.at[pl.ds(0, height - 1)], sd)
        settle(d_own.at[pl.ds(0, half - height)], sx)
        mate.wait_send()
        for copies in [atom_copies] + coeff_copies:
            for copy in copies:
                copy.wait_send()
        if band_count > 1:
            settle(dens_part.at[pl.ds(0, band_count - 1)], sp)
            settle(dens_full.at[pl.ds(0, ROWS - share)], sf)
    return kernel


def finish(psi_ref, col_ref, table_ref, got_ref, dens_in, out_ref, dens_ref, work):
    back = got_ref[...].reshape(got_ref.shape[0] * 4, N).T
    b_hi, b_lo = halves(back)
    result = mm(b_hi, table_ref[0]) + mm(b_lo, table_ref[0]) + mm(b_hi, table_ref[1])
    dens_ref[...] = dens_in[...]
    work[...] = jnp.zeros_like(work)
    work[0:1, 0:COLS] = col_ref[...].astype(F32)
    codes = jnp.broadcast_to(work[0:1, :], (N, N)).T.astype(jnp.int32)[0:COLS]

    def signed(index):
        return jnp.where(index >= N // 2, index - N, index)

    fy, fz, fx = signed(codes // N), signed(codes % N), signed(iota((COLS, N), 1))
    kinetic = KINETIC * (fx * fx + fy * fy + fz * fz).astype(F32)
    for part in range(2):
        for member in range(BANDS):
            out_ref[part, member] = (
                result[member * SLOT : member * SLOT + COLS, part * N : (part + 1) * N]
                + kinetic * psi_ref[part, member]
            )


def solution(mesh):
    grid_count = mesh.shape["grid"]
    band_count = mesh.shape["band"]
    half = grid_count // 2
    constants = tables(grid_count)

    def step(psi_g, col_index, v_local, proj_values, pair_atom, pair_row, d_matrices, occupations):
        x_table, y_table, y_back, z_table, z_back = [jnp.asarray(t) for t in constants]
        hbm = pl.BlockSpec(memory_space=pl.ANY)
        dma = pltpu.SemaphoreType.DMA
        col_row = col_index.reshape(1, COLS)
        got, dens = pl.pallas_call(
            make_kernel(grid_count, band_count),
            out_shape=(
                jax.ShapeDtypeStruct((grid_count, 4, N), F32),
                jax.ShapeDtypeStruct((ROWS, N), F32),
            ),
            in_specs=[hbm] * 12 + [pl.BlockSpec(memory_space=pltpu.SMEM)],
            out_specs=(hbm, hbm),
            scratch_shapes=[
                pltpu.VMEM((2, BANDS, COLS, N), F32),
                pltpu.VMEM((1, COLS), jnp.int32),
                pltpu.VMEM((2, 2 * N, 2 * N), BF16),
                pltpu.VMEM((PROJ, ATOMS, PROJ), F32),
                pltpu.VMEM((1, PAIRS), jnp.int32),
                pltpu.VMEM((PLANES, N, N), F32),
                pltpu.VMEM((PROJ, PAIRS, N), F32),
                pltpu.VMEM((1, PAIRS), jnp.int32),
                pltpu.VMEM((2, BANDS * BOX, 2 * BANDS * N), BF16),
                pltpu.VMEM((2, 2 * N, 2 * BOX), BF16),
                pltpu.VMEM((2, 2 * BOX, 2 * N), BF16),
                pltpu.VMEM((2, BANDS * N, 2 * BANDS * BOX), BF16),
                pltpu.VMEM((PROJ, N, PAIRS), F32),
                pltpu.VMEM((BANDS * SLOT, 2 * N), F32),
                pltpu.VMEM((grid_count, 4, N), F32),
                pltpu.VMEM((grid_count, 4, N), F32),
                pltpu.VMEM((grid_count, 4, N), F32),
                pltpu.VMEM((grid_count, 1, N), jnp.int32),
                pltpu.VMEM((grid_count, BANDS * BOX, N), BF16),
                pltpu.VMEM((BANDS * BOX, 2 * PLANES * BOX), F32),
                pltpu.VMEM((COMBOS * N, ROWS), F32),
                pltpu.VMEM((COMBOS * N, PAIRS), F32),
                pltpu.VMEM((PROJ * COMBOS, PAIRS), F32),
                pltpu.VMEM((4, PROJ * COMBOS, PAIRS), F32),
                pltpu.VMEM((4, 1, PAIRS), jnp.int32),
                pltpu.VMEM((PAIRS, N), F32),
                pltpu.VMEM((N, ROWS), F32),
                pltpu.VMEM((half, 3, ATOMS, N), F32),
                pltpu.VMEM((half, 3, ATOMS, N), F32),
                pltpu.VMEM((2, 3 * N + 24, N), F32),
                pltpu.VMEM((3, ATOMS, N), F32),
                pltpu.VMEM((PROJ * COMBOS, PAIRS), F32),
                pltpu.VMEM((COMBOS, 24, PAIRS), F32),
                pltpu.VMEM((COMBOS * N, PAIRS), F32),
                pltpu.VMEM((COMBOS * N, ROWS), F32),
                pltpu.VMEM((ROWS, N), F32),
                pltpu.VMEM((band_count, ROWS // band_count, N), F32),
                pltpu.VMEM((ROWS, N), F32),
                pltpu.VMEM((8, N), F32),
                dma((12,)), dma, dma, dma((grid_count // 16,)), dma, dma, dma, dma, dma, dma, dma, dma,
                dma((4,)), dma((4,)), dma((4, 3)), dma((4, 3)), dma, dma, dma, dma,
            ],
            compiler_params=pltpu.CompilerParams(
                collective_id=0, has_side_effects=True, vmem_limit_bytes=60 << 20
            ),
        )(
            psi_g,
            col_row,
            x_table,
            d_matrices.transpose(1, 0, 2),
            pair_atom.reshape(1, PAIRS),
            v_local,
            proj_values.transpose(1, 0, 2),
            pair_row.reshape(1, PAIRS),
            y_table,
            z_table,
            z_back,
            y_back,
            occupations.reshape(1, BANDS),
        )
        out, dens = pl.pallas_call(
            finish,
            out_shape=(
                jax.ShapeDtypeStruct(psi_g.shape, F32),
                jax.ShapeDtypeStruct((ROWS, N), F32),
            ),
            in_specs=[pl.BlockSpec(memory_space=pltpu.VMEM)] * 5,
            out_specs=(pl.BlockSpec(memory_space=pltpu.VMEM),) * 2,
            scratch_shapes=[pltpu.VMEM((8, N), F32)],
            compiler_params=pltpu.CompilerParams(vmem_limit_bytes=60 << 20),
        )(psi_g, col_row, x_table, got, dens)
        return out, dens.reshape(PLANES, N, N)

    return jax.shard_map(
        step,
        mesh=mesh,
        in_specs=(
            P(None, "band", "grid", None),
            P("grid"),
            P("grid", None, None),
            P("grid", None, None),
            P("grid"),
            P("grid"),
            P("grid", None, None),
            P("band"),
        ),
        out_specs=(P(None, "band", "grid", None), P("grid", None, None)),
        check_vma=False,
    )
```

```python
import functools

import jax
import jax.numpy as jnp
import numpy as np
from jax import lax
from jax.experimental import pallas as pl
from jax.experimental.pallas import tpu as pltpu
from jax.sharding import PartitionSpec as P

MESH = pl.DeviceIdType.MESH
F32 = jnp.float32
BF16 = jnp.bfloat16
KINETIC = 0.0005

N = 128
BOX = 64
PLANES = 2
BANDS = 2
COLS = 48
SLOT = 64
PROJ = 18
PAIRS = 256
ATOMS = 8
COMBOS = 4
ROWS = PLANES * N


def split(table):
    high = table.astype(jnp.bfloat16)
    low = (table - high.astype(np.float64)).astype(jnp.bfloat16)
    return np.stack([high, low])


def tables(grid_count):
    scale = 1.0 / np.sqrt(N)
    pos = np.arange(N)
    box = np.arange(BOX)
    freq = np.where(box >= BOX // 2, box - BOX, box)

    def cos_sin(left, right):
        angle = 2.0 * np.pi / N * (np.outer(left, right) % N)
        return np.cos(angle) * scale, np.sin(angle) * scale

    cos_x, sin_x = cos_sin(pos, pos)
    x_table = np.zeros((grid_count, 2, PLANES, 2, N))
    cos_r = cos_x.reshape(grid_count, PLANES, N)
    sin_r = sin_x.reshape(grid_count, PLANES, N)
    x_table[:, 0, :, 0] = cos_r
    x_table[:, 0, :, 1] = -sin_r
    x_table[:, 1, :, 0] = sin_r
    x_table[:, 1, :, 1] = cos_r
    x_table = x_table.reshape(2 * N, 2 * N)
    cos_y, sin_y = cos_sin(freq, pos)
    y_table = np.zeros((BANDS, BOX, 2, BANDS, N))
    for band in range(BANDS):
        y_table[band, :, 0, band] = cos_y
        y_table[band, :, 1, band] = sin_y
    y_back = y_table.transpose(3, 4, 2, 0, 1).reshape(BANDS * N, 2 * BANDS * BOX)
    y_table = y_table.reshape(BANDS * BOX, 2 * BANDS * N)
    cos_z, sin_z = cos_sin(pos, freq)
    z_table = np.block([[cos_z, -sin_z], [sin_z, cos_z]])
    return [split(t) for t in (x_table, y_table, y_back, z_table, z_table.T)]


def halves(value):
    high = value.astype(BF16)
    low = (value - high.astype(F32)).astype(BF16)
    return high, low


def mm(left, right, dims=((1,), (0,))):
    return lax.dot_general(left, right, (dims, ((), ())), preferred_element_type=F32)


NT = ((1,), (1,))
TN = ((0,), (0,))


def iota(shape, dim):
    return lax.broadcasted_iota(jnp.int32, shape, dim)


def make_kernel(grid_count, band_count):
    peers = grid_count - 1
    half = grid_count // 2
    width = 4
    height = half // width

    def kernel(
        psi_in, col_in, xt_in, dmat_in, atom_in, vloc_in, proj_in, row_in, yt_in, zt_in, zb_in,
        yb_in, occ_ref,
        got2, dens_hbm,
        psi_ref, col_ref, xt_ref, dmat_ref, atom_ref, vloc_ref, proj_buf, row_ref, yt_ref, zt_ref,
        zb_ref, yb_ref, proj_t, psi_pad, msg1, got1, msg2, code_z, oh_y, box_ref,
        field, tiles, coeff, near_coeff, near_atom, atom_col, vloc_t,
        d_own, d_mate, d_slot, d_send, summed, applied, added, h_ref,
        dens_loc, dens_part, dens_full, work,
        here, all_here, in_sem, out_sem, s1, r1, s2, r2, sd, rd, sx, rx, sh, rh, sm, rm, sa, ra, sc, rc, sp, rp, sf, rf,
    ):
        me = lax.axis_index("grid")
        band = lax.axis_index("band")
        core = lax.rem(me, 2)
        chip = me // 2
        at_x = lax.rem(chip, width)
        at_y = chip // width

        def to_grid(src, dst, send, recv, target):
            return pltpu.make_async_remote_copy(
                src_ref=src, dst_ref=dst, send_sem=send, recv_sem=recv,
                device_id={"grid": target}, device_id_type=MESH,
            )

        def to_band(src, dst, send, recv, target):
            return pltpu.make_async_remote_copy(
                src_ref=src, dst_ref=dst, send_sem=send, recv_sem=recv,
                device_id={"band": target}, device_id_type=MESH,
            )

        def settle(ref, sem):
            pltpu.make_async_copy(ref, ref, sem).wait()

        def far(step):
            return half + (1 - 2 * (step % 2)) * ((step + 1) // 2)

        barrier = pltpu.get_barrier_semaphore()
        envoy = 0
        is_envoy = me == envoy

        def greet(step, carry):
            target = lax.rem(me + far(step), grid_count)

            @pl.when(target != envoy)
            def _():
                pl.semaphore_signal(
                    barrier, inc=1, device_id={"grid": target}, device_id_type=MESH
                )

            return carry

        inputs = [
            pltpu.make_async_copy(src, dst, in_sem.at[i])
            for i, (src, dst) in enumerate(
                [
                    (psi_in, psi_ref), (col_in, col_ref), (xt_in, xt_ref), (dmat_in, dmat_ref),
                    (atom_in, atom_ref), (vloc_in, vloc_ref), (proj_in, proj_buf),
                    (row_in, row_ref), (yt_in, yt_ref), (zt_in, zt_ref), (zb_in, zb_ref),
                    (yb_in, yb_ref),
                ]
            )
        ]
        for copy in inputs[:4]:
            copy.start()
        lax.fori_loop(0, peers, greet, 0, unroll=9)
        for copy in inputs[4:]:
            copy.start()

        early = band < 3
        foremost = band < 2
        middle = band == 2
        late = band >= 3
        share = ROWS // band_count
        mine = pl.ds(pl.multiple_of(band * share, share), share)

        def tell_group():
            @pl.when(is_envoy)
            def _():
                pl.semaphore_wait(barrier, band_count - 1)

                def pass_on(step, carry):
                    pl.semaphore_signal(
                        all_here, inc=1, device_id={"grid": lax.rem(me + far(step), grid_count)},
                        device_id_type=MESH,
                    )
                    return carry

                lax.fori_loop(0, peers, pass_on, 0)

        def send_parts():
            @pl.when(jnp.logical_not(is_envoy))
            def _():
                pl.semaphore_wait(all_here, 1)

            def send_part(step, carry):
                target = lax.rem(band + step, band_count)
                first = pl.multiple_of(target * share, share)
                to_band(
                    dens_loc.at[pl.ds(first, share)], dens_part.at[band], sp, rp, target
                ).start()
                return carry

            lax.fori_loop(1, band_count, send_part, 0)

        def add_parts():
            settle(dens_part.at[pl.ds(0, band_count - 1)], rp)
            dens_part[band] = dens_loc[mine, :]
            whole = dens_part[0]
            for other in range(1, band_count):
                whole += dens_part[other]
            dens_full[mine, :] = whole

            def send_full(step, carry):
                target = lax.rem(band + step, band_count)
                to_band(dens_full.at[mine], dens_full.at[mine], sf, rf, target).start()
                return carry

            lax.fori_loop(1, band_count, send_full, 0)

        psi_pad[...] = jnp.zeros_like(psi_pad)
        for copy in inputs[:4]:
            copy.wait()
        for member in range(BANDS):
            for part in range(2):
                psi_pad[member * SLOT : member * SLOT + COLS, part * N : (part + 1) * N] = psi_ref[
                    part, member
                ]
        psi_hi, psi_lo = halves(psi_pad[...])
        spread = mm(xt_ref[0], psi_hi, NT) + mm(xt_ref[1], psi_hi, NT) + mm(xt_ref[0], psi_lo, NT)
        work[...] = jnp.zeros_like(work)
        work[0:1, 0:COLS] = col_ref[...].astype(F32)
        codes = jnp.broadcast_to(work[0:1, :], (8, N))
        sub = iota((8, N), 0) % 4
        lane = iota((8, N), 1)
        pattern = jnp.where(
            sub == 0,
            pltpu.roll(codes, 48, 1),
            jnp.where(sub == 1, pltpu.roll(codes, 32, 1), pltpu.roll(codes, 16, 1)),
        )
        pattern = jnp.where((lane >= COLS) & (lane < SLOT) & (sub < 3), pattern, 0.0)
        for pair in range(grid_count // 2):
            both = spread[8 * pair : 8 * pair + 8] + pattern
            msg1[2 * pair] = both[0:4]
            msg1[2 * pair + 1] = both[4:8]
        own_copy = pltpu.make_async_copy(msg1.at[me], got1.at[me], r1.at[grid_count // 16 - 1])
        own_copy.start()
        d_send[...] = jnp.zeros_like(d_send)
        for i in range(PROJ):
            first = (i % 7) * PROJ
            d_send[i // 7, :, first : first + PROJ] = dmat_ref[i]
        d_own[at_x * height + at_y] = d_send[...]

        @pl.when(jnp.logical_not(is_envoy))
        def _():
            pl.semaphore_wait(barrier, peers)
            pl.semaphore_signal(here, inc=1, device_id={"grid": envoy}, device_id_type=MESH)

        @pl.when(is_envoy)
        def _():
            pl.semaphore_wait(here, peers)

        def send1(count, carry):
            step = peers - 1 - count
            target = lax.rem(me + far(step), grid_count)
            to_grid(msg1.at[target], got1.at[me], s1, r1.at[step // 16], target).start()
            return carry

        lax.fori_loop(0, peers, send1, 0, unroll=9)
        if band_count > 1:

            @pl.when(is_envoy)
            def _():
                for step in range(1, band_count):
                    pl.semaphore_signal(
                        barrier, inc=1, device_id={"band": lax.rem(band + step, band_count)},
                        device_id_type=MESH,
                    )

        near = [lax.rem(me + off + grid_count, grid_count) for off in (1, -1, 2, -2)]
        inputs[4].wait()
        atom_copies = [
            to_grid(atom_ref, near_atom.at[i], sa.at[i], ra.at[i], near[i]) for i in range(4)
        ]
        for copy in atom_copies:
            copy.start()

        for step in range(1, height):
            other = lax.rem(at_y + step, height) * width + at_x
            to_grid(d_send, d_own.at[at_x * height + at_y], sd, rd, 2 * other + core).start()

        inputs[5].wait()
        for plane in range(PLANES):
            vloc_t[:, plane * N : (plane + 1) * N] = vloc_ref[plane].T
        atom_row = atom_ref[...].astype(F32)
        for part in range(2):
            atom_col[part * N : (part + 1) * N, :] = jnp.broadcast_to(
                atom_row[:, part * N : (part + 1) * N], (N, N)
            ).T
        inputs[6].wait()
        for i in range(PROJ):
            for part in range(2):
                proj_t[i, :, part * N : (part + 1) * N] = proj_buf[i, part * N : (part + 1) * N, :].T

        box_ref[...] = jnp.zeros_like(box_ref)
        row_id = iota((BANDS * BOX, N), 0).astype(F32).astype(BF16)
        z_id = iota((BOX, N), 0)
        z_id16 = z_id.astype(F32).astype(BF16)
        sub = iota((8, N), 0)
        lane = iota((8, N), 1)
        one, zero = jnp.ones((), BF16), jnp.zeros((), BF16)
        code_place = lane // 16 == (sub + 3) % 8
        lane = iota((1, N), 1)
        filled = lane % SLOT < COLS
        upper = lane >= SLOT

        apart = lax.rem(me - envoy + grid_count, grid_count)
        envoy_step = jnp.where(apart > half, 2 * (apart - half), 2 * (half - apart) - 1)
        last_group = jnp.where(apart == half, 0, envoy_step // 16)
        groups = grid_count // 16

        def fill(step, carry):
            group = groups - 1 - step
            group = jnp.where(group > last_group, group, group - 1)
            group = jnp.where(step == groups - 1, last_group, group)
            with jax.named_scope("s_fillwait"):
                settle(got1.at[pl.ds(0, 16)], r1.at[group])
            total = jnp.zeros((BANDS * BOX, 2 * PLANES * BOX), F32)
            for pair in range(8):
                senders = [
                    lax.rem(me + grid_count - far(16 * group + 2 * pair + k), grid_count)
                    for k in range(2)
                ]
                data = [got1[sender] for sender in senders]
                codes = pltpu.roll(jnp.concatenate(data, axis=0), 0, 1, stride=16, stride_axis=0)
                codes = jnp.where(code_place, codes, 0.0)
                picks, highs, lows = [], [], []
                for k in range(2):
                    code = jnp.sum(codes[4 * k : 4 * k + 4], axis=0, keepdims=True)
                    code = jnp.broadcast_to(code, (8, N))
                    turned = [pltpu.roll(code, 80, 1), pltpu.roll(code, 16, 1)]
                    code = jnp.where(upper, turned[1 - k], turned[k])[0:1]
                    code = code.astype(jnp.int32)
                    at_y = jnp.where(filled, (code // N) % BOX + jnp.where(upper, BOX, 0), -1)
                    at_z = jnp.where(filled, code % BOX, -1)
                    code_z[senders[k]] = at_z
                    picker = jnp.where(row_id == at_y.astype(F32).astype(BF16), one, zero)
                    oh_y[senders[k]] = picker
                    picks.append(picker)
                    high, rest = halves(data[k])
                    at = z_id16 == at_z.astype(F32).astype(BF16)
                    for value, store in ((high, highs), (rest, lows)):
                        store.append(
                            jnp.concatenate(
                                [jnp.where(at, value[r : r + 1], zero) for r in range(4)], axis=0
                            )
                        )
                pick = jnp.concatenate(picks, axis=1)
                total += mm(pick, jnp.concatenate(highs, axis=1), NT)
                total += mm(pick, jnp.concatenate(lows, axis=1), NT)
            box_ref[...] += total
            return carry

        lax.fori_loop(0, groups - 1, fill, 0)
        settle(d_own.at[pl.ds(0, height - 1)], rd)

        def column(offset, first=0, count=height):
            return pl.ds(lax.rem(at_x + offset + width, width) * height + first, count)

        def along_x(offset):
            return 2 * (at_y * width + lax.rem(at_x + offset + width, width)) + core

        def to_mate(block):
            to_grid(d_own.at[block], d_mate.at[block], sm, rm, 2 * chip + 1 - core).start()

        for offset in (1, -1):
            block = d_own.at[column(0)]
            to_grid(block, block, sx, rx, along_x(offset)).start()
        if band_count > 1:

            @pl.when(jnp.logical_not(early))
            def _():
                tell_group()

        lax.fori_loop(groups - 1, groups, fill, 0)
        for copy in inputs[7:]:
            copy.wait()
        box_hi, box_lo = halves(box_ref[...].T)
        turned = mm(box_hi, yt_ref[0]) + mm(box_lo, yt_ref[0]) + mm(box_hi, yt_ref[1])
        mid, end = PLANES * BOX, BANDS * N
        part_re = turned[:mid, :end] - turned[mid:, end:]
        part_im = turned[:mid, end:] + turned[mid:, :end]
        for plane in range(PLANES):
            here = slice(plane * BOX, (plane + 1) * BOX)
            value = jnp.concatenate([part_re[here], part_im[here]], axis=0)
            v_hi, v_lo = halves(value)
            wave = mm(zt_ref[0], v_hi) + mm(zt_ref[1], v_hi) + mm(zt_ref[0], v_lo)
            for part in range(2):
                for member in range(BANDS):
                    first = (part * BANDS + member) * N
                    field[first : first + N, plane * N : (plane + 1) * N] = wave[
                        part * N : (part + 1) * N, member * N : (member + 1) * N
                    ]

        settle(d_own.at[pl.ds(0, 2 * height)], rx)
        for offset, first in ((1, 0), (-1, height // 2)):
            block = d_own.at[column(-offset, first, height // 2)]
            to_grid(block, block, sh, rh, along_x(offset)).start()
        for offset in (0, 1, -1):
            to_mate(column(offset))

        dens_t = jnp.zeros((N, ROWS), F32)
        for member in range(BANDS):
            real = field[member * N : (member + 1) * N, :]
            imag = field[(BANDS + member) * N : (BANDS + member + 1) * N, :]
            dens_t += occ_ref[0, member] * (real * real + imag * imag)
        for plane in range(PLANES):
            dens_loc[plane * N : (plane + 1) * N, :] = dens_t[:, plane * N : (plane + 1) * N].T

        if band_count > 1:

            @pl.when(early)
            def _():
                tell_group()

            @pl.when(jnp.logical_not(early))
            def _():
                send_parts()

        local_row = row_ref[...] - me * ROWS
        row_pick = jnp.where(iota((ROWS, PAIRS), 0) == local_row, 1.0, 0.0).astype(BF16)
        f_hi, f_lo = halves(field[...])
        tiles[...] = mm(f_hi, row_pick) + mm(f_lo, row_pick)

        def project(step, carry):
            found = []
            for k in range(2):
                values = proj_t[2 * step + k]
                for combo in range(COMBOS):
                    found.append(
                        jnp.sum(values * tiles[combo * N : (combo + 1) * N, :], axis=0, keepdims=True)
                    )
            coeff[pl.ds(pl.multiple_of(step * 8, 8), 8), :] = jnp.concatenate(found, axis=0)
            return carry

        coeff_copies = []
        for part in range(3):
            lax.fori_loop(3 * part, 3 * part + 3, project, 0)
            rows = pl.ds(24 * part, 24)
            coeff_copies.append(
                [
                    to_grid(
                        coeff.at[rows], near_coeff.at[i, rows], sc.at[i, part], rc.at[i, part], near[i]
                    )
                    for i in range(4)
                ]
            )
            for copy in coeff_copies[-1]:
                copy.start()

        if band_count > 1:

            @pl.when(early)
            def _():
                send_parts()

        settle(d_own.at[pl.ds(0, height)], rh)
        to_mate(column(2))
        place = iota((half * ATOMS, PAIRS), 0)
        slot = place // ATOMS
        atom_base = ((slot % height) * width + slot // height) * (2 * ATOMS) + place % ATOMS
        atoms = atom_ref[...]
        own_pick = jnp.where(atom_base + core * ATOMS == atoms, 1.0, 0.0).astype(BF16)
        mate_pick = jnp.where(atom_base + (1 - core) * ATOMS == atoms, 1.0, 0.0).astype(BF16)
        for q in range(3):
            d_hi, d_lo = halves(d_own[:, q].reshape(half * ATOMS, N))
            slots = mm(d_hi, own_pick, TN) + mm(d_lo, own_pick, TN)
            for lanes in range(2):
                d_slot[lanes, q * N : (q + 1) * N, :] = slots[:, lanes * N : (lanes + 1) * N]
        settle(d_mate, rm)
        for q in range(3):
            d_hi, d_lo = halves(d_mate[:, q].reshape(half * ATOMS, N))
            slots = mm(d_hi, mate_pick, TN) + mm(d_lo, mate_pick, TN)
            for lanes in range(2):
                d_slot[lanes, q * N : (q + 1) * N, :] += slots[:, lanes * N : (lanes + 1) * N]

        if band_count > 1:

            @pl.when(late)
            def _():
                add_parts()

        for copy in atom_copies:
            copy.wait_recv()
        column = jnp.concatenate([atom_col[...], atom_col[...]], axis=1)

        def same(other_row):
            return jnp.where(column == other_row.astype(F32), 1.0, 0.0).astype(BF16)

        c_hi, c_lo = halves(coeff[...])
        pick = same(atoms)
        total = mm(c_hi, pick, NT) + mm(c_lo, pick, NT)
        for i in range(4):
            with jax.named_scope("s_coefwait"):
                for part in range(3):
                    coeff_copies[part][i].wait_recv()
            c_hi, c_lo = halves(near_coeff[i])
            pick = same(near_atom[i])
            total += mm(c_hi, pick, NT) + mm(c_lo, pick, NT)
        summed[...] = total

        d_slot[:, 3 * N :, :] = jnp.zeros((2, 24, N), F32)
        values = [jnp.zeros((24, PAIRS), F32) for _ in range(COMBOS)]
        for j in range(PROJ):
            part = jnp.concatenate(
                [
                    jnp.concatenate(
                        [d_slot[lanes, pl.ds(q * N + j, 8, stride=PROJ), :] for lanes in range(2)],
                        axis=1,
                    )
                    for q in range(3)
                ],
                axis=0,
            )
            for combo in range(COMBOS):
                row = j * COMBOS + combo
                values[combo] += part * summed[row : row + 1, :]
        for combo in range(COMBOS):
            applied[combo] = values[combo]

        depth = 32

        def spread_back(step, carry):
            first = pl.multiple_of(step * depth, depth)
            totals = [jnp.zeros((depth, PAIRS), F32) for _ in range(COMBOS)]
            for i in range(PROJ):
                values = proj_t[i, pl.ds(first, depth), :]
                for combo in range(COMBOS):
                    totals[combo] += values * applied[combo, 8 * (i // 7) + i % 7 : 8 * (i // 7) + i % 7 + 1, :]
            for combo in range(COMBOS):
                added[pl.ds(pl.multiple_of(combo * N + first, depth), depth), :] = totals[combo]
            return carry

        lax.fori_loop(0, N // depth, spread_back, 0)
        a_hi, a_lo = halves(added[...])
        projected = mm(a_hi, row_pick, NT) + mm(a_lo, row_pick, NT)
        for combo in range(COMBOS):
            here = slice(combo * N, (combo + 1) * N)
            h_ref[here, :] = vloc_t[...] * field[here, :] + projected[here]

        spectra = []
        for plane in range(PLANES):
            lanes = slice(plane * N, (plane + 1) * N)
            value = jnp.concatenate(
                [
                    jnp.concatenate(
                        [
                            h_ref[(part * BANDS + member) * N : (part * BANDS + member + 1) * N, lanes]
                            for member in range(BANDS)
                        ],
                        axis=1,
                    )
                    for part in range(2)
                ],
                axis=0,
            )
            v_hi, v_lo = halves(value)
            spectra.append(mm(zb_ref[0], v_hi) + mm(zb_ref[1], v_hi) + mm(zb_ref[0], v_lo))
        turned = jnp.concatenate(
            [spectra[plane][part * BOX : (part + 1) * BOX] for part in range(2) for plane in range(PLANES)],
            axis=0,
        )
        t_hi, t_lo = halves(turned)
        turned = mm(t_hi, yb_ref[0]) + mm(t_lo, yb_ref[0]) + mm(t_hi, yb_ref[1])
        end = BANDS * BOX
        final = jnp.concatenate(
            [turned[:mid, :end] + turned[mid:, end:], turned[mid:, :end] - turned[:mid, end:]], axis=0
        )
        q_hi, q_lo = halves(final)
        both = jnp.concatenate([q_hi, q_lo], axis=1)

        if band_count > 1:

            @pl.when(middle)
            def _():
                add_parts()

        batch = 16

        def take(targets):
            for first in range(0, batch, 2):
                two = targets[first : first + 2]
                pick = jnp.concatenate([oh_y[target] for target in two], axis=1)
                found = mm(both, jnp.concatenate([pick, pick], axis=0))
                for k, target in enumerate(two):
                    at = z_id == code_z[target]
                    msg2[target] = jnp.concatenate(
                        [
                            jnp.sum(
                                jnp.where(
                                    at, found[r * BOX : (r + 1) * BOX, k * N : (k + 1) * N], 0.0
                                ),
                                axis=0,
                                keepdims=True,
                            )
                            for r in range(4)
                        ],
                        axis=0,
                    )

        def partners(step):
            return [lax.rem(me + far(batch * step + k), grid_count) for k in range(batch)]

        def send2(target):
            to_grid(msg2.at[target], got2.at[me], s2, r2, target).start()

        def take_and_send(step, carry):
            targets = partners(step)
            take(targets)
            for target in targets:
                send2(target)
            return carry

        lax.fori_loop(0, grid_count // batch - 1, take_and_send, 0)
        targets = partners(grid_count // batch - 1)
        take(targets)
        for target in targets[:-1]:
            send2(target)
        own_back = pltpu.make_async_copy(msg2.at[me], got2.at[me], out_sem)
        own_back.start()

        if band_count > 1:

            @pl.when(foremost)
            def _():
                add_parts()

            settle(dens_full.at[pl.ds(0, ROWS - share)], rf)
        dens_out = pltpu.make_async_copy(dens_full, dens_hbm, in_sem.at[0])
        dens_out.start()
        settle(got2.at[pl.ds(0, peers)], r2)
        own_back.wait()

        dens_out.wait()
        settle(msg1.at[pl.ds(0, peers)], s1)
        settle(msg2.at[pl.ds(0, peers)], s2)
        settle(d_own.at[pl.ds(0, height - 1)], sd)
        settle(d_own.at[pl.ds(0, 2 * height)], sx)
        settle(d_own.at[pl.ds(0, height)], sh)
        settle(d_mate, sm)
        for copies in [atom_copies] + coeff_copies:
            for copy in copies:
                copy.wait_send()
        if band_count > 1:
            settle(dens_part.at[pl.ds(0, band_count - 1)], sp)
            settle(dens_full.at[pl.ds(0, ROWS - share)], sf)
    return kernel


def finish(psi_ref, col_ref, table_ref, got_ref, dens_in, out_ref, dens_ref, work):
    back = got_ref[...].reshape(got_ref.shape[0] * 4, N).T
    b_hi, b_lo = halves(back)
    result = mm(b_hi, table_ref[0]) + mm(b_lo, table_ref[0]) + mm(b_hi, table_ref[1])
    dens_ref[...] = dens_in[...]
    work[...] = jnp.zeros_like(work)
    work[0:1, 0:COLS] = col_ref[...].astype(F32)
    codes = jnp.broadcast_to(work[0:1, :], (N, N)).T.astype(jnp.int32)[0:COLS]

    def signed(index):
        return jnp.where(index >= N // 2, index - N, index)

    fy, fz, fx = signed(codes // N), signed(codes % N), signed(iota((COLS, N), 1))
    kinetic = KINETIC * (fx * fx + fy * fy + fz * fz).astype(F32)
    for part in range(2):
        for member in range(BANDS):
            out_ref[part, member] = (
                result[member * SLOT : member * SLOT + COLS, part * N : (part + 1) * N]
                + kinetic * psi_ref[part, member]
            )


def solution(mesh):
    grid_count = mesh.shape["grid"]
    band_count = mesh.shape["band"]
    half = grid_count // 2
    constants = tables(grid_count)

    def step(psi_g, col_index, v_local, proj_values, pair_atom, pair_row, d_matrices, occupations):
        x_table, y_table, y_back, z_table, z_back = [jnp.asarray(t) for t in constants]
        hbm = pl.BlockSpec(memory_space=pl.ANY)
        dma = pltpu.SemaphoreType.DMA
        col_row = col_index.reshape(1, COLS)
        got, dens = pl.pallas_call(
            make_kernel(grid_count, band_count),
            out_shape=(
                jax.ShapeDtypeStruct((grid_count, 4, N), F32),
                jax.ShapeDtypeStruct((ROWS, N), F32),
            ),
            in_specs=[hbm] * 12 + [pl.BlockSpec(memory_space=pltpu.SMEM)],
            out_specs=(hbm, hbm),
            scratch_shapes=[
                pltpu.VMEM((2, BANDS, COLS, N), F32),
                pltpu.VMEM((1, COLS), jnp.int32),
                pltpu.VMEM((2, 2 * N, 2 * N), BF16),
                pltpu.VMEM((PROJ, ATOMS, PROJ), F32),
                pltpu.VMEM((1, PAIRS), jnp.int32),
                pltpu.VMEM((PLANES, N, N), F32),
                pltpu.VMEM((PROJ, PAIRS, N), F32),
                pltpu.VMEM((1, PAIRS), jnp.int32),
                pltpu.VMEM((2, BANDS * BOX, 2 * BANDS * N), BF16),
                pltpu.VMEM((2, 2 * N, 2 * BOX), BF16),
                pltpu.VMEM((2, 2 * BOX, 2 * N), BF16),
                pltpu.VMEM((2, BANDS * N, 2 * BANDS * BOX), BF16),
                pltpu.VMEM((PROJ, N, PAIRS), F32),
                pltpu.VMEM((BANDS * SLOT, 2 * N), F32),
                pltpu.VMEM((grid_count, 4, N), F32),
                pltpu.VMEM((grid_count, 4, N), F32),
                pltpu.VMEM((grid_count, 4, N), F32),
                pltpu.VMEM((grid_count, 1, N), jnp.int32),
                pltpu.VMEM((grid_count, BANDS * BOX, N), BF16),
                pltpu.VMEM((BANDS * BOX, 2 * PLANES * BOX), F32),
                pltpu.VMEM((COMBOS * N, ROWS), F32),
                pltpu.VMEM((COMBOS * N, PAIRS), F32),
                pltpu.VMEM((PROJ * COMBOS, PAIRS), F32),
                pltpu.VMEM((4, PROJ * COMBOS, PAIRS), F32),
                pltpu.VMEM((4, 1, PAIRS), jnp.int32),
                pltpu.VMEM((PAIRS, N), F32),
                pltpu.VMEM((N, ROWS), F32),
                pltpu.VMEM((half, 3, ATOMS, N), F32),
                pltpu.VMEM((half, 3, ATOMS, N), F32),
                pltpu.VMEM((2, 3 * N + 24, N), F32),
                pltpu.VMEM((3, ATOMS, N), F32),
                pltpu.VMEM((PROJ * COMBOS, PAIRS), F32),
                pltpu.VMEM((COMBOS, 24, PAIRS), F32),
                pltpu.VMEM((COMBOS * N, PAIRS), F32),
                pltpu.VMEM((COMBOS * N, ROWS), F32),
                pltpu.VMEM((ROWS, N), F32),
                pltpu.VMEM((band_count, ROWS // band_count, N), F32),
                pltpu.VMEM((ROWS, N), F32),
                pltpu.VMEM((8, N), F32),
                pltpu.SemaphoreType.REGULAR, pltpu.SemaphoreType.REGULAR,
                dma((12,)), dma, dma, dma((grid_count // 16,)), dma, dma, dma, dma, dma, dma, dma, dma, dma, dma,
                dma((4,)), dma((4,)), dma((4, 3)), dma((4, 3)), dma, dma, dma, dma,
            ],
            compiler_params=pltpu.CompilerParams(
                collective_id=0, has_side_effects=True, vmem_limit_bytes=60 << 20
            ),
        )(
            psi_g,
            col_row,
            x_table,
            d_matrices.transpose(1, 0, 2),
            pair_atom.reshape(1, PAIRS),
            v_local,
            proj_values.transpose(1, 0, 2),
            pair_row.reshape(1, PAIRS),
            y_table,
            z_table,
            z_back,
            y_back,
            occupations.reshape(1, BANDS),
        )
        out, dens = pl.pallas_call(
            finish,
            out_shape=(
                jax.ShapeDtypeStruct(psi_g.shape, F32),
                jax.ShapeDtypeStruct((ROWS, N), F32),
            ),
            in_specs=[pl.BlockSpec(memory_space=pltpu.VMEM)] * 5,
            out_specs=(pl.BlockSpec(memory_space=pltpu.VMEM),) * 2,
            scratch_shapes=[pltpu.VMEM((8, N), F32)],
            compiler_params=pltpu.CompilerParams(vmem_limit_bytes=60 << 20),
        )(psi_g, col_row, x_table, got, dens)
        return out, dens.reshape(PLANES, N, N)

    return jax.shard_map(
        step,
        mesh=mesh,
        in_specs=(
            P(None, "band", "grid", None),
            P("grid"),
            P("grid", None, None),
            P("grid", None, None),
            P("grid"),
            P("grid"),
            P("grid", None, None),
            P("band"),
        ),
        out_specs=(P(None, "band", "grid", None), P("grid", None, None)),
        check_vma=False,
    )
```

```python
import functools

import jax
import jax.numpy as jnp
import numpy as np
from jax import lax
from jax.experimental import pallas as pl
from jax.experimental.pallas import tpu as pltpu
from jax.sharding import PartitionSpec as P

MESH = pl.DeviceIdType.MESH
F32 = jnp.float32
BF16 = jnp.bfloat16
KINETIC = 0.0005

N = 128
BOX = 64
PLANES = 2
BANDS = 2
COLS = 48
SLOT = 64
PROJ = 18
PAIRS = 256
ATOMS = 8
COMBOS = 4
ROWS = PLANES * N


def split(table):
    high = table.astype(jnp.bfloat16)
    low = (table - high.astype(np.float64)).astype(jnp.bfloat16)
    return np.stack([high, low])


def tables(grid_count):
    scale = 1.0 / np.sqrt(N)
    pos = np.arange(N)
    box = np.arange(BOX)
    freq = np.where(box >= BOX // 2, box - BOX, box)

    def cos_sin(left, right):
        angle = 2.0 * np.pi / N * (np.outer(left, right) % N)
        return np.cos(angle) * scale, np.sin(angle) * scale

    cos_x, sin_x = cos_sin(pos, pos)
    x_table = np.zeros((grid_count, 2, PLANES, 2, N))
    cos_r = cos_x.reshape(grid_count, PLANES, N)
    sin_r = sin_x.reshape(grid_count, PLANES, N)
    x_table[:, 0, :, 0] = cos_r
    x_table[:, 0, :, 1] = -sin_r
    x_table[:, 1, :, 0] = sin_r
    x_table[:, 1, :, 1] = cos_r
    x_table = x_table.reshape(2 * N, 2 * N)
    cos_y, sin_y = cos_sin(freq, pos)
    y_table = np.zeros((BANDS, BOX, 2, BANDS, N))
    for band in range(BANDS):
        y_table[band, :, 0, band] = cos_y
        y_table[band, :, 1, band] = sin_y
    y_back = y_table.transpose(3, 4, 2, 0, 1).reshape(BANDS * N, 2 * BANDS * BOX)
    y_table = y_table.reshape(BANDS * BOX, 2 * BANDS * N)
    cos_z, sin_z = cos_sin(pos, freq)
    z_table = np.block([[cos_z, -sin_z], [sin_z, cos_z]])
    return [split(t) for t in (x_table, y_table, y_back, z_table, z_table.T)]


def halves(value):
    high = value.astype(BF16)
    low = (value - high.astype(F32)).astype(BF16)
    return high, low


def mm(left, right, dims=((1,), (0,))):
    return lax.dot_general(left, right, (dims, ((), ())), preferred_element_type=F32)


NT = ((1,), (1,))
TN = ((0,), (0,))


def iota(shape, dim):
    return lax.broadcasted_iota(jnp.int32, shape, dim)


def make_kernel(grid_count, band_count):
    peers = grid_count - 1
    half = grid_count // 2
    width = 4
    height = half // width

    def kernel(
        psi_in, col_in, xt_in, dmat_in, atom_in, vloc_in, proj_in, row_in, yt_in, zt_in, zb_in,
        yb_in, occ_ref,
        got2, dens_hbm,
        psi_ref, col_ref, xt_ref, dmat_ref, atom_ref, vloc_ref, proj_buf, row_ref, yt_ref, zt_ref,
        zb_ref, yb_ref, proj_t, psi_pad, msg1, got1, msg2, code_z, oh_y, box_ref,
        field, tiles, coeff, near_coeff, near_atom, atom_col, vloc_t,
        d_own, d_mate, d_slot, d_send, summed, applied, added, h_ref,
        dens_loc, dens_part, dens_full, work, row_pick, d_pick, same,
        here, all_here, in_sem, out_sem, s1, r1, s2, r2, sd, rd, sx, rx, sm, rm, sa, ra, sc, rc, sp, rp, sf, rf,
    ):
        me = lax.axis_index("grid")
        band = lax.axis_index("band")
        core = lax.rem(me, 2)
        chip = me // 2
        at_x = lax.rem(chip, width)
        at_y = chip // width

        def to_grid(src, dst, send, recv, target):
            return pltpu.make_async_remote_copy(
                src_ref=src, dst_ref=dst, send_sem=send, recv_sem=recv,
                device_id={"grid": target}, device_id_type=MESH,
            )

        def to_band(src, dst, send, recv, target):
            return pltpu.make_async_remote_copy(
                src_ref=src, dst_ref=dst, send_sem=send, recv_sem=recv,
                device_id={"band": target}, device_id_type=MESH,
            )

        def settle(ref, sem):
            pltpu.make_async_copy(ref, ref, sem).wait()

        def far(step):
            return half + (1 - 2 * (step % 2)) * ((step + 1) // 2)

        barrier = pltpu.get_barrier_semaphore()
        envoy = 0
        is_envoy = me == envoy

        apart = lax.rem(me - envoy + grid_count, grid_count)
        envoy_step = jnp.where(apart > half, 2 * (apart - half), 2 * (half - apart) - 1)
        last_group = jnp.where(apart == half, 0, envoy_step // 16)
        groups = grid_count // 16

        def greet(step, carry):
            target = lax.rem(me + far(step), grid_count)

            @pl.when(target != envoy)
            def _():
                pl.semaphore_signal(
                    barrier, inc=1, device_id={"grid": target}, device_id_type=MESH
                )

            return carry

        inputs = [
            pltpu.make_async_copy(src, dst, in_sem.at[i])
            for i, (src, dst) in enumerate(
                [
                    (psi_in, psi_ref), (col_in, col_ref), (xt_in, xt_ref), (dmat_in, dmat_ref),
                    (atom_in, atom_ref), (vloc_in, vloc_ref), (proj_in, proj_buf),
                    (row_in, row_ref), (yt_in, yt_ref), (zt_in, zt_ref), (zb_in, zb_ref),
                    (yb_in, yb_ref),
                ]
            )
        ]
        for copy in inputs[:4]:
            copy.start()
        lax.fori_loop(0, peers, greet, 0, unroll=9)
        for copy in inputs[4:]:
            copy.start()

        early = band < 3
        foremost = band < 2
        middle = band == 2
        late = band >= 3
        share = ROWS // band_count
        mine = pl.ds(pl.multiple_of(band * share, share), share)

        def tell_group():
            @pl.when(is_envoy)
            def _():
                pl.semaphore_wait(barrier, band_count - 1)

                def pass_on(step, carry):
                    pl.semaphore_signal(
                        all_here, inc=1, device_id={"grid": lax.rem(me + far(step), grid_count)},
                        device_id_type=MESH,
                    )
                    return carry

                lax.fori_loop(0, peers, pass_on, 0)

        def send_parts():
            @pl.when(jnp.logical_not(is_envoy))
            def _():
                pl.semaphore_wait(all_here, 1)

            def send_part(step, carry):
                target = lax.rem(band + step, band_count)
                first = pl.multiple_of(target * share, share)
                to_band(
                    dens_loc.at[pl.ds(first, share)], dens_part.at[band], sp, rp, target
                ).start()
                return carry

            lax.fori_loop(1, band_count, send_part, 0)

        def add_parts():
            settle(dens_part.at[pl.ds(0, band_count - 1)], rp)
            dens_part[band] = dens_loc[mine, :]
            whole = dens_part[0]
            for other in range(1, band_count):
                whole += dens_part[other]
            dens_full[mine, :] = whole

            def send_full(step, carry):
                target = lax.rem(band + step, band_count)
                to_band(dens_full.at[mine], dens_full.at[mine], sf, rf, target).start()
                return carry

            lax.fori_loop(1, band_count, send_full, 0)

        psi_pad[...] = jnp.zeros_like(psi_pad)
        for copy in inputs[:4]:
            copy.wait()
        for member in range(BANDS):
            for part in range(2):
                psi_pad[member * SLOT : member * SLOT + COLS, part * N : (part + 1) * N] = psi_ref[
                    part, member
                ]
        psi_hi, psi_lo = halves(psi_pad[...])
        spread = mm(xt_ref[0], psi_hi, NT) + mm(xt_ref[1], psi_hi, NT) + mm(xt_ref[0], psi_lo, NT)
        work[...] = jnp.zeros_like(work)
        work[0:1, 0:COLS] = col_ref[...].astype(F32)
        codes = jnp.broadcast_to(work[0:1, :], (8, N))
        sub = iota((8, N), 0) % 4
        lane = iota((8, N), 1)
        pattern = jnp.where(
            sub == 0,
            pltpu.roll(codes, 48, 1),
            jnp.where(sub == 1, pltpu.roll(codes, 32, 1), pltpu.roll(codes, 16, 1)),
        )
        pattern = jnp.where((lane >= COLS) & (lane < SLOT) & (sub < 3), pattern, 0.0)
        for pair in range(grid_count // 2):
            both = spread[8 * pair : 8 * pair + 8] + pattern
            msg1[2 * pair] = both[0:4]
            msg1[2 * pair + 1] = both[4:8]
        own_copy = pltpu.make_async_copy(msg1.at[me], got1.at[me], r1.at[grid_count // 16 - 1])
        own_copy.start()
        d_send[...] = jnp.zeros_like(d_send)
        for i in range(PROJ):
            first = (i % 7) * PROJ
            d_send[i // 7, :, first : first + PROJ] = dmat_ref[i]
        d_own[at_x * height + at_y] = d_send[...]

        @pl.when(jnp.logical_not(is_envoy))
        def _():
            pl.semaphore_wait(barrier, peers)
            pl.semaphore_signal(
                here.at[last_group], inc=1, device_id={"grid": envoy}, device_id_type=MESH
            )

        def send1(count, carry):
            step = peers - 1 - count
            target = lax.rem(me + far(step), grid_count)
            to_grid(msg1.at[target], got1.at[me], s1, r1.at[step // 16], target).start()
            return carry

        @pl.when(jnp.logical_not(is_envoy))
        def _():
            lax.fori_loop(0, peers, send1, 0, unroll=9)

        @pl.when(is_envoy)
        def _():
            for group in range(groups):
                sent = max(16 * group - 1, 0)
                pl.semaphore_wait(here.at[groups - 1 - group], 16 * group + 15 - sent)
                lax.fori_loop(sent, 16 * group + 15, send1, 0)

        if band_count > 1:

            @pl.when(is_envoy)
            def _():
                for step in range(1, band_count):
                    pl.semaphore_signal(
                        barrier, inc=1, device_id={"band": lax.rem(band + step, band_count)},
                        device_id_type=MESH,
                    )

        near = [lax.rem(me + off + grid_count, grid_count) for off in (1, -1, 2, -2)]
        inputs[4].wait()
        atom_copies = [
            to_grid(atom_ref, near_atom.at[i], sa.at[i], ra.at[i], near[i]) for i in range(4)
        ]
        for copy in atom_copies:
            copy.start()

        for step in range(1, height):
            other = lax.rem(at_y + step, height) * width + at_x
            to_grid(d_send, d_own.at[at_x * height + at_y], sd, rd, 2 * other + core).start()

        inputs[5].wait()
        for plane in range(PLANES):
            vloc_t[:, plane * N : (plane + 1) * N] = vloc_ref[plane].T
        atom_row = atom_ref[...].astype(F32)
        for part in range(2):
            atom_col[part * N : (part + 1) * N, :] = jnp.broadcast_to(
                atom_row[:, part * N : (part + 1) * N], (N, N)
            ).T
        for copy in inputs[6:]:
            copy.wait()
        for i in range(PROJ):
            for part in range(2):
                proj_t[i, :, part * N : (part + 1) * N] = proj_buf[i, part * N : (part + 1) * N, :].T

        local_row = row_ref[...] - me * ROWS
        row_pick[...] = jnp.where(iota((ROWS, PAIRS), 0) == local_row, 1.0, 0.0).astype(BF16)
        atoms = atom_ref[...]
        place = iota((half * ATOMS, PAIRS), 0)
        slot = place // ATOMS
        atom_base = ((slot % height) * width + slot // height) * (2 * ATOMS) + place % ATOMS
        for which in range(2):
            shift = jnp.where(which == 0, core, 1 - core) * ATOMS
            d_pick[which] = jnp.where(atom_base + shift == atoms, 1.0, 0.0).astype(BF16)
        wide = jnp.concatenate([atom_col[...], atom_col[...]], axis=1)
        same[0] = jnp.where(wide == atom_row, 1.0, 0.0).astype(BF16)
        for i in range(4):
            atom_copies[i].wait_recv()
            same[1 + i] = jnp.where(wide == near_atom[i].astype(F32), 1.0, 0.0).astype(BF16)

        box_ref[...] = jnp.zeros_like(box_ref)
        row_id = iota((BANDS * BOX, N), 0).astype(F32).astype(BF16)
        z_id = iota((BOX, N), 0)
        z_id16 = z_id.astype(F32).astype(BF16)
        sub = iota((8, N), 0)
        lane = iota((8, N), 1)
        one, zero = jnp.ones((), BF16), jnp.zeros((), BF16)
        code_place = lane // 16 == (sub + 3) % 8
        lane = iota((1, N), 1)
        filled = lane % SLOT < COLS
        upper = lane >= SLOT

        def fill(step, carry):
            group = groups - 1 - step
            group = jnp.where(group > last_group, group, group - 1)
            group = jnp.where(step == groups - 1, last_group, group)
            with jax.named_scope("s_fillwait"):
                settle(got1.at[pl.ds(0, 16)], r1.at[group])
            total = jnp.zeros((BANDS * BOX, 2 * PLANES * BOX), F32)
            for pair in range(8):
                senders = [
                    lax.rem(me + grid_count - far(16 * group + 2 * pair + k), grid_count)
                    for k in range(2)
                ]
                data = [got1[sender] for sender in senders]
                codes = pltpu.roll(jnp.concatenate(data, axis=0), 0, 1, stride=16, stride_axis=0)
                codes = jnp.where(code_place, codes, 0.0)
                picks, highs, lows = [], [], []
                for k in range(2):
                    code = jnp.sum(codes[4 * k : 4 * k + 4], axis=0, keepdims=True)
                    code = jnp.broadcast_to(code, (8, N))
                    turned = [pltpu.roll(code, 80, 1), pltpu.roll(code, 16, 1)]
                    code = jnp.where(upper, turned[1 - k], turned[k])[0:1]
                    code = code.astype(jnp.int32)
                    at_y = jnp.where(filled, (code // N) % BOX + jnp.where(upper, BOX, 0), -1)
                    at_z = jnp.where(filled, code % BOX, -1)
                    code_z[senders[k]] = at_z
                    picker = jnp.where(row_id == at_y.astype(F32).astype(BF16), one, zero)
                    oh_y[senders[k]] = picker
                    picks.append(picker)
                    high, rest = halves(data[k])
                    at = z_id16 == at_z.astype(F32).astype(BF16)
                    for value, store in ((high, highs), (rest, lows)):
                        store.append(
                            jnp.concatenate(
                                [jnp.where(at, value[r : r + 1], zero) for r in range(4)], axis=0
                            )
                        )
                pick = jnp.concatenate(picks, axis=1)
                total += mm(pick, jnp.concatenate(highs, axis=1), NT)
                total += mm(pick, jnp.concatenate(lows, axis=1), NT)
            box_ref[...] += total
            return carry

        lax.fori_loop(0, groups // 2, fill, 0)
        if band_count > 1:

            @pl.when(jnp.logical_not(early))
            def _():
                tell_group()

        lax.fori_loop(groups // 2, groups - 1, fill, 0)
        settle(d_own.at[pl.ds(0, height - 1)], rd)

        def column(offset):
            return pl.ds(lax.rem(at_x + offset + width, width) * height, height)

        for i, offset in enumerate((2, 1, -1)):
            block = d_own.at[column(0)]
            target = 2 * (at_y * width + lax.rem(at_x + offset + width, width)) + core
            to_grid(block, block, sx.at[i], rx.at[i], target).start()

        def to_mate(block):
            to_grid(d_own.at[block], d_mate.at[block], sm, rm, 2 * chip + 1 - core).start()

        to_mate(column(0))
        lax.fori_loop(groups - 1, groups, fill, 0)

        box_hi, box_lo = halves(box_ref[...].T)
        turned = mm(box_hi, yt_ref[0]) + mm(box_lo, yt_ref[0]) + mm(box_hi, yt_ref[1])
        mid, end = PLANES * BOX, BANDS * N
        part_re = turned[:mid, :end] - turned[mid:, end:]
        part_im = turned[:mid, end:] + turned[mid:, :end]
        for plane in range(PLANES):
            here = slice(plane * BOX, (plane + 1) * BOX)
            value = jnp.concatenate([part_re[here], part_im[here]], axis=0)
            v_hi, v_lo = halves(value)
            wave = mm(zt_ref[0], v_hi) + mm(zt_ref[1], v_hi) + mm(zt_ref[0], v_lo)
            for part in range(2):
                for member in range(BANDS):
                    first = (part * BANDS + member) * N
                    field[first : first + N, plane * N : (plane + 1) * N] = wave[
                        part * N : (part + 1) * N, member * N : (member + 1) * N
                    ]

        dens_t = jnp.zeros((N, ROWS), F32)
        for member in range(BANDS):
            real = field[member * N : (member + 1) * N, :]
            imag = field[(BANDS + member) * N : (BANDS + member + 1) * N, :]
            dens_t += occ_ref[0, member] * (real * real + imag * imag)
        for plane in range(PLANES):
            dens_loc[plane * N : (plane + 1) * N, :] = dens_t[:, plane * N : (plane + 1) * N].T

        if band_count > 1:

            @pl.when(early)
            def _():
                tell_group()

            @pl.when(jnp.logical_not(early))
            def _():
                send_parts()

        f_hi, f_lo = halves(field[...])
        tiles[...] = mm(f_hi, row_pick[...]) + mm(f_lo, row_pick[...])

        def project(step, carry):
            found = []
            for k in range(2):
                values = proj_t[2 * step + k]
                for combo in range(COMBOS):
                    found.append(
                        jnp.sum(values * tiles[combo * N : (combo + 1) * N, :], axis=0, keepdims=True)
                    )
            coeff[pl.ds(pl.multiple_of(step * 8, 8), 8), :] = jnp.concatenate(found, axis=0)
            return carry

        coeff_copies = []
        for part in range(3):
            lax.fori_loop(3 * part, 3 * part + 3, project, 0)
            rows = pl.ds(24 * part, 24)
            coeff_copies.append(
                [
                    to_grid(
                        coeff.at[rows], near_coeff.at[i, rows], sc.at[i, part], rc.at[i, part], near[i]
                    )
                    for i in range(4)
                ]
            )
            for copy in coeff_copies[-1]:
                copy.start()

        if band_count > 1:

            @pl.when(early)
            def _():
                send_parts()

        for i, offset in ((1, 1), (2, -1), (0, 2)):
            settle(d_own.at[pl.ds(0, height)], rx.at[i])
            to_mate(column(-offset))
        for q in range(3):
            d_hi, d_lo = halves(d_own[:, q].reshape(half * ATOMS, N))
            slots = mm(d_hi, d_pick[0], TN) + mm(d_lo, d_pick[0], TN)
            for lanes in range(2):
                d_slot[lanes, q * N : (q + 1) * N, :] = slots[:, lanes * N : (lanes + 1) * N]
        settle(d_mate, rm)
        for q in range(3):
            d_hi, d_lo = halves(d_mate[:, q].reshape(half * ATOMS, N))
            slots = mm(d_hi, d_pick[1], TN) + mm(d_lo, d_pick[1], TN)
            for lanes in range(2):
                d_slot[lanes, q * N : (q + 1) * N, :] += slots[:, lanes * N : (lanes + 1) * N]

        if band_count > 1:

            @pl.when(late)
            def _():
                add_parts()

        c_hi, c_lo = halves(coeff[...])
        total = mm(c_hi, same[0], NT) + mm(c_lo, same[0], NT)
        for i in range(4):
            with jax.named_scope("s_coefwait"):
                for part in range(3):
                    coeff_copies[part][i].wait_recv()
            c_hi, c_lo = halves(near_coeff[i])
            total += mm(c_hi, same[1 + i], NT) + mm(c_lo, same[1 + i], NT)
        summed[...] = total

        d_slot[:, 3 * N :, :] = jnp.zeros((2, 24, N), F32)
        values = [jnp.zeros((24, PAIRS), F32) for _ in range(COMBOS)]
        for j in range(PROJ):
            part = jnp.concatenate(
                [
                    jnp.concatenate(
                        [d_slot[lanes, pl.ds(q * N + j, 8, stride=PROJ), :] for lanes in range(2)],
                        axis=1,
                    )
                    for q in range(3)
                ],
                axis=0,
            )
            for combo in range(COMBOS):
                row = j * COMBOS + combo
                values[combo] += part * summed[row : row + 1, :]
        for combo in range(COMBOS):
            applied[combo] = values[combo]

        depth = 32

        def spread_back(step, carry):
            first = pl.multiple_of(step * depth, depth)
            totals = [jnp.zeros((depth, PAIRS), F32) for _ in range(COMBOS)]
            for i in range(PROJ):
                values = proj_t[i, pl.ds(first, depth), :]
                for combo in range(COMBOS):
                    totals[combo] += values * applied[combo, 8 * (i // 7) + i % 7 : 8 * (i // 7) + i % 7 + 1, :]
            for combo in range(COMBOS):
                added[pl.ds(pl.multiple_of(combo * N + first, depth), depth), :] = totals[combo]
            return carry

        lax.fori_loop(0, N // depth, spread_back, 0)
        a_hi, a_lo = halves(added[...])
        projected = mm(a_hi, row_pick[...], NT) + mm(a_lo, row_pick[...], NT)
        for combo in range(COMBOS):
            here = slice(combo * N, (combo + 1) * N)
            h_ref[here, :] = vloc_t[...] * field[here, :] + projected[here]

        spectra = []
        for plane in range(PLANES):
            lanes = slice(plane * N, (plane + 1) * N)
            value = jnp.concatenate(
                [
                    jnp.concatenate(
                        [
                            h_ref[(part * BANDS + member) * N : (part * BANDS + member + 1) * N, lanes]
                            for member in range(BANDS)
                        ],
                        axis=1,
                    )
                    for part in range(2)
                ],
                axis=0,
            )
            v_hi, v_lo = halves(value)
            spectra.append(mm(zb_ref[0], v_hi) + mm(zb_ref[1], v_hi) + mm(zb_ref[0], v_lo))
        turned = jnp.concatenate(
            [spectra[plane][part * BOX : (part + 1) * BOX] for part in range(2) for plane in range(PLANES)],
            axis=0,
        )
        t_hi, t_lo = halves(turned)
        turned = mm(t_hi, yb_ref[0]) + mm(t_lo, yb_ref[0]) + mm(t_hi, yb_ref[1])
        end = BANDS * BOX
        final = jnp.concatenate(
            [turned[:mid, :end] + turned[mid:, end:], turned[mid:, :end] - turned[:mid, end:]], axis=0
        )
        q_hi, q_lo = halves(final)
        both = jnp.concatenate([q_hi, q_lo], axis=1)

        if band_count > 1:

            @pl.when(middle)
            def _():
                add_parts()

        batch = 16

        def take(targets):
            for first in range(0, batch, 2):
                two = targets[first : first + 2]
                pick = jnp.concatenate([oh_y[target] for target in two], axis=1)
                found = mm(both, jnp.concatenate([pick, pick], axis=0))
                for k, target in enumerate(two):
                    at = z_id == code_z[target]
                    msg2[target] = jnp.concatenate(
                        [
                            jnp.sum(
                                jnp.where(
                                    at, found[r * BOX : (r + 1) * BOX, k * N : (k + 1) * N], 0.0
                                ),
                                axis=0,
                                keepdims=True,
                            )
                            for r in range(4)
                        ],
                        axis=0,
                    )

        def partners(step):
            return [lax.rem(me + far(batch * step + k), grid_count) for k in range(batch)]

        def send2(target):
            to_grid(msg2.at[target], got2.at[me], s2, r2, target).start()

        def take_and_send(step, carry):
            targets = partners(step)
            take(targets)
            for target in targets:
                send2(target)
            return carry

        lax.fori_loop(0, grid_count // batch - 1, take_and_send, 0)
        targets = partners(grid_count // batch - 1)
        take(targets)
        for target in targets[:-1]:
            send2(target)
        own_back = pltpu.make_async_copy(msg2.at[me], got2.at[me], out_sem)
        own_back.start()

        if band_count > 1:

            @pl.when(foremost)
            def _():
                add_parts()

            settle(dens_full.at[pl.ds(0, ROWS - share)], rf)
        dens_out = pltpu.make_async_copy(dens_full, dens_hbm, in_sem.at[0])
        dens_out.start()
        settle(got2.at[pl.ds(0, peers)], r2)
        own_back.wait()

        dens_out.wait()
        settle(msg1.at[pl.ds(0, peers)], s1)
        settle(msg2.at[pl.ds(0, peers)], s2)
        settle(d_own.at[pl.ds(0, height - 1)], sd)
        for i in range(3):
            settle(d_own.at[pl.ds(0, height)], sx.at[i])
        settle(d_mate, sm)
        for copies in [atom_copies] + coeff_copies:
            for copy in copies:
                copy.wait_send()
        if band_count > 1:
            settle(dens_part.at[pl.ds(0, band_count - 1)], sp)
            settle(dens_full.at[pl.ds(0, ROWS - share)], sf)
    return kernel


def finish(psi_ref, col_ref, table_ref, got_ref, dens_in, out_ref, dens_ref, work):
    back = got_ref[...].reshape(got_ref.shape[0] * 4, N).T
    b_hi, b_lo = halves(back)
    result = mm(b_hi, table_ref[0]) + mm(b_lo, table_ref[0]) + mm(b_hi, table_ref[1])
    dens_ref[...] = dens_in[...]
    work[...] = jnp.zeros_like(work)
    work[0:1, 0:COLS] = col_ref[...].astype(F32)
    codes = jnp.broadcast_to(work[0:1, :], (N, N)).T.astype(jnp.int32)[0:COLS]

    def signed(index):
        return jnp.where(index >= N // 2, index - N, index)

    fy, fz, fx = signed(codes // N), signed(codes % N), signed(iota((COLS, N), 1))
    kinetic = KINETIC * (fx * fx + fy * fy + fz * fz).astype(F32)
    for part in range(2):
        for member in range(BANDS):
            out_ref[part, member] = (
                result[member * SLOT : member * SLOT + COLS, part * N : (part + 1) * N]
                + kinetic * psi_ref[part, member]
            )


def solution(mesh):
    grid_count = mesh.shape["grid"]
    band_count = mesh.shape["band"]
    half = grid_count // 2
    constants = tables(grid_count)

    def step(psi_g, col_index, v_local, proj_values, pair_atom, pair_row, d_matrices, occupations):
        x_table, y_table, y_back, z_table, z_back = [jnp.asarray(t) for t in constants]
        hbm = pl.BlockSpec(memory_space=pl.ANY)
        dma = pltpu.SemaphoreType.DMA
        col_row = col_index.reshape(1, COLS)
        got, dens = pl.pallas_call(
            make_kernel(grid_count, band_count),
            out_shape=(
                jax.ShapeDtypeStruct((grid_count, 4, N), F32),
                jax.ShapeDtypeStruct((ROWS, N), F32),
            ),
            in_specs=[hbm] * 12 + [pl.BlockSpec(memory_space=pltpu.SMEM)],
            out_specs=(hbm, hbm),
            scratch_shapes=[
                pltpu.VMEM((2, BANDS, COLS, N), F32),
                pltpu.VMEM((1, COLS), jnp.int32),
                pltpu.VMEM((2, 2 * N, 2 * N), BF16),
                pltpu.VMEM((PROJ, ATOMS, PROJ), F32),
                pltpu.VMEM((1, PAIRS), jnp.int32),
                pltpu.VMEM((PLANES, N, N), F32),
                pltpu.VMEM((PROJ, PAIRS, N), F32),
                pltpu.VMEM((1, PAIRS), jnp.int32),
                pltpu.VMEM((2, BANDS * BOX, 2 * BANDS * N), BF16),
                pltpu.VMEM((2, 2 * N, 2 * BOX), BF16),
                pltpu.VMEM((2, 2 * BOX, 2 * N), BF16),
                pltpu.VMEM((2, BANDS * N, 2 * BANDS * BOX), BF16),
                pltpu.VMEM((PROJ, N, PAIRS), F32),
                pltpu.VMEM((BANDS * SLOT, 2 * N), F32),
                pltpu.VMEM((grid_count, 4, N), F32),
                pltpu.VMEM((grid_count, 4, N), F32),
                pltpu.VMEM((grid_count, 4, N), F32),
                pltpu.VMEM((grid_count, 1, N), jnp.int32),
                pltpu.VMEM((grid_count, BANDS * BOX, N), BF16),
                pltpu.VMEM((BANDS * BOX, 2 * PLANES * BOX), F32),
                pltpu.VMEM((COMBOS * N, ROWS), F32),
                pltpu.VMEM((COMBOS * N, PAIRS), F32),
                pltpu.VMEM((PROJ * COMBOS, PAIRS), F32),
                pltpu.VMEM((4, PROJ * COMBOS, PAIRS), F32),
                pltpu.VMEM((4, 1, PAIRS), jnp.int32),
                pltpu.VMEM((PAIRS, N), F32),
                pltpu.VMEM((N, ROWS), F32),
                pltpu.VMEM((half, 3, ATOMS, N), F32),
                pltpu.VMEM((half, 3, ATOMS, N), F32),
                pltpu.VMEM((2, 3 * N + 24, N), F32),
                pltpu.VMEM((3, ATOMS, N), F32),
                pltpu.VMEM((PROJ * COMBOS, PAIRS), F32),
                pltpu.VMEM((COMBOS, 24, PAIRS), F32),
                pltpu.VMEM((COMBOS * N, PAIRS), F32),
                pltpu.VMEM((COMBOS * N, ROWS), F32),
                pltpu.VMEM((ROWS, N), F32),
                pltpu.VMEM((band_count, ROWS // band_count, N), F32),
                pltpu.VMEM((ROWS, N), F32),
                pltpu.VMEM((8, N), F32),
                pltpu.VMEM((ROWS, PAIRS), BF16),
                pltpu.VMEM((2, half * ATOMS, PAIRS), BF16),
                pltpu.VMEM((5, PAIRS, PAIRS), BF16),
                pltpu.SemaphoreType.REGULAR((grid_count // 16,)), pltpu.SemaphoreType.REGULAR,
                dma((12,)), dma, dma, dma((grid_count // 16,)), dma, dma, dma, dma, dma((3,)), dma((3,)), dma, dma,
                dma((4,)), dma((4,)), dma((4, 3)), dma((4, 3)), dma, dma, dma, dma,
            ],
            compiler_params=pltpu.CompilerParams(
                collective_id=0, has_side_effects=True, vmem_limit_bytes=60 << 20
            ),
        )(
            psi_g,
            col_row,
            x_table,
            d_matrices.transpose(1, 0, 2),
            pair_atom.reshape(1, PAIRS),
            v_local,
            proj_values.transpose(1, 0, 2),
            pair_row.reshape(1, PAIRS),
            y_table,
            z_table,
            z_back,
            y_back,
            occupations.reshape(1, BANDS),
        )
        out, dens = pl.pallas_call(
            finish,
            out_shape=(
                jax.ShapeDtypeStruct(psi_g.shape, F32),
                jax.ShapeDtypeStruct((ROWS, N), F32),
            ),
            in_specs=[pl.BlockSpec(memory_space=pltpu.VMEM)] * 5,
            out_specs=(pl.BlockSpec(memory_space=pltpu.VMEM),) * 2,
            scratch_shapes=[pltpu.VMEM((8, N), F32)],
            compiler_params=pltpu.CompilerParams(vmem_limit_bytes=60 << 20),
        )(psi_g, col_row, x_table, got, dens)
        return out, dens.reshape(PLANES, N, N)

    return jax.shard_map(
        step,
        mesh=mesh,
        in_specs=(
            P(None, "band", "grid", None),
            P("grid"),
            P("grid", None, None),
            P("grid", None, None),
            P("grid"),
            P("grid"),
            P("grid", None, None),
            P("band"),
        ),
        out_specs=(P(None, "band", "grid", None), P("grid", None, None)),
        check_vma=False,
    )
```

```python
import functools

import jax
import jax.numpy as jnp
import numpy as np
from jax import lax
from jax.experimental import pallas as pl
from jax.experimental.pallas import tpu as pltpu
from jax.sharding import PartitionSpec as P

MESH = pl.DeviceIdType.MESH
F32 = jnp.float32
BF16 = jnp.bfloat16
KINETIC = 0.0005

N = 128
BOX = 64
PLANES = 2
BANDS = 2
COLS = 48
SLOT = 64
PROJ = 18
PAIRS = 256
ATOMS = 8
COMBOS = 4
ROWS = PLANES * N


def split(table):
    high = table.astype(jnp.bfloat16)
    low = (table - high.astype(np.float64)).astype(jnp.bfloat16)
    return np.stack([high, low])


def tables(grid_count):
    scale = 1.0 / np.sqrt(N)
    pos = np.arange(N)
    box = np.arange(BOX)
    freq = np.where(box >= BOX // 2, box - BOX, box)

    def cos_sin(left, right):
        angle = 2.0 * np.pi / N * (np.outer(left, right) % N)
        return np.cos(angle) * scale, np.sin(angle) * scale

    cos_x, sin_x = cos_sin(pos, pos)
    x_table = np.zeros((grid_count, 2, PLANES, 2, N))
    cos_r = cos_x.reshape(grid_count, PLANES, N)
    sin_r = sin_x.reshape(grid_count, PLANES, N)
    x_table[:, 0, :, 0] = cos_r
    x_table[:, 0, :, 1] = -sin_r
    x_table[:, 1, :, 0] = sin_r
    x_table[:, 1, :, 1] = cos_r
    x_table = x_table.reshape(2 * N, 2 * N)
    cos_y, sin_y = cos_sin(freq, pos)
    y_table = np.zeros((BANDS, BOX, 2, BANDS, N))
    for band in range(BANDS):
        y_table[band, :, 0, band] = cos_y
        y_table[band, :, 1, band] = sin_y
    y_back = y_table.transpose(3, 4, 2, 0, 1).reshape(BANDS * N, 2 * BANDS * BOX)
    y_table = y_table.reshape(BANDS * BOX, 2 * BANDS * N)
    cos_z, sin_z = cos_sin(pos, freq)
    z_table = np.block([[cos_z, -sin_z], [sin_z, cos_z]])
    return [split(t) for t in (x_table, y_table, y_back, z_table, z_table.T)]


def halves(value):
    high = value.astype(BF16)
    low = (value - high.astype(F32)).astype(BF16)
    return high, low


def mm(left, right, dims=((1,), (0,))):
    return lax.dot_general(left, right, (dims, ((), ())), preferred_element_type=F32)


NT = ((1,), (1,))
TN = ((0,), (0,))


def iota(shape, dim):
    return lax.broadcasted_iota(jnp.int32, shape, dim)


def make_kernel(grid_count, band_count):
    peers = grid_count - 1
    half = grid_count // 2
    width = 4
    height = half // width

    def kernel(
        psi_in, col_in, xt_in, dmat_in, atom_in, vloc_in, proj_in, row_in, yt_in, zt_in, zb_in,
        yb_in, occ_ref,
        got2, dens_hbm,
        psi_ref, col_ref, xt_ref, dmat_ref, atom_ref, vloc_ref, proj_buf, row_ref, yt_ref, zt_ref,
        zb_ref, yb_ref, proj_t, psi_pad, msg1, got1, msg2, code_z, oh_y, box_ref,
        field, tiles, coeff, near_coeff, near_atom, atom_col, vloc_t,
        d_own, d_mate, d_rest, rest_mate, d_slot, d_send, summed, applied, added, h_ref,
        dens_loc, dens_part, dens_full, work, row_pick, d_pick, same,
        here, all_here, in_sem, out_sem, s1, r1, s2, r2, sd, rd, sx, rx, se, re, sg, rg, sh, rh, sm, rm, sa, ra, sc, rc, sp, rp, sf, rf,
    ):
        me = lax.axis_index("grid")
        band = lax.axis_index("band")
        core = lax.rem(me, 2)
        chip = me // 2
        at_x = lax.rem(chip, width)
        at_y = chip // width

        def to_grid(src, dst, send, recv, target):
            return pltpu.make_async_remote_copy(
                src_ref=src, dst_ref=dst, send_sem=send, recv_sem=recv,
                device_id={"grid": target}, device_id_type=MESH,
            )

        def to_band(src, dst, send, recv, target):
            return pltpu.make_async_remote_copy(
                src_ref=src, dst_ref=dst, send_sem=send, recv_sem=recv,
                device_id={"band": target}, device_id_type=MESH,
            )

        def settle(ref, sem):
            pltpu.make_async_copy(ref, ref, sem).wait()

        def wrap(index):
            return jnp.where(index >= grid_count, index - grid_count, index)

        def far(pair):
            return half + pair, half - 1 - pair

        barrier = pltpu.get_barrier_semaphore()
        envoy = 0
        is_envoy = me == envoy

        apart = wrap(me - envoy + grid_count)
        envoy_step = jnp.where(apart > half, 2 * (apart - half), 2 * (half - apart) - 1)
        last_group = jnp.where(apart == half, 0, envoy_step // 16)
        groups = grid_count // 16

        def greet(offset):
            target = wrap(me + offset)

            @pl.when(target != envoy)
            def _():
                pl.semaphore_signal(
                    barrier, inc=1, device_id={"grid": target}, device_id_type=MESH
                )

        inputs = [
            pltpu.make_async_copy(src, dst, in_sem.at[i])
            for i, (src, dst) in enumerate(
                [
                    (psi_in, psi_ref), (col_in, col_ref), (xt_in, xt_ref), (dmat_in, dmat_ref),
                    (atom_in, atom_ref), (vloc_in, vloc_ref), (proj_in, proj_buf),
                    (row_in, row_ref), (yt_in, yt_ref), (zt_in, zt_ref), (zb_in, zb_ref),
                    (yb_in, yb_ref),
                ]
            )
        ]
        for copy in inputs[:4]:
            copy.start()
        for pair in range(half):
            for offset in far(pair):
                if offset > 0:
                    greet(offset)
        for copy in inputs[4:]:
            copy.start()

        early = band < 3
        foremost = band < 3
        middle = band == 3
        late = band >= 4
        share = ROWS // band_count
        mine = pl.ds(pl.multiple_of(band * share, share), share)

        def tell_group():
            @pl.when(is_envoy)
            def _():
                pl.semaphore_wait(barrier, band_count - 1)

                def pass_on(offset, carry):
                    pl.semaphore_signal(
                        all_here, inc=1, device_id={"grid": wrap(me + offset)}, device_id_type=MESH
                    )
                    return carry

                lax.fori_loop(1, grid_count, pass_on, 0)

        def send_parts():
            @pl.when(jnp.logical_not(is_envoy))
            def _():
                pl.semaphore_wait(all_here, 1)

            def send_part(step, carry):
                target = jnp.where(step >= band, step + 1, step)
                first = pl.multiple_of(target * share, share)
                to_band(
                    dens_loc.at[pl.ds(first, share)], dens_part.at[band], sp, rp, target
                ).start()
                return carry

            lax.fori_loop(0, band_count - 1, send_part, 0)

        def add_parts():
            settle(dens_part.at[pl.ds(0, band_count - 1)], rp)
            dens_part[band] = dens_loc[mine, :]
            whole = dens_part[0]
            for other in range(1, band_count):
                whole += dens_part[other]
            dens_full[mine, :] = whole

            def send_full(step, carry):
                target = jnp.where(step >= band, step + 1, step)
                to_band(dens_full.at[mine], dens_full.at[mine], sf, rf, target).start()
                return carry

            lax.fori_loop(0, band_count - 1, send_full, 0)

        psi_pad[...] = jnp.zeros_like(psi_pad)
        for copy in inputs[:3]:
            copy.wait()
        for member in range(BANDS):
            for part in range(2):
                psi_pad[member * SLOT : member * SLOT + COLS, part * N : (part + 1) * N] = psi_ref[
                    part, member
                ]
        psi_hi, psi_lo = halves(psi_pad[...])
        spread = mm(xt_ref[0], psi_hi, NT) + mm(xt_ref[1], psi_hi, NT) + mm(xt_ref[0], psi_lo, NT)
        work[...] = jnp.zeros_like(work)
        work[0:1, 0:COLS] = col_ref[...].astype(F32)
        codes = jnp.broadcast_to(work[0:1, :], (8, N))
        sub = iota((8, N), 0) % 4
        lane = iota((8, N), 1)
        pattern = jnp.where(
            sub == 0,
            pltpu.roll(codes, 48, 1),
            jnp.where(sub == 1, pltpu.roll(codes, 32, 1), pltpu.roll(codes, 16, 1)),
        )
        pattern = jnp.where((lane >= COLS) & (lane < SLOT) & (sub < 3), pattern, 0.0)
        for pair in range(grid_count // 2):
            both = spread[8 * pair : 8 * pair + 8] + pattern
            msg1[2 * pair] = both[0:4]
            msg1[2 * pair + 1] = both[4:8]
        own_copy = pltpu.make_async_copy(msg1.at[me], got1.at[me], r1.at[grid_count // 16 - 1])
        own_copy.start()

        @pl.when(jnp.logical_not(is_envoy))
        def _():
            pl.semaphore_wait(barrier, peers)
            pl.semaphore_signal(
                here.at[last_group], inc=1, device_id={"grid": envoy}, device_id_type=MESH
            )

        for group in reversed(range(groups)):

            @pl.when(is_envoy)
            def _(group=group):
                pl.semaphore_wait(here.at[group], 16 if group < groups - 1 else 15)

            for pair in reversed(range(8 * group, 8 * group + 8)):
                for offset in reversed(far(pair)):
                    if offset > 0:
                        target = wrap(me + offset)
                        to_grid(
                            msg1.at[target], got1.at[me], s1, r1.at[group], target
                        ).start()

        if band_count > 1:

            @pl.when(is_envoy)
            def _():
                for step in range(1, band_count):
                    pl.semaphore_signal(
                        barrier, inc=1, device_id={"band": lax.rem(band + step, band_count)},
                        device_id_type=MESH,
                    )

        near = [lax.rem(me + off + grid_count, grid_count) for off in (1, -1, 2, -2)]
        inputs[4].wait()
        atom_copies = [
            to_grid(atom_ref, near_atom.at[i], sa.at[i], ra.at[i], near[i]) for i in range(4)
        ]
        for copy in atom_copies:
            copy.start()

        inputs[3].wait()
        d_send[...] = jnp.zeros_like(d_send)
        for i in range(PROJ):
            first = (i % 7) * PROJ
            d_send[i // 7, :, first : first + PROJ] = dmat_ref[i]
        d_own[at_x * height + at_y] = d_send[0:2]
        d_rest[chip] = d_send[2]
        for step in range(1, height):
            other = lax.rem(at_y + step, height) * width + at_x
            to_grid(
                d_send.at[pl.ds(0, 2)], d_own.at[at_x * height + at_y], sd, rd, 2 * other + core
            ).start()
        for step in range(1, width):
            other = at_y * width + lax.rem(at_x + step, width)
            to_grid(d_send.at[2], d_rest.at[chip], se, re, 2 * other + core).start()

        inputs[5].wait()
        for plane in range(PLANES):
            vloc_t[:, plane * N : (plane + 1) * N] = vloc_ref[plane].T
        atom_row = atom_ref[...].astype(F32)
        for part in range(2):
            atom_col[part * N : (part + 1) * N, :] = jnp.broadcast_to(
                atom_row[:, part * N : (part + 1) * N], (N, N)
            ).T
        for copy in inputs[6:]:
            copy.wait()
        for i in range(PROJ):
            for part in range(2):
                proj_t[i, :, part * N : (part + 1) * N] = proj_buf[i, part * N : (part + 1) * N, :].T

        local_row = row_ref[...] - me * ROWS
        row_pick[...] = jnp.where(iota((ROWS, PAIRS), 0) == local_row, 1.0, 0.0).astype(BF16)
        atoms = atom_ref[...]
        place = iota((half * ATOMS, PAIRS), 0)
        slot = place // ATOMS
        for which in range(2):
            shift = (core if which == 0 else 1 - core) * ATOMS + place % ATOMS
            for order, holder in enumerate([(slot % height) * width + slot // height, slot]):
                d_pick[which, order] = jnp.where(
                    holder * (2 * ATOMS) + shift == atoms, 1.0, 0.0
                ).astype(BF16)
        wide = jnp.concatenate([atom_col[...], atom_col[...]], axis=1)
        same[0] = jnp.where(wide == atom_row, 1.0, 0.0).astype(BF16)
        for i in range(4):
            atom_copies[i].wait_recv()
            same[1 + i] = jnp.where(wide == near_atom[i].astype(F32), 1.0, 0.0).astype(BF16)

        box_ref[...] = jnp.zeros_like(box_ref)
        row_id = iota((BANDS * BOX, N), 0).astype(F32).astype(BF16)
        z_id = iota((BOX, N), 0)
        z_id16 = z_id.astype(F32).astype(BF16)
        sub = iota((8, N), 0)
        lane = iota((8, N), 1)
        one, zero = jnp.ones((), BF16), jnp.zeros((), BF16)
        code_place = lane // 16 == (sub + 3) % 8
        lane = iota((1, N), 1)
        filled = lane % SLOT < COLS
        upper = lane >= SLOT

        def fill(step, carry):
            group = groups - 1 - step
            group = jnp.where(group > last_group, group, group - 1)
            group = jnp.where(step == groups - 1, last_group, group)
            with jax.named_scope("s_fillwait"):
                settle(got1.at[pl.ds(0, 16)], r1.at[group])
            total = jnp.zeros((BANDS * BOX, 2 * PLANES * BOX), F32)
            for pair in range(8):
                senders = [wrap(me + grid_count - offset) for offset in far(8 * group + pair)]
                data = [got1[sender] for sender in senders]
                codes = pltpu.roll(jnp.concatenate(data, axis=0), 0, 1, stride=16, stride_axis=0)
                codes = jnp.where(code_place, codes, 0.0)
                picks, highs, lows = [], [], []
                for k in range(2):
                    code = jnp.sum(codes[4 * k : 4 * k + 4], axis=0, keepdims=True)
                    code = jnp.broadcast_to(code, (8, N))
                    turned = [pltpu.roll(code, 80, 1), pltpu.roll(code, 16, 1)]
                    code = jnp.where(upper, turned[1 - k], turned[k])[0:1]
                    code = code.astype(jnp.int32)
                    at_y = jnp.where(filled, (code // N) % BOX + jnp.where(upper, BOX, 0), -1)
                    at_z = jnp.where(filled, code % BOX, -1)
                    code_z[senders[k]] = at_z
                    picker = jnp.where(row_id == at_y.astype(F32).astype(BF16), one, zero)
                    oh_y[senders[k]] = picker
                    picks.append(picker)
                    high, rest = halves(data[k])
                    at = z_id16 == at_z.astype(F32).astype(BF16)
                    for value, store in ((high, highs), (rest, lows)):
                        store.append(
                            jnp.concatenate(
                                [jnp.where(at, value[r : r + 1], zero) for r in range(4)], axis=0
                            )
                        )
                pick = jnp.concatenate(picks, axis=1)
                total += mm(pick, jnp.concatenate(highs, axis=1), NT)
                total += mm(pick, jnp.concatenate(lows, axis=1), NT)
            box_ref[...] += total
            return carry

        lax.fori_loop(0, groups // 2, fill, 0)
        if band_count > 1:

            @pl.when(jnp.logical_not(early))
            def _():
                tell_group()

        settle(d_own.at[pl.ds(0, height - 1)], rd)

        def column(offset):
            return pl.ds(lax.rem(at_x + offset + width, width) * height, height)

        for i, offset in enumerate((2, 1, -1)):
            block = d_own.at[column(0)]
            target = 2 * (at_y * width + lax.rem(at_x + offset + width, width)) + core
            to_grid(block, block, sx.at[i], rx.at[i], target).start()

        def to_mate(block):
            to_grid(d_own.at[block], d_mate.at[block], sm, rm, 2 * chip + 1 - core).start()

        settle(d_rest.at[pl.ds(0, width - 1)], re)
        line = d_rest.at[pl.ds(at_y * width, width)]
        for step in range(1, height):
            other = lax.rem(at_y + step, height) * width + at_x
            to_grid(line, line, sg, rg, 2 * other + core).start()
        to_mate(column(0))
        lax.fori_loop(groups // 2, groups, fill, 0)

        box_hi, box_lo = halves(box_ref[...].T)
        turned = mm(box_hi, yt_ref[0]) + mm(box_lo, yt_ref[0]) + mm(box_hi, yt_ref[1])
        mid, end = PLANES * BOX, BANDS * N
        part_re = turned[:mid, :end] - turned[mid:, end:]
        part_im = turned[:mid, end:] + turned[mid:, :end]
        for plane in range(PLANES):
            here = slice(plane * BOX, (plane + 1) * BOX)
            value = jnp.concatenate([part_re[here], part_im[here]], axis=0)
            v_hi, v_lo = halves(value)
            wave = mm(zt_ref[0], v_hi) + mm(zt_ref[1], v_hi) + mm(zt_ref[0], v_lo)
            for part in range(2):
                for member in range(BANDS):
                    first = (part * BANDS + member) * N
                    field[first : first + N, plane * N : (plane + 1) * N] = wave[
                        part * N : (part + 1) * N, member * N : (member + 1) * N
                    ]

        dens_t = jnp.zeros((N, ROWS), F32)
        for member in range(BANDS):
            real = field[member * N : (member + 1) * N, :]
            imag = field[(BANDS + member) * N : (BANDS + member + 1) * N, :]
            dens_t += occ_ref[0, member] * (real * real + imag * imag)
        for plane in range(PLANES):
            dens_loc[plane * N : (plane + 1) * N, :] = dens_t[:, plane * N : (plane + 1) * N].T

        if band_count > 1:

            @pl.when(early)
            def _():
                tell_group()

            @pl.when(jnp.logical_not(early))
            def _():
                send_parts()

        f_hi, f_lo = halves(field[...])
        tiles[...] = mm(f_hi, row_pick[...]) + mm(f_lo, row_pick[...])

        def project(step, carry):
            found = []
            for k in range(2):
                values = proj_t[2 * step + k]
                for combo in range(COMBOS):
                    found.append(
                        jnp.sum(values * tiles[combo * N : (combo + 1) * N, :], axis=0, keepdims=True)
                    )
            coeff[pl.ds(pl.multiple_of(step * 8, 8), 8), :] = jnp.concatenate(found, axis=0)
            return carry

        coeff_copies = []
        for part in range(3):
            lax.fori_loop(3 * part, 3 * part + 3, project, 0)
            rows = pl.ds(24 * part, 24)
            coeff_copies.append(
                [
                    to_grid(
                        coeff.at[rows], near_coeff.at[i, rows], sc.at[i, part], rc.at[i, part], near[i]
                    )
                    for i in range(4)
                ]
            )
            for copy in coeff_copies[-1]:
                copy.start()

        if band_count > 1:

            @pl.when(early)
            def _():
                send_parts()

        for i, offset in ((1, 1), (2, -1), (0, 2)):
            settle(d_own.at[pl.ds(0, height)], rx.at[i])
            to_mate(column(-offset))
        settle(d_rest.at[pl.ds(0, half - width)], rg)
        rest_copy = to_grid(d_rest, rest_mate, sh, rh, 2 * chip + 1 - core)
        rest_copy.start()
        def gather_couplings(which, main, rest):
            for q in range(3):
                values = main[:, q] if q < 2 else rest[...]
                d_hi, d_lo = halves(values.reshape(half * ATOMS, N))
                pick = d_pick[which, q // 2]
                slots = mm(d_hi, pick, TN) + mm(d_lo, pick, TN)
                for lanes in range(2):
                    part = slots[:, lanes * N : (lanes + 1) * N]
                    rows = slice(q * N, (q + 1) * N)
                    d_slot[lanes, rows, :] = part if which == 0 else d_slot[lanes, rows, :] + part

        gather_couplings(0, d_own, d_rest)
        settle(d_mate, rm)
        rest_copy.wait_recv()
        gather_couplings(1, d_mate, rest_mate)

        if band_count > 1:

            @pl.when(late)
            def _():
                add_parts()

        c_hi, c_lo = halves(coeff[...])
        total = mm(c_hi, same[0], NT) + mm(c_lo, same[0], NT)
        for i in range(4):
            with jax.named_scope("s_coefwait"):
                for part in range(3):
                    coeff_copies[part][i].wait_recv()
            c_hi, c_lo = halves(near_coeff[i])
            total += mm(c_hi, same[1 + i], NT) + mm(c_lo, same[1 + i], NT)
        summed[...] = total

        d_slot[:, 3 * N :, :] = jnp.zeros((2, 24, N), F32)
        values = [jnp.zeros((24, PAIRS), F32) for _ in range(COMBOS)]
        for j in range(PROJ):
            part = jnp.concatenate(
                [
                    jnp.concatenate(
                        [d_slot[lanes, pl.ds(q * N + j, 8, stride=PROJ), :] for lanes in range(2)],
                        axis=1,
                    )
                    for q in range(3)
                ],
                axis=0,
            )
            for combo in range(COMBOS):
                row = j * COMBOS + combo
                values[combo] += part * summed[row : row + 1, :]
        for combo in range(COMBOS):
            applied[combo] = values[combo]

        depth = 32

        def spread_back(step, carry):
            first = pl.multiple_of(step * depth, depth)
            totals = [jnp.zeros((depth, PAIRS), F32) for _ in range(COMBOS)]
            for i in range(PROJ):
                values = proj_t[i, pl.ds(first, depth), :]
                for combo in range(COMBOS):
                    totals[combo] += values * applied[combo, 8 * (i // 7) + i % 7 : 8 * (i // 7) + i % 7 + 1, :]
            for combo in range(COMBOS):
                added[pl.ds(pl.multiple_of(combo * N + first, depth), depth), :] = totals[combo]
            return carry

        lax.fori_loop(0, N // depth, spread_back, 0)
        a_hi, a_lo = halves(added[...])
        projected = mm(a_hi, row_pick[...], NT) + mm(a_lo, row_pick[...], NT)
        for combo in range(COMBOS):
            here = slice(combo * N, (combo + 1) * N)
            h_ref[here, :] = vloc_t[...] * field[here, :] + projected[here]

        spectra = []
        for plane in range(PLANES):
            lanes = slice(plane * N, (plane + 1) * N)
            value = jnp.concatenate(
                [
                    jnp.concatenate(
                        [
                            h_ref[(part * BANDS + member) * N : (part * BANDS + member + 1) * N, lanes]
                            for member in range(BANDS)
                        ],
                        axis=1,
                    )
                    for part in range(2)
                ],
                axis=0,
            )
            v_hi, v_lo = halves(value)
            spectra.append(mm(zb_ref[0], v_hi) + mm(zb_ref[1], v_hi) + mm(zb_ref[0], v_lo))
        turned = jnp.concatenate(
            [spectra[plane][part * BOX : (part + 1) * BOX] for part in range(2) for plane in range(PLANES)],
            axis=0,
        )
        t_hi, t_lo = halves(turned)
        turned = mm(t_hi, yb_ref[0]) + mm(t_lo, yb_ref[0]) + mm(t_hi, yb_ref[1])
        end = BANDS * BOX
        final = jnp.concatenate(
            [turned[:mid, :end] + turned[mid:, end:], turned[mid:, :end] - turned[:mid, end:]], axis=0
        )
        q_hi, q_lo = halves(final)
        both = jnp.concatenate([q_hi, q_lo], axis=1)

        if band_count > 1:

            @pl.when(middle)
            def _():
                add_parts()

        batch = 16

        def take(targets):
            for first in range(0, batch, 2):
                two = targets[first : first + 2]
                pick = jnp.concatenate([oh_y[target] for target in two], axis=1)
                found = mm(both, jnp.concatenate([pick, pick], axis=0))
                for k, target in enumerate(two):
                    at = z_id == code_z[target]
                    msg2[target] = jnp.concatenate(
                        [
                            jnp.sum(
                                jnp.where(
                                    at, found[r * BOX : (r + 1) * BOX, k * N : (k + 1) * N], 0.0
                                ),
                                axis=0,
                                keepdims=True,
                            )
                            for r in range(4)
                        ],
                        axis=0,
                    )

        def partners(step):
            return [
                wrap(me + offset)
                for pair in range(batch // 2)
                for offset in far(batch // 2 * step + pair)
            ]

        def send2(target):
            to_grid(msg2.at[target], got2.at[me], s2, r2, target).start()

        def take_and_send(step, carry):
            targets = partners(step)
            take(targets)
            for target in targets:
                send2(target)
            return carry

        lax.fori_loop(0, grid_count // batch - 1, take_and_send, 0)
        targets = partners(grid_count // batch - 1)
        take(targets)
        for target in targets[:-1]:
            send2(target)
        own_back = pltpu.make_async_copy(msg2.at[me], got2.at[me], out_sem)
        own_back.start()

        if band_count > 1:

            @pl.when(foremost)
            def _():
                add_parts()

            settle(dens_full.at[pl.ds(0, ROWS - share)], rf)
        dens_out = pltpu.make_async_copy(dens_full, dens_hbm, in_sem.at[0])
        dens_out.start()
        settle(got2.at[pl.ds(0, peers)], r2)
        own_back.wait()

        dens_out.wait()
        settle(msg1.at[pl.ds(0, peers)], s1)
        settle(msg2.at[pl.ds(0, peers)], s2)
        settle(d_own.at[pl.ds(0, height - 1)], sd)
        settle(d_rest.at[pl.ds(0, width - 1)], se)
        settle(d_rest.at[pl.ds(0, half - width)], sg)
        rest_copy.wait_send()
        for i in range(3):
            settle(d_own.at[pl.ds(0, height)], sx.at[i])
        settle(d_mate, sm)
        for copies in [atom_copies] + coeff_copies:
            for copy in copies:
                copy.wait_send()
        if band_count > 1:
            settle(dens_part.at[pl.ds(0, band_count - 1)], sp)
            settle(dens_full.at[pl.ds(0, ROWS - share)], sf)
    return kernel


def finish(psi_ref, col_ref, table_ref, got_ref, dens_in, out_ref, dens_ref, work):
    back = got_ref[...].reshape(got_ref.shape[0] * 4, N).T
    b_hi, b_lo = halves(back)
    result = mm(b_hi, table_ref[0]) + mm(b_lo, table_ref[0]) + mm(b_hi, table_ref[1])
    dens_ref[...] = dens_in[...]
    work[...] = jnp.zeros_like(work)
    work[0:1, 0:COLS] = col_ref[...].astype(F32)
    codes = jnp.broadcast_to(work[0:1, :], (N, N)).T.astype(jnp.int32)[0:COLS]

    def signed(index):
        return jnp.where(index >= N // 2, index - N, index)

    fy, fz, fx = signed(codes // N), signed(codes % N), signed(iota((COLS, N), 1))
    kinetic = KINETIC * (fx * fx + fy * fy + fz * fz).astype(F32)
    for part in range(2):
        for member in range(BANDS):
            out_ref[part, member] = (
                result[member * SLOT : member * SLOT + COLS, part * N : (part + 1) * N]
                + kinetic * psi_ref[part, member]
            )


def solution(mesh):
    grid_count = mesh.shape["grid"]
    band_count = mesh.shape["band"]
    half = grid_count // 2
    constants = tables(grid_count)

    def step(psi_g, col_index, v_local, proj_values, pair_atom, pair_row, d_matrices, occupations):
        x_table, y_table, y_back, z_table, z_back = [jnp.asarray(t) for t in constants]
        hbm = pl.BlockSpec(memory_space=pl.ANY)
        dma = pltpu.SemaphoreType.DMA
        col_row = col_index.reshape(1, COLS)
        got, dens = pl.pallas_call(
            make_kernel(grid_count, band_count),
            out_shape=(
                jax.ShapeDtypeStruct((grid_count, 4, N), F32),
                jax.ShapeDtypeStruct((ROWS, N), F32),
            ),
            in_specs=[hbm] * 12 + [pl.BlockSpec(memory_space=pltpu.SMEM)],
            out_specs=(hbm, hbm),
            scratch_shapes=[
                pltpu.VMEM((2, BANDS, COLS, N), F32),
                pltpu.VMEM((1, COLS), jnp.int32),
                pltpu.VMEM((2, 2 * N, 2 * N), BF16),
                pltpu.VMEM((PROJ, ATOMS, PROJ), F32),
                pltpu.VMEM((1, PAIRS), jnp.int32),
                pltpu.VMEM((PLANES, N, N), F32),
                pltpu.VMEM((PROJ, PAIRS, N), F32),
                pltpu.VMEM((1, PAIRS), jnp.int32),
                pltpu.VMEM((2, BANDS * BOX, 2 * BANDS * N), BF16),
                pltpu.VMEM((2, 2 * N, 2 * BOX), BF16),
                pltpu.VMEM((2, 2 * BOX, 2 * N), BF16),
                pltpu.VMEM((2, BANDS * N, 2 * BANDS * BOX), BF16),
                pltpu.VMEM((PROJ, N, PAIRS), F32),
                pltpu.VMEM((BANDS * SLOT, 2 * N), F32),
                pltpu.VMEM((grid_count, 4, N), F32),
                pltpu.VMEM((grid_count, 4, N), F32),
                pltpu.VMEM((grid_count, 4, N), F32),
                pltpu.VMEM((grid_count, 1, N), jnp.int32),
                pltpu.VMEM((grid_count, BANDS * BOX, N), BF16),
                pltpu.VMEM((BANDS * BOX, 2 * PLANES * BOX), F32),
                pltpu.VMEM((COMBOS * N, ROWS), F32),
                pltpu.VMEM((COMBOS * N, PAIRS), F32),
                pltpu.VMEM((PROJ * COMBOS, PAIRS), F32),
                pltpu.VMEM((4, PROJ * COMBOS, PAIRS), F32),
                pltpu.VMEM((4, 1, PAIRS), jnp.int32),
                pltpu.VMEM((PAIRS, N), F32),
                pltpu.VMEM((N, ROWS), F32),
                pltpu.VMEM((half, 2, ATOMS, N), F32),
                pltpu.VMEM((half, 2, ATOMS, N), F32),
                pltpu.VMEM((half, ATOMS, N), F32),
                pltpu.VMEM((half, ATOMS, N), F32),
                pltpu.VMEM((2, 3 * N + 24, N), F32),
                pltpu.VMEM((3, ATOMS, N), F32),
                pltpu.VMEM((PROJ * COMBOS, PAIRS), F32),
                pltpu.VMEM((COMBOS, 24, PAIRS), F32),
                pltpu.VMEM((COMBOS * N, PAIRS), F32),
                pltpu.VMEM((COMBOS * N, ROWS), F32),
                pltpu.VMEM((ROWS, N), F32),
                pltpu.VMEM((band_count, ROWS // band_count, N), F32),
                pltpu.VMEM((ROWS, N), F32),
                pltpu.VMEM((8, N), F32),
                pltpu.VMEM((ROWS, PAIRS), BF16),
                pltpu.VMEM((2, 2, half * ATOMS, PAIRS), BF16),
                pltpu.VMEM((5, PAIRS, PAIRS), BF16),
                pltpu.SemaphoreType.REGULAR((grid_count // 16,)), pltpu.SemaphoreType.REGULAR,
                dma((12,)), dma, dma, dma((grid_count // 16,)), dma, dma, dma, dma, dma((3,)), dma((3,)), dma, dma, dma, dma, dma, dma, dma, dma,
                dma((4,)), dma((4,)), dma((4, 3)), dma((4, 3)), dma, dma, dma, dma,
            ],
            compiler_params=pltpu.CompilerParams(
                collective_id=0, has_side_effects=True, vmem_limit_bytes=60 << 20
            ),
        )(
            psi_g,
            col_row,
            x_table,
            d_matrices.transpose(1, 0, 2),
            pair_atom.reshape(1, PAIRS),
            v_local,
            proj_values.transpose(1, 0, 2),
            pair_row.reshape(1, PAIRS),
            y_table,
            z_table,
            z_back,
            y_back,
            occupations.reshape(1, BANDS),
        )
        out, dens = pl.pallas_call(
            finish,
            out_shape=(
                jax.ShapeDtypeStruct(psi_g.shape, F32),
                jax.ShapeDtypeStruct((ROWS, N), F32),
            ),
            in_specs=[pl.BlockSpec(memory_space=pltpu.VMEM)] * 5,
            out_specs=(pl.BlockSpec(memory_space=pltpu.VMEM),) * 2,
            scratch_shapes=[pltpu.VMEM((8, N), F32)],
            compiler_params=pltpu.CompilerParams(vmem_limit_bytes=60 << 20),
        )(psi_g, col_row, x_table, got, dens)
        return out, dens.reshape(PLANES, N, N)

    return jax.shard_map(
        step,
        mesh=mesh,
        in_specs=(
            P(None, "band", "grid", None),
            P("grid"),
            P("grid", None, None),
            P("grid", None, None),
            P("grid"),
            P("grid"),
            P("grid", None, None),
            P("band"),
        ),
        out_specs=(P(None, "band", "grid", None), P("grid", None, None)),
        check_vma=False,
    )
```

```python
import functools

import jax
import jax.numpy as jnp
import numpy as np
from jax import lax
from jax.experimental import pallas as pl
from jax.experimental.pallas import tpu as pltpu
from jax.sharding import PartitionSpec as P

MESH = pl.DeviceIdType.MESH
F32 = jnp.float32
BF16 = jnp.bfloat16
KINETIC = 0.0005

N = 128
BOX = 64
PLANES = 2
BANDS = 2
COLS = 48
SLOT = 64
PROJ = 18
PAIRS = 256
ATOMS = 8
COMBOS = 4
ROWS = PLANES * N


def split(table):
    high = table.astype(jnp.bfloat16)
    low = (table - high.astype(np.float64)).astype(jnp.bfloat16)
    return np.stack([high, low])


def tables(grid_count):
    scale = 1.0 / np.sqrt(N)
    pos = np.arange(N)
    box = np.arange(BOX)
    freq = np.where(box >= BOX // 2, box - BOX, box)

    def cos_sin(left, right):
        angle = 2.0 * np.pi / N * (np.outer(left, right) % N)
        return np.cos(angle) * scale, np.sin(angle) * scale

    cos_x, sin_x = cos_sin(pos, pos)
    x_table = np.zeros((grid_count, 2, PLANES, 2, N))
    cos_r = cos_x.reshape(grid_count, PLANES, N)
    sin_r = sin_x.reshape(grid_count, PLANES, N)
    x_table[:, 0, :, 0] = cos_r
    x_table[:, 0, :, 1] = -sin_r
    x_table[:, 1, :, 0] = sin_r
    x_table[:, 1, :, 1] = cos_r
    x_table = x_table.reshape(2 * N, 2 * N)
    cos_y, sin_y = cos_sin(freq, pos)
    y_table = np.zeros((BANDS, BOX, 2, BANDS, N))
    for band in range(BANDS):
        y_table[band, :, 0, band] = cos_y
        y_table[band, :, 1, band] = sin_y
    y_back = y_table.transpose(3, 4, 2, 0, 1).reshape(BANDS * N, 2 * BANDS * BOX)
    y_table = y_table.reshape(BANDS * BOX, 2 * BANDS * N)
    cos_z, sin_z = cos_sin(pos, freq)
    z_table = np.block([[cos_z, -sin_z], [sin_z, cos_z]])
    return [split(t) for t in (x_table, y_table, y_back, z_table, z_table.T)]


def halves(value):
    high = value.astype(BF16)
    low = (value - high.astype(F32)).astype(BF16)
    return high, low


def mm(left, right, dims=((1,), (0,))):
    return lax.dot_general(left, right, (dims, ((), ())), preferred_element_type=F32)


NT = ((1,), (1,))
TN = ((0,), (0,))


def iota(shape, dim):
    return lax.broadcasted_iota(jnp.int32, shape, dim)


def make_kernel(grid_count, band_count):
    peers = grid_count - 1
    half = grid_count // 2
    width = 4
    height = half // width

    def kernel(
        psi_in, col_in, xt_in, dmat_in, atom_in, vloc_in, proj_in, row_in, yt_in, zt_in, zb_in,
        yb_in, occ_ref,
        got2, dens_hbm,
        psi_ref, col_ref, xt_ref, dmat_ref, atom_ref, vloc_ref, proj_buf, row_ref, yt_ref, zt_ref,
        zb_ref, yb_ref, proj_t, psi_pad, msg1, got1, msg2, code_z, oh_y, box_ref,
        field, tiles, coeff, near_coeff, near_atom, atom_col, vloc_t,
        d_own, d_mate, d_rest, rest_mate, d_slot, d_send, summed, applied, added, h_ref,
        dens_loc, dens_part, dens_full, work, row_pick, d_pick, same,
        here, all_here, in_sem, out_sem, s1, r1, s2, r2, sd, rd, sx, rx, se, re, sg, rg, sh, rh, sm, rm, sa, ra, sc, rc, sp, rp, sf, rf,
    ):
        me = lax.axis_index("grid")
        band = lax.axis_index("band")
        core = lax.rem(me, 2)
        chip = me // 2
        at_x = lax.rem(chip, width)
        at_y = chip // width

        def to_grid(src, dst, send, recv, target):
            return pltpu.make_async_remote_copy(
                src_ref=src, dst_ref=dst, send_sem=send, recv_sem=recv,
                device_id={"grid": target}, device_id_type=MESH,
            )

        def to_band(src, dst, send, recv, target):
            return pltpu.make_async_remote_copy(
                src_ref=src, dst_ref=dst, send_sem=send, recv_sem=recv,
                device_id={"band": target}, device_id_type=MESH,
            )

        def settle(ref, sem):
            pltpu.make_async_copy(ref, ref, sem).wait()

        def wrap(index):
            return jnp.where(index >= grid_count, index - grid_count, index)

        def far(pair):
            return half + pair, half - 1 - pair

        barrier = pltpu.get_barrier_semaphore()
        envoy = 2
        is_envoy = me == envoy

        apart = wrap(me - envoy + grid_count)
        envoy_step = jnp.where(apart > half, 2 * (apart - half), 2 * (half - apart) - 1)
        last_group = jnp.where(apart == half, 0, envoy_step // 16)
        groups = grid_count // 16

        def greet(offset):
            target = wrap(me + offset)

            @pl.when(target != envoy)
            def _():
                pl.semaphore_signal(
                    barrier, inc=1, device_id={"grid": target}, device_id_type=MESH
                )

        inputs = [
            pltpu.make_async_copy(src, dst, in_sem.at[i])
            for i, (src, dst) in enumerate(
                [
                    (psi_in, psi_ref), (col_in, col_ref), (xt_in, xt_ref), (dmat_in, dmat_ref),
                    (atom_in, atom_ref), (vloc_in, vloc_ref), (proj_in, proj_buf),
                    (row_in, row_ref), (yt_in, yt_ref), (zt_in, zt_ref), (zb_in, zb_ref),
                    (yb_in, yb_ref),
                ]
            )
        ]
        for copy in inputs[:4]:
            copy.start()
        for pair in range(half):
            for offset in far(pair):
                if offset > 0:
                    greet(offset)
        for copy in inputs[4:]:
            copy.start()

        early = band < 3
        foremost = band < 3
        middle = band == 3
        late = band >= 4
        share = ROWS // band_count
        mine = pl.ds(pl.multiple_of(band * share, share), share)

        def tell_group():
            @pl.when(is_envoy)
            def _():
                pl.semaphore_wait(barrier, band_count - 1)

                def pass_on(offset, carry):
                    pl.semaphore_signal(
                        all_here, inc=1, device_id={"grid": wrap(me + offset)}, device_id_type=MESH
                    )
                    return carry

                lax.fori_loop(1, grid_count, pass_on, 0, unroll=9)

        def send_parts():
            @pl.when(jnp.logical_not(is_envoy))
            def _():
                pl.semaphore_wait(all_here, 1)

            def send_part(step, carry):
                target = jnp.where(step >= band, step + 1, step)
                first = pl.multiple_of(target * share, share)
                to_band(
                    dens_loc.at[pl.ds(first, share)], dens_part.at[band], sp, rp, target
                ).start()
                return carry

            lax.fori_loop(0, band_count - 1, send_part, 0)

        def add_parts():
            settle(dens_part.at[pl.ds(0, band_count - 1)], rp)
            dens_part[band] = dens_loc[mine, :]
            whole = dens_part[0]
            for other in range(1, band_count):
                whole += dens_part[other]
            dens_full[mine, :] = whole

            def send_full(step, carry):
                target = jnp.where(step >= band, step + 1, step)
                to_band(dens_full.at[mine], dens_full.at[mine], sf, rf, target).start()
                return carry

            lax.fori_loop(0, band_count - 1, send_full, 0)

        psi_pad[...] = jnp.zeros_like(psi_pad)
        for copy in inputs[:3]:
            copy.wait()
        for member in range(BANDS):
            for part in range(2):
                psi_pad[member * SLOT : member * SLOT + COLS, part * N : (part + 1) * N] = psi_ref[
                    part, member
                ]
        psi_hi, psi_lo = halves(psi_pad[...])
        spread = mm(xt_ref[0], psi_hi, NT) + mm(xt_ref[1], psi_hi, NT) + mm(xt_ref[0], psi_lo, NT)
        work[...] = jnp.zeros_like(work)
        work[0:1, 0:COLS] = col_ref[...].astype(F32)
        codes = jnp.broadcast_to(work[0:1, :], (8, N))
        sub = iota((8, N), 0) % 4
        lane = iota((8, N), 1)
        pattern = jnp.where(
            sub == 0,
            pltpu.roll(codes, 48, 1),
            jnp.where(sub == 1, pltpu.roll(codes, 32, 1), pltpu.roll(codes, 16, 1)),
        )
        pattern = jnp.where((lane >= COLS) & (lane < SLOT) & (sub < 3), pattern, 0.0)
        for pair in range(grid_count // 2):
            both = spread[8 * pair : 8 * pair + 8] + pattern
            msg1[2 * pair] = both[0:4]
            msg1[2 * pair + 1] = both[4:8]
        own_copy = pltpu.make_async_copy(msg1.at[me], got1.at[me], r1.at[grid_count // 16 - 1])
        own_copy.start()

        @pl.when(jnp.logical_not(is_envoy))
        def _():
            pl.semaphore_wait(barrier, peers)
            pl.semaphore_signal(
                here.at[last_group], inc=1, device_id={"grid": envoy}, device_id_type=MESH
            )

        def prepare():
            inputs[5].wait()
            for plane in range(PLANES):
                vloc_t[:, plane * N : (plane + 1) * N] = vloc_ref[plane].T
            atom_row = atom_ref[...].astype(F32)
            for part in range(2):
                atom_col[part * N : (part + 1) * N, :] = jnp.broadcast_to(
                    atom_row[:, part * N : (part + 1) * N], (N, N)
                ).T
            for copy in inputs[6:]:
                copy.wait()
            for i in range(PROJ):
                for part in range(2):
                    proj_t[i, :, part * N : (part + 1) * N] = proj_buf[i, part * N : (part + 1) * N, :].T

        inputs[4].wait()
        @pl.when(is_envoy)
        def _():
            prepare()

        for group in reversed(range(groups)):

            @pl.when(is_envoy)
            def _(group=group):
                pl.semaphore_wait(here.at[group], 16 if group < groups - 1 else 15)

            for pair in reversed(range(8 * group, 8 * group + 8)):
                for offset in reversed(far(pair)):
                    if offset > 0:
                        target = wrap(me + offset)
                        to_grid(
                            msg1.at[target], got1.at[me], s1, r1.at[group], target
                        ).start()

        if band_count > 1:

            @pl.when(is_envoy)
            def _():
                for step in range(1, band_count):
                    pl.semaphore_signal(
                        barrier, inc=1, device_id={"band": lax.rem(band + step, band_count)},
                        device_id_type=MESH,
                    )

        near = [lax.rem(me + off + grid_count, grid_count) for off in (1, -1, 2, -2)]
        atom_copies = [
            to_grid(atom_ref, near_atom.at[i], sa.at[i], ra.at[i], near[i]) for i in range(4)
        ]
        for copy in atom_copies:
            copy.start()

        inputs[3].wait()
        d_send[...] = jnp.zeros_like(d_send)
        for i in range(PROJ):
            first = (i % 7) * PROJ
            d_send[i // 7, :, first : first + PROJ] = dmat_ref[i]
        d_own[at_x * height + at_y] = d_send[0:2]
        d_rest[chip] = d_send[2]
        for step in range(1, height):
            other = lax.rem(at_y + step, height) * width + at_x
            to_grid(
                d_send.at[pl.ds(0, 2)], d_own.at[at_x * height + at_y], sd, rd, 2 * other + core
            ).start()
        for step in range(1, width):
            other = at_y * width + lax.rem(at_x + step, width)
            to_grid(d_send.at[2], d_rest.at[chip], se, re, 2 * other + core).start()

        @pl.when(jnp.logical_not(is_envoy))
        def _():
            prepare()

        atom_row = atom_ref[...].astype(F32)
        local_row = row_ref[...] - me * ROWS
        row_pick[...] = jnp.where(iota((ROWS, PAIRS), 0) == local_row, 1.0, 0.0).astype(BF16)
        atoms = atom_ref[...]
        place = iota((half * ATOMS, PAIRS), 0)
        slot = place // ATOMS
        for which in range(2):
            shift = (core if which == 0 else 1 - core) * ATOMS + place % ATOMS
            for order, holder in enumerate([(slot % height) * width + slot // height, slot]):
                d_pick[which, order] = jnp.where(
                    holder * (2 * ATOMS) + shift == atoms, 1.0, 0.0
                ).astype(BF16)
        wide = jnp.concatenate([atom_col[...], atom_col[...]], axis=1)
        same[0] = jnp.where(wide == atom_row, 1.0, 0.0).astype(BF16)

        box_ref[...] = jnp.zeros_like(box_ref)
        row_id = iota((BANDS * BOX, N), 0).astype(F32).astype(BF16)
        z_id = iota((BOX, N), 0)
        z_id16 = z_id.astype(F32).astype(BF16)
        sub = iota((8, N), 0)
        lane = iota((8, N), 1)
        one, zero = jnp.ones((), BF16), jnp.zeros((), BF16)
        code_place = lane // 16 == (sub + 3) % 8
        lane = iota((1, N), 1)
        filled = lane % SLOT < COLS
        upper = lane >= SLOT

        def fill(step, carry):
            group = groups - 1 - step
            group = jnp.where(group > last_group, group, group - 1)
            group = jnp.where(step == groups - 1, last_group, group)
            with jax.named_scope("columns_arrive"):
                settle(got1.at[pl.ds(0, 16)], r1.at[group])
            total = jnp.zeros((BANDS * BOX, 2 * PLANES * BOX), F32)
            for pair in range(8):
                senders = [wrap(me + grid_count - offset) for offset in far(8 * group + pair)]
                data = [got1[sender] for sender in senders]
                codes = pltpu.roll(jnp.concatenate(data, axis=0), 0, 1, stride=16, stride_axis=0)
                codes = jnp.where(code_place, codes, 0.0)
                picks, highs, lows = [], [], []
                for k in range(2):
                    code = jnp.sum(codes[4 * k : 4 * k + 4], axis=0, keepdims=True)
                    code = jnp.broadcast_to(code, (8, N))
                    turned = [pltpu.roll(code, 80, 1), pltpu.roll(code, 16, 1)]
                    code = jnp.where(upper, turned[1 - k], turned[k])[0:1]
                    code = code.astype(jnp.int32)
                    at_y = jnp.where(filled, (code // N) % BOX + jnp.where(upper, BOX, 0), -1)
                    at_z = jnp.where(filled, code % BOX, -1)
                    code_z[senders[k]] = at_z
                    picker = jnp.where(row_id == at_y.astype(F32).astype(BF16), one, zero)
                    oh_y[senders[k]] = picker
                    picks.append(picker)
                    high, rest = halves(data[k])
                    at = z_id16 == at_z.astype(F32).astype(BF16)
                    for value, store in ((high, highs), (rest, lows)):
                        store.append(
                            jnp.concatenate(
                                [jnp.where(at, value[r : r + 1], zero) for r in range(4)], axis=0
                            )
                        )
                pick = jnp.concatenate(picks, axis=1)
                total += mm(pick, jnp.concatenate(highs, axis=1), NT)
                total += mm(pick, jnp.concatenate(lows, axis=1), NT)
            box_ref[...] += total
            return carry

        lax.fori_loop(0, groups // 2, fill, 0)
        if band_count > 1:

            @pl.when(jnp.logical_not(early))
            def _():
                tell_group()

        settle(d_own.at[pl.ds(0, height - 1)], rd)

        def column(offset):
            return pl.ds(lax.rem(at_x + offset + width, width) * height, height)

        for i, offset in enumerate((2, 1, -1)):
            block = d_own.at[column(0)]
            target = 2 * (at_y * width + lax.rem(at_x + offset + width, width)) + core
            to_grid(block, block, sx.at[i], rx.at[i], target).start()

        def to_mate(block):
            to_grid(d_own.at[block], d_mate.at[block], sm, rm, 2 * chip + 1 - core).start()

        settle(d_rest.at[pl.ds(0, width - 1)], re)
        line = d_rest.at[pl.ds(at_y * width, width)]
        for step in range(1, height):
            other = lax.rem(at_y + step, height) * width + at_x
            to_grid(line, line, sg, rg, 2 * other + core).start()
        to_mate(column(0))
        lax.fori_loop(groups // 2, groups, fill, 0)

        if band_count > 1:

            @pl.when(early)
            def _():
                tell_group()

        box_hi, box_lo = halves(box_ref[...].T)
        turned = mm(box_hi, yt_ref[0]) + mm(box_lo, yt_ref[0]) + mm(box_hi, yt_ref[1])
        mid, end = PLANES * BOX, BANDS * N
        part_re = turned[:mid, :end] - turned[mid:, end:]
        part_im = turned[:mid, end:] + turned[mid:, :end]
        for plane in range(PLANES):
            here = slice(plane * BOX, (plane + 1) * BOX)
            value = jnp.concatenate([part_re[here], part_im[here]], axis=0)
            v_hi, v_lo = halves(value)
            wave = mm(zt_ref[0], v_hi) + mm(zt_ref[1], v_hi) + mm(zt_ref[0], v_lo)
            for part in range(2):
                for member in range(BANDS):
                    first = (part * BANDS + member) * N
                    field[first : first + N, plane * N : (plane + 1) * N] = wave[
                        part * N : (part + 1) * N, member * N : (member + 1) * N
                    ]

        dens_t = jnp.zeros((N, ROWS), F32)
        for member in range(BANDS):
            real = field[member * N : (member + 1) * N, :]
            imag = field[(BANDS + member) * N : (BANDS + member + 1) * N, :]
            dens_t += occ_ref[0, member] * (real * real + imag * imag)
        for plane in range(PLANES):
            dens_loc[plane * N : (plane + 1) * N, :] = dens_t[:, plane * N : (plane + 1) * N].T

        if band_count > 1:

            @pl.when(jnp.logical_not(early))
            def _():
                send_parts()

        f_hi, f_lo = halves(field[...])
        tiles[...] = mm(f_hi, row_pick[...]) + mm(f_lo, row_pick[...])

        def project(step, carry):
            found = []
            for k in range(2):
                values = proj_t[2 * step + k]
                for combo in range(COMBOS):
                    found.append(
                        jnp.sum(values * tiles[combo * N : (combo + 1) * N, :], axis=0, keepdims=True)
                    )
            coeff[pl.ds(pl.multiple_of(step * 8, 8), 8), :] = jnp.concatenate(found, axis=0)
            return carry

        coeff_copies = []
        for part in range(3):
            lax.fori_loop(3 * part, 3 * part + 3, project, 0)
            rows = pl.ds(24 * part, 24)
            coeff_copies.append(
                [
                    to_grid(
                        coeff.at[rows], near_coeff.at[i, rows], sc.at[i, part], rc.at[i, part], near[i]
                    )
                    for i in range(4)
                ]
            )
            for copy in coeff_copies[-1]:
                copy.start()

        for i in range(4):
            atom_copies[i].wait_recv()
            same[1 + i] = jnp.where(wide == near_atom[i].astype(F32), 1.0, 0.0).astype(BF16)
        if band_count > 1:

            @pl.when(early)
            def _():
                send_parts()

        for i, offset in ((1, 1), (2, -1), (0, 2)):
            settle(d_own.at[pl.ds(0, height)], rx.at[i])
            to_mate(column(-offset))
        settle(d_rest.at[pl.ds(0, half - width)], rg)
        rest_copy = to_grid(d_rest, rest_mate, sh, rh, 2 * chip + 1 - core)
        rest_copy.start()
        def gather_couplings(which, main, rest):
            for q in range(3):
                values = main[:, q] if q < 2 else rest[...]
                d_hi, d_lo = halves(values.reshape(half * ATOMS, N))
                pick = d_pick[which, q // 2]
                slots = mm(d_hi, pick, TN) + mm(d_lo, pick, TN)
                for lanes in range(2):
                    part = slots[:, lanes * N : (lanes + 1) * N]
                    rows = slice(q * N, (q + 1) * N)
                    d_slot[lanes, rows, :] = part if which == 0 else d_slot[lanes, rows, :] + part

        gather_couplings(0, d_own, d_rest)
        settle(d_mate, rm)
        rest_copy.wait_recv()
        gather_couplings(1, d_mate, rest_mate)

        if band_count > 1:

            @pl.when(late)
            def _():
                add_parts()

        c_hi, c_lo = halves(coeff[...])
        total = mm(c_hi, same[0], NT) + mm(c_lo, same[0], NT)
        for i in range(4):
            with jax.named_scope("coefficients_arrive"):
                for part in range(3):
                    coeff_copies[part][i].wait_recv()
            c_hi, c_lo = halves(near_coeff[i])
            total += mm(c_hi, same[1 + i], NT) + mm(c_lo, same[1 + i], NT)
        summed[...] = total

        d_slot[:, 3 * N :, :] = jnp.zeros((2, 24, N), F32)
        values = [jnp.zeros((24, PAIRS), F32) for _ in range(COMBOS)]
        for j in range(PROJ):
            part = jnp.concatenate(
                [
                    jnp.concatenate(
                        [d_slot[lanes, pl.ds(q * N + j, 8, stride=PROJ), :] for lanes in range(2)],
                        axis=1,
                    )
                    for q in range(3)
                ],
                axis=0,
            )
            for combo in range(COMBOS):
                row = j * COMBOS + combo
                values[combo] += part * summed[row : row + 1, :]
        for combo in range(COMBOS):
            applied[combo] = values[combo]

        depth = 32

        def spread_back(step, carry):
            first = pl.multiple_of(step * depth, depth)
            totals = [jnp.zeros((depth, PAIRS), F32) for _ in range(COMBOS)]
            for i in range(PROJ):
                values = proj_t[i, pl.ds(first, depth), :]
                for combo in range(COMBOS):
                    totals[combo] += values * applied[combo, 8 * (i // 7) + i % 7 : 8 * (i // 7) + i % 7 + 1, :]
            for combo in range(COMBOS):
                added[pl.ds(pl.multiple_of(combo * N + first, depth), depth), :] = totals[combo]
            return carry

        lax.fori_loop(0, N // depth, spread_back, 0)
        a_hi, a_lo = halves(added[...])
        projected = mm(a_hi, row_pick[...], NT) + mm(a_lo, row_pick[...], NT)
        for combo in range(COMBOS):
            here = slice(combo * N, (combo + 1) * N)
            h_ref[here, :] = vloc_t[...] * field[here, :] + projected[here]

        spectra = []
        for plane in range(PLANES):
            lanes = slice(plane * N, (plane + 1) * N)
            value = jnp.concatenate(
                [
                    jnp.concatenate(
                        [
                            h_ref[(part * BANDS + member) * N : (part * BANDS + member + 1) * N, lanes]
                            for member in range(BANDS)
                        ],
                        axis=1,
                    )
                    for part in range(2)
                ],
                axis=0,
            )
            v_hi, v_lo = halves(value)
            spectra.append(mm(zb_ref[0], v_hi) + mm(zb_ref[1], v_hi) + mm(zb_ref[0], v_lo))
        turned = jnp.concatenate(
            [spectra[plane][part * BOX : (part + 1) * BOX] for part in range(2) for plane in range(PLANES)],
            axis=0,
        )
        t_hi, t_lo = halves(turned)
        turned = mm(t_hi, yb_ref[0]) + mm(t_lo, yb_ref[0]) + mm(t_hi, yb_ref[1])
        end = BANDS * BOX
        final = jnp.concatenate(
            [turned[:mid, :end] + turned[mid:, end:], turned[mid:, :end] - turned[:mid, end:]], axis=0
        )
        q_hi, q_lo = halves(final)
        both = jnp.concatenate([q_hi, q_lo], axis=1)

        if band_count > 1:

            @pl.when(middle)
            def _():
                add_parts()

        batch = 16

        def take(targets):
            for first in range(0, batch, 2):
                two = targets[first : first + 2]
                pick = jnp.concatenate([oh_y[target] for target in two], axis=1)
                found = mm(both, jnp.concatenate([pick, pick], axis=0))
                for k, target in enumerate(two):
                    at = z_id == code_z[target]
                    msg2[target] = jnp.concatenate(
                        [
                            jnp.sum(
                                jnp.where(
                                    at, found[r * BOX : (r + 1) * BOX, k * N : (k + 1) * N], 0.0
                                ),
                                axis=0,
                                keepdims=True,
                            )
                            for r in range(4)
                        ],
                        axis=0,
                    )

        def partners(step):
            return [
                wrap(me + offset)
                for pair in range(batch // 2)
                for offset in far(batch // 2 * step + pair)
            ]

        def send2(target):
            to_grid(msg2.at[target], got2.at[me], s2, r2, target).start()

        def take_and_send(step, carry):
            targets = partners(step)
            take(targets)
            for target in targets:
                send2(target)
            return carry

        batches = grid_count // batch
        lax.fori_loop(0, batches // 2, take_and_send, 0)
        if band_count > 1:

            @pl.when(foremost)
            def _():
                add_parts()

        lax.fori_loop(batches // 2, batches - 1, take_and_send, 0)
        targets = partners(batches - 1)
        take(targets)
        for target in targets[:-1]:
            send2(target)
        own_back = pltpu.make_async_copy(msg2.at[me], got2.at[me], out_sem)
        own_back.start()

        if band_count > 1:

            settle(dens_full.at[pl.ds(0, ROWS - share)], rf)
        dens_out = pltpu.make_async_copy(dens_full, dens_hbm, in_sem.at[0])
        dens_out.start()
        settle(got2.at[pl.ds(0, peers)], r2)
        own_back.wait()

        dens_out.wait()
        settle(msg1.at[pl.ds(0, peers)], s1)
        settle(msg2.at[pl.ds(0, peers)], s2)
        settle(d_own.at[pl.ds(0, height - 1)], sd)
        settle(d_rest.at[pl.ds(0, width - 1)], se)
        settle(d_rest.at[pl.ds(0, half - width)], sg)
        rest_copy.wait_send()
        for i in range(3):
            settle(d_own.at[pl.ds(0, height)], sx.at[i])
        settle(d_mate, sm)
        for copies in [atom_copies] + coeff_copies:
            for copy in copies:
                copy.wait_send()
        if band_count > 1:
            settle(dens_part.at[pl.ds(0, band_count - 1)], sp)
            settle(dens_full.at[pl.ds(0, ROWS - share)], sf)
    return kernel


def finish(psi_ref, col_ref, table_ref, got_ref, dens_in, out_ref, dens_ref, work):
    back = got_ref[...].reshape(got_ref.shape[0] * 4, N).T
    b_hi, b_lo = halves(back)
    result = mm(b_hi, table_ref[0]) + mm(b_lo, table_ref[0]) + mm(b_hi, table_ref[1])
    dens_ref[...] = dens_in[...]
    work[...] = jnp.zeros_like(work)
    work[0:1, 0:COLS] = col_ref[...].astype(F32)
    codes = jnp.broadcast_to(work[0:1, :], (N, N)).T.astype(jnp.int32)[0:COLS]

    def signed(index):
        return jnp.where(index >= N // 2, index - N, index)

    fy, fz, fx = signed(codes // N), signed(codes % N), signed(iota((COLS, N), 1))
    kinetic = KINETIC * (fx * fx + fy * fy + fz * fz).astype(F32)
    for part in range(2):
        for member in range(BANDS):
            out_ref[part, member] = (
                result[member * SLOT : member * SLOT + COLS, part * N : (part + 1) * N]
                + kinetic * psi_ref[part, member]
            )


def solution(mesh):
    grid_count = mesh.shape["grid"]
    band_count = mesh.shape["band"]
    half = grid_count // 2
    constants = tables(grid_count)

    def step(psi_g, col_index, v_local, proj_values, pair_atom, pair_row, d_matrices, occupations):
        x_table, y_table, y_back, z_table, z_back = [jnp.asarray(t) for t in constants]
        hbm = pl.BlockSpec(memory_space=pl.ANY)
        dma = pltpu.SemaphoreType.DMA
        col_row = col_index.reshape(1, COLS)
        got, dens = pl.pallas_call(
            make_kernel(grid_count, band_count),
            out_shape=(
                jax.ShapeDtypeStruct((grid_count, 4, N), F32),
                jax.ShapeDtypeStruct((ROWS, N), F32),
            ),
            in_specs=[hbm] * 12 + [pl.BlockSpec(memory_space=pltpu.SMEM)],
            out_specs=(hbm, hbm),
            scratch_shapes=[
                pltpu.VMEM((2, BANDS, COLS, N), F32),
                pltpu.VMEM((1, COLS), jnp.int32),
                pltpu.VMEM((2, 2 * N, 2 * N), BF16),
                pltpu.VMEM((PROJ, ATOMS, PROJ), F32),
                pltpu.VMEM((1, PAIRS), jnp.int32),
                pltpu.VMEM((PLANES, N, N), F32),
                pltpu.VMEM((PROJ, PAIRS, N), F32),
                pltpu.VMEM((1, PAIRS), jnp.int32),
                pltpu.VMEM((2, BANDS * BOX, 2 * BANDS * N), BF16),
                pltpu.VMEM((2, 2 * N, 2 * BOX), BF16),
                pltpu.VMEM((2, 2 * BOX, 2 * N), BF16),
                pltpu.VMEM((2, BANDS * N, 2 * BANDS * BOX), BF16),
                pltpu.VMEM((PROJ, N, PAIRS), F32),
                pltpu.VMEM((BANDS * SLOT, 2 * N), F32),
                pltpu.VMEM((grid_count, 4, N), F32),
                pltpu.VMEM((grid_count, 4, N), F32),
                pltpu.VMEM((grid_count, 4, N), F32),
                pltpu.VMEM((grid_count, 1, N), jnp.int32),
                pltpu.VMEM((grid_count, BANDS * BOX, N), BF16),
                pltpu.VMEM((BANDS * BOX, 2 * PLANES * BOX), F32),
                pltpu.VMEM((COMBOS * N, ROWS), F32),
                pltpu.VMEM((COMBOS * N, PAIRS), F32),
                pltpu.VMEM((PROJ * COMBOS, PAIRS), F32),
                pltpu.VMEM((4, PROJ * COMBOS, PAIRS), F32),
                pltpu.VMEM((4, 1, PAIRS), jnp.int32),
                pltpu.VMEM((PAIRS, N), F32),
                pltpu.VMEM((N, ROWS), F32),
                pltpu.VMEM((half, 2, ATOMS, N), F32),
                pltpu.VMEM((half, 2, ATOMS, N), F32),
                pltpu.VMEM((half, ATOMS, N), F32),
                pltpu.VMEM((half, ATOMS, N), F32),
                pltpu.VMEM((2, 3 * N + 24, N), F32),
                pltpu.VMEM((3, ATOMS, N), F32),
                pltpu.VMEM((PROJ * COMBOS, PAIRS), F32),
                pltpu.VMEM((COMBOS, 24, PAIRS), F32),
                pltpu.VMEM((COMBOS * N, PAIRS), F32),
                pltpu.VMEM((COMBOS * N, ROWS), F32),
                pltpu.VMEM((ROWS, N), F32),
                pltpu.VMEM((band_count, ROWS // band_count, N), F32),
                pltpu.VMEM((ROWS, N), F32),
                pltpu.VMEM((8, N), F32),
                pltpu.VMEM((ROWS, PAIRS), BF16),
                pltpu.VMEM((2, 2, half * ATOMS, PAIRS), BF16),
                pltpu.VMEM((5, PAIRS, PAIRS), BF16),
                pltpu.SemaphoreType.REGULAR((grid_count // 16,)), pltpu.SemaphoreType.REGULAR,
                dma((12,)), dma, dma, dma((grid_count // 16,)), dma, dma, dma, dma, dma((3,)), dma((3,)), dma, dma, dma, dma, dma, dma, dma, dma,
                dma((4,)), dma((4,)), dma((4, 3)), dma((4, 3)), dma, dma, dma, dma,
            ],
            compiler_params=pltpu.CompilerParams(
                collective_id=0, has_side_effects=True, vmem_limit_bytes=60 << 20
            ),
        )(
            psi_g,
            col_row,
            x_table,
            d_matrices.transpose(1, 0, 2),
            pair_atom.reshape(1, PAIRS),
            v_local,
            proj_values.transpose(1, 0, 2),
            pair_row.reshape(1, PAIRS),
            y_table,
            z_table,
            z_back,
            y_back,
            occupations.reshape(1, BANDS),
        )
        out, dens = pl.pallas_call(
            finish,
            out_shape=(
                jax.ShapeDtypeStruct(psi_g.shape, F32),
                jax.ShapeDtypeStruct((ROWS, N), F32),
            ),
            in_specs=[pl.BlockSpec(memory_space=pltpu.VMEM)] * 5,
            out_specs=(pl.BlockSpec(memory_space=pltpu.VMEM),) * 2,
            scratch_shapes=[pltpu.VMEM((8, N), F32)],
            compiler_params=pltpu.CompilerParams(vmem_limit_bytes=60 << 20),
        )(psi_g, col_row, x_table, got, dens)
        return out, dens.reshape(PLANES, N, N)

    return jax.shard_map(
        step,
        mesh=mesh,
        in_specs=(
            P(None, "band", "grid", None),
            P("grid"),
            P("grid", None, None),
            P("grid", None, None),
            P("grid"),
            P("grid"),
            P("grid", None, None),
            P("band"),
        ),
        out_specs=(P(None, "band", "grid", None), P("grid", None, None)),
        check_vma=False,
    )
```

```python
import functools

import jax
import jax.numpy as jnp
import numpy as np
from jax import lax
from jax.experimental import pallas as pl
from jax.experimental.pallas import tpu as pltpu
from jax.sharding import PartitionSpec as P

MESH = pl.DeviceIdType.MESH
F32 = jnp.float32
BF16 = jnp.bfloat16
KINETIC = 0.0005

N = 128
BOX = 64
PLANES = 2
BANDS = 2
COLS = 48
SLOT = 64
PROJ = 18
PAIRS = 256
ATOMS = 8
COMBOS = 4
ROWS = PLANES * N


def split(table):
    high = table.astype(jnp.bfloat16)
    low = (table - high.astype(np.float64)).astype(jnp.bfloat16)
    return np.stack([high, low])


def tables(grid_count):
    scale = 1.0 / np.sqrt(N)
    pos = np.arange(N)
    box = np.arange(BOX)
    freq = np.where(box >= BOX // 2, box - BOX, box)

    def cos_sin(left, right):
        angle = 2.0 * np.pi / N * (np.outer(left, right) % N)
        return np.cos(angle) * scale, np.sin(angle) * scale

    cos_x, sin_x = cos_sin(pos, pos)
    x_table = np.zeros((grid_count, 2, PLANES, 2, N))
    cos_r = cos_x.reshape(grid_count, PLANES, N)
    sin_r = sin_x.reshape(grid_count, PLANES, N)
    x_table[:, 0, :, 0] = cos_r
    x_table[:, 0, :, 1] = -sin_r
    x_table[:, 1, :, 0] = sin_r
    x_table[:, 1, :, 1] = cos_r
    x_table = x_table.reshape(2 * N, 2 * N)
    cos_y, sin_y = cos_sin(freq, pos)
    y_table = np.zeros((BANDS, BOX, 2, BANDS, N))
    for band in range(BANDS):
        y_table[band, :, 0, band] = cos_y
        y_table[band, :, 1, band] = sin_y
    y_back = y_table.transpose(3, 4, 2, 0, 1).reshape(BANDS * N, 2 * BANDS * BOX)
    y_table = y_table.reshape(BANDS * BOX, 2 * BANDS * N)
    cos_z, sin_z = cos_sin(pos, freq)
    z_table = np.block([[cos_z, -sin_z], [sin_z, cos_z]])
    return [split(t) for t in (x_table, y_table, y_back, z_table, z_table.T)]


def halves(value):
    high = value.astype(BF16)
    low = (value - high.astype(F32)).astype(BF16)
    return high, low


def mm(left, right, dims=((1,), (0,))):
    return lax.dot_general(left, right, (dims, ((), ())), preferred_element_type=F32)


NT = ((1,), (1,))
TN = ((0,), (0,))


def iota(shape, dim):
    return lax.broadcasted_iota(jnp.int32, shape, dim)


def make_kernel(grid_count, band_count):
    peers = grid_count - 1
    half = grid_count // 2
    width = 4
    height = half // width

    def kernel(
        psi_in, col_in, xt_in, dmat_in, atom_in, vloc_in, proj_in, row_in, yt_in, zt_in, zb_in,
        yb_in, occ_ref,
        got2, dens_hbm,
        psi_ref, col_ref, xt_ref, dmat_ref, atom_ref, vloc_ref, proj_buf, row_ref, yt_ref, zt_ref,
        zb_ref, yb_ref, proj_t, psi_pad, msg1, got1, msg2, code_z, oh_y, box_ref,
        field, tiles, coeff, near_coeff, near_atom, atom_col, vloc_t,
        d_own, d_mate, d_rest, rest_mate, d_slot, d_send, summed, applied, added, h_ref,
        dens_loc, dens_part, dens_full, work, row_pick, d_pick, same,
        here, all_here, in_sem, out_sem, s1, r1, s2, r2, sd, rd, sx, rx, se, re, sg, rg, sh, rh, sm, rm, sa, ra, sc, rc, sp, rp, sf, rf,
    ):
        me = lax.axis_index("grid")
        band = lax.axis_index("band")
        core = lax.rem(me, 2)
        chip = me // 2
        at_x = lax.rem(chip, width)
        at_y = chip // width

        def to_grid(src, dst, send, recv, target):
            return pltpu.make_async_remote_copy(
                src_ref=src, dst_ref=dst, send_sem=send, recv_sem=recv,
                device_id={"grid": target}, device_id_type=MESH,
            )

        def to_band(src, dst, send, recv, target):
            return pltpu.make_async_remote_copy(
                src_ref=src, dst_ref=dst, send_sem=send, recv_sem=recv,
                device_id={"band": target}, device_id_type=MESH,
            )

        def settle(ref, sem):
            pltpu.make_async_copy(ref, ref, sem).wait()

        def wrap(index):
            return jnp.where(index >= grid_count, index - grid_count, index)

        def far(pair):
            return half + pair, half - 1 - pair

        barrier = pltpu.get_barrier_semaphore()
        envoy = 2
        is_envoy = me == envoy

        apart = wrap(me - envoy + grid_count)
        envoy_step = jnp.where(apart > half, 2 * (apart - half), 2 * (half - apart) - 1)
        last_group = jnp.where(apart == half, 0, envoy_step // 16)
        groups = grid_count // 16

        def greet(offset):
            target = wrap(me + offset)

            @pl.when(target != envoy)
            def _():
                pl.semaphore_signal(
                    barrier, inc=1, device_id={"grid": target}, device_id_type=MESH
                )

        inputs = [
            pltpu.make_async_copy(src, dst, in_sem.at[i])
            for i, (src, dst) in enumerate(
                [
                    (psi_in, psi_ref), (col_in, col_ref), (xt_in, xt_ref), (dmat_in, dmat_ref),
                    (atom_in, atom_ref), (vloc_in, vloc_ref), (proj_in, proj_buf),
                    (row_in, row_ref), (yt_in, yt_ref), (zt_in, zt_ref), (zb_in, zb_ref),
                    (yb_in, yb_ref),
                ]
            )
        ]
        for copy in inputs[:4]:
            copy.start()
        for pair in range(half):
            for offset in far(pair):
                if offset > 0:
                    greet(offset)
        for copy in inputs[4:]:
            copy.start()

        early = band < 3
        foremost = band < 3
        middle = band == 3
        late = band >= 4
        share = ROWS // band_count
        mine = pl.ds(pl.multiple_of(band * share, share), share)

        def tell_group():
            @pl.when(is_envoy)
            def _():
                pl.semaphore_wait(barrier, band_count - 1)

                def pass_on(offset, carry):
                    pl.semaphore_signal(
                        all_here, inc=1, device_id={"grid": wrap(me + offset)}, device_id_type=MESH
                    )
                    return carry

                lax.fori_loop(1, grid_count, pass_on, 0, unroll=9)

        def send_parts():
            @pl.when(jnp.logical_not(is_envoy))
            def _():
                pl.semaphore_wait(all_here, 1)

            def send_part(step, carry):
                target = jnp.where(step >= band, step + 1, step)
                first = pl.multiple_of(target * share, share)
                to_band(
                    dens_loc.at[pl.ds(first, share)], dens_part.at[band], sp, rp, target
                ).start()
                return carry

            lax.fori_loop(0, band_count - 1, send_part, 0)

        def add_parts():
            settle(dens_part.at[pl.ds(0, band_count - 1)], rp)
            dens_part[band] = dens_loc[mine, :]
            whole = dens_part[0]
            for other in range(1, band_count):
                whole += dens_part[other]
            dens_full[mine, :] = whole

            def send_full(step, carry):
                target = jnp.where(step >= band, step + 1, step)
                to_band(dens_full.at[mine], dens_full.at[mine], sf, rf, target).start()
                return carry

            lax.fori_loop(0, band_count - 1, send_full, 0)

        psi_pad[...] = jnp.zeros_like(psi_pad)
        for copy in inputs[:3]:
            copy.wait()
        for member in range(BANDS):
            for part in range(2):
                psi_pad[member * SLOT : member * SLOT + COLS, part * N : (part + 1) * N] = psi_ref[
                    part, member
                ]
        psi_hi, psi_lo = halves(psi_pad[...])
        spread = mm(xt_ref[0], psi_hi, NT) + mm(xt_ref[1], psi_hi, NT) + mm(xt_ref[0], psi_lo, NT)
        work[...] = jnp.zeros_like(work)
        work[0:1, 0:COLS] = col_ref[...].astype(F32)
        codes = jnp.broadcast_to(work[0:1, :], (8, N))
        sub = iota((8, N), 0) % 4
        lane = iota((8, N), 1)
        pattern = jnp.where(
            sub == 0,
            pltpu.roll(codes, 48, 1),
            jnp.where(sub == 1, pltpu.roll(codes, 32, 1), pltpu.roll(codes, 16, 1)),
        )
        pattern = jnp.where((lane >= COLS) & (lane < SLOT) & (sub < 3), pattern, 0.0)
        for pair in range(grid_count // 2):
            both = spread[8 * pair : 8 * pair + 8] + pattern
            msg1[2 * pair] = both[0:4]
            msg1[2 * pair + 1] = both[4:8]
        own_copy = pltpu.make_async_copy(msg1.at[me], got1.at[me], r1.at[grid_count // 16 - 1])
        own_copy.start()

        @pl.when(jnp.logical_not(is_envoy))
        def _():
            pl.semaphore_wait(barrier, peers)
            pl.semaphore_signal(
                here.at[last_group], inc=1, device_id={"grid": envoy}, device_id_type=MESH
            )

        def prepare():
            inputs[5].wait()
            for plane in range(PLANES):
                vloc_t[:, plane * N : (plane + 1) * N] = vloc_ref[plane].T
            atom_row = atom_ref[...].astype(F32)
            for part in range(2):
                atom_col[part * N : (part + 1) * N, :] = jnp.broadcast_to(
                    atom_row[:, part * N : (part + 1) * N], (N, N)
                ).T
            for copy in inputs[6:]:
                copy.wait()
            for i in range(PROJ):
                for part in range(2):
                    proj_t[i, :, part * N : (part + 1) * N] = proj_buf[i, part * N : (part + 1) * N, :].T

        inputs[4].wait()
        @pl.when(is_envoy)
        def _():
            prepare()

        for group in reversed(range(groups)):

            @pl.when(is_envoy)
            def _(group=group):
                pl.semaphore_wait(here.at[group], 16 if group < groups - 1 else 15)

            for pair in reversed(range(8 * group, 8 * group + 8)):
                for offset in reversed(far(pair)):
                    if offset > 0:
                        target = wrap(me + offset)
                        to_grid(
                            msg1.at[target], got1.at[me], s1, r1.at[group], target
                        ).start()

        if band_count > 1:

            @pl.when(is_envoy)
            def _():
                for step in range(1, band_count):
                    pl.semaphore_signal(
                        barrier, inc=1, device_id={"band": lax.rem(band + step, band_count)},
                        device_id_type=MESH,
                    )

        near = [lax.rem(me + off + grid_count, grid_count) for off in (1, -1, 2, -2)]
        atom_copies = [
            to_grid(atom_ref, near_atom.at[i], sa.at[i], ra.at[i], near[i]) for i in range(4)
        ]
        for copy in atom_copies:
            copy.start()

        inputs[3].wait()
        d_send[...] = jnp.zeros_like(d_send)
        for i in range(PROJ):
            first = (i % 7) * PROJ
            d_send[i // 7, :, first : first + PROJ] = dmat_ref[i]
        d_own[at_x * height + at_y] = d_send[0:2]
        d_rest[chip] = d_send[2]
        for step in range(1, height):
            other = lax.rem(at_y + step, height) * width + at_x
            to_grid(
                d_send.at[pl.ds(0, 2)], d_own.at[at_x * height + at_y], sd, rd, 2 * other + core
            ).start()
        for step in range(1, width):
            other = at_y * width + lax.rem(at_x + step, width)
            to_grid(d_send.at[2], d_rest.at[chip], se, re, 2 * other + core).start()

        @pl.when(jnp.logical_not(is_envoy))
        def _():
            prepare()

        atom_row = atom_ref[...].astype(F32)
        local_row = row_ref[...] - me * ROWS
        row_pick[...] = jnp.where(iota((ROWS, PAIRS), 0) == local_row, 1.0, 0.0).astype(BF16)
        atoms = atom_ref[...]
        place = iota((half * ATOMS, PAIRS), 0)
        slot = place // ATOMS
        for which in range(2):
            shift = (core if which == 0 else 1 - core) * ATOMS + place % ATOMS
            for order, holder in enumerate([(slot % height) * width + slot // height, slot]):
                d_pick[which, order] = jnp.where(
                    holder * (2 * ATOMS) + shift == atoms, 1.0, 0.0
                ).astype(BF16)
        wide = jnp.concatenate([atom_col[...], atom_col[...]], axis=1)
        same[0] = jnp.where(wide == atom_row, 1.0, 0.0).astype(BF16)

        box_ref[...] = jnp.zeros_like(box_ref)
        row_id = iota((BANDS * BOX, N), 0).astype(F32).astype(BF16)
        z_id = iota((BOX, N), 0)
        z_id16 = z_id.astype(F32).astype(BF16)
        sub = iota((8, N), 0)
        lane = iota((8, N), 1)
        one, zero = jnp.ones((), BF16), jnp.zeros((), BF16)
        code_place = lane // 16 == (sub + 3) % 8
        lane = iota((1, N), 1)
        filled = lane % SLOT < COLS
        upper = lane >= SLOT

        def fill(step, carry):
            group = groups - 1 - step
            group = jnp.where(group > last_group, group, group - 1)
            group = jnp.where(step == groups - 1, last_group, group)
            with jax.named_scope("columns_arrive"):
                settle(got1.at[pl.ds(0, 16)], r1.at[group])
            total = jnp.zeros((BANDS * BOX, 2 * PLANES * BOX), F32)
            for pair in range(8):
                senders = [wrap(me + grid_count - offset) for offset in far(8 * group + pair)]
                data = [got1[sender] for sender in senders]
                codes = pltpu.roll(jnp.concatenate(data, axis=0), 0, 1, stride=16, stride_axis=0)
                codes = jnp.where(code_place, codes, 0.0)
                picks, highs, lows = [], [], []
                for k in range(2):
                    code = jnp.sum(codes[4 * k : 4 * k + 4], axis=0, keepdims=True)
                    code = jnp.broadcast_to(code, (8, N))
                    turned = [pltpu.roll(code, 80, 1), pltpu.roll(code, 16, 1)]
                    code = jnp.where(upper, turned[1 - k], turned[k])[0:1]
                    code = code.astype(jnp.int32)
                    at_y = jnp.where(filled, (code // N) % BOX + jnp.where(upper, BOX, 0), -1)
                    at_z = jnp.where(filled, code % BOX, -1)
                    code_z[senders[k]] = at_z
                    picker = jnp.where(row_id == at_y.astype(F32).astype(BF16), one, zero)
                    oh_y[senders[k]] = picker
                    picks.append(picker)
                    high, rest = halves(data[k])
                    at = z_id16 == at_z.astype(F32).astype(BF16)
                    for value, store in ((high, highs), (rest, lows)):
                        store.append(
                            jnp.concatenate(
                                [jnp.where(at, value[r : r + 1], zero) for r in range(4)], axis=0
                            )
                        )
                pick = jnp.concatenate(picks, axis=1)
                total += mm(pick, jnp.concatenate(highs, axis=1), NT)
                total += mm(pick, jnp.concatenate(lows, axis=1), NT)
            box_ref[...] += total
            return carry

        lax.fori_loop(0, groups // 2, fill, 0)
        if band_count > 1:

            @pl.when(jnp.logical_not(early))
            def _():
                tell_group()

        lax.fori_loop(groups // 2, groups - 1, fill, 0)
        settle(d_own.at[pl.ds(0, height - 1)], rd)

        def column(offset):
            return pl.ds(lax.rem(at_x + offset + width, width) * height, height)

        for i, offset in enumerate((2, 1, -1)):
            block = d_own.at[column(0)]
            target = 2 * (at_y * width + lax.rem(at_x + offset + width, width)) + core
            to_grid(block, block, sx.at[i], rx.at[i], target).start()

        def to_mate(block):
            to_grid(d_own.at[block], d_mate.at[block], sm, rm, 2 * chip + 1 - core).start()

        settle(d_rest.at[pl.ds(0, width - 1)], re)
        line = d_rest.at[pl.ds(at_y * width, width)]
        for step in range(1, height):
            other = lax.rem(at_y + step, height) * width + at_x
            to_grid(line, line, sg, rg, 2 * other + core).start()
        to_mate(column(0))
        lax.fori_loop(groups - 1, groups, fill, 0)

        if band_count > 1:

            @pl.when(early)
            def _():
                tell_group()

        box_hi, box_lo = halves(box_ref[...].T)
        turned = mm(box_hi, yt_ref[0]) + mm(box_lo, yt_ref[0]) + mm(box_hi, yt_ref[1])
        mid, end = PLANES * BOX, BANDS * N
        part_re = turned[:mid, :end] - turned[mid:, end:]
        part_im = turned[:mid, end:] + turned[mid:, :end]
        for plane in range(PLANES):
            here = slice(plane * BOX, (plane + 1) * BOX)
            value = jnp.concatenate([part_re[here], part_im[here]], axis=0)
            v_hi, v_lo = halves(value)
            wave = mm(zt_ref[0], v_hi) + mm(zt_ref[1], v_hi) + mm(zt_ref[0], v_lo)
            for part in range(2):
                for member in range(BANDS):
                    first = (part * BANDS + member) * N
                    field[first : first + N, plane * N : (plane + 1) * N] = wave[
                        part * N : (part + 1) * N, member * N : (member + 1) * N
                    ]

        dens_t = jnp.zeros((N, ROWS), F32)
        for member in range(BANDS):
            real = field[member * N : (member + 1) * N, :]
            imag = field[(BANDS + member) * N : (BANDS + member + 1) * N, :]
            dens_t += occ_ref[0, member] * (real * real + imag * imag)
        for plane in range(PLANES):
            dens_loc[plane * N : (plane + 1) * N, :] = dens_t[:, plane * N : (plane + 1) * N].T

        if band_count > 1:

            @pl.when(jnp.logical_not(early))
            def _():
                send_parts()

        f_hi, f_lo = halves(field[...])
        tiles[...] = mm(f_hi, row_pick[...]) + mm(f_lo, row_pick[...])

        def project(step, carry):
            found = []
            for k in range(2):
                values = proj_t[2 * step + k]
                for combo in range(COMBOS):
                    found.append(
                        jnp.sum(values * tiles[combo * N : (combo + 1) * N, :], axis=0, keepdims=True)
                    )
            coeff[pl.ds(pl.multiple_of(step * 8, 8), 8), :] = jnp.concatenate(found, axis=0)
            return carry

        coeff_copies = []
        for part in range(3):
            lax.fori_loop(3 * part, 3 * part + 3, project, 0)
            rows = pl.ds(24 * part, 24)
            coeff_copies.append(
                [
                    to_grid(
                        coeff.at[rows], near_coeff.at[i, rows], sc.at[i, part], rc.at[i, part], near[i]
                    )
                    for i in range(4)
                ]
            )
            for copy in coeff_copies[-1]:
                copy.start()

        for i in range(4):
            atom_copies[i].wait_recv()
            same[1 + i] = jnp.where(wide == near_atom[i].astype(F32), 1.0, 0.0).astype(BF16)
        if band_count > 1:

            @pl.when(early)
            def _():
                send_parts()

        for i, offset in ((1, 1), (2, -1), (0, 2)):
            settle(d_own.at[pl.ds(0, height)], rx.at[i])
            to_mate(column(-offset))
        settle(d_rest.at[pl.ds(0, half - width)], rg)
        rest_copy = to_grid(d_rest, rest_mate, sh, rh, 2 * chip + 1 - core)
        rest_copy.start()
        def gather_couplings(which, main, rest):
            for q in range(3):
                values = main[:, q] if q < 2 else rest[...]
                d_hi, d_lo = halves(values.reshape(half * ATOMS, N))
                pick = d_pick[which, q // 2]
                slots = mm(d_hi, pick, TN) + mm(d_lo, pick, TN)
                for lanes in range(2):
                    part = slots[:, lanes * N : (lanes + 1) * N]
                    rows = slice(q * N, (q + 1) * N)
                    d_slot[lanes, rows, :] = part if which == 0 else d_slot[lanes, rows, :] + part

        gather_couplings(0, d_own, d_rest)
        settle(d_mate, rm)
        rest_copy.wait_recv()
        gather_couplings(1, d_mate, rest_mate)

        if band_count > 1:

            @pl.when(late)
            def _():
                add_parts()

        c_hi, c_lo = halves(coeff[...])
        total = mm(c_hi, same[0], NT) + mm(c_lo, same[0], NT)
        for i in range(4):
            with jax.named_scope("coefficients_arrive"):
                for part in range(3):
                    coeff_copies[part][i].wait_recv()
            c_hi, c_lo = halves(near_coeff[i])
            total += mm(c_hi, same[1 + i], NT) + mm(c_lo, same[1 + i], NT)
        summed[...] = total

        d_slot[:, 3 * N :, :] = jnp.zeros((2, 24, N), F32)
        values = [jnp.zeros((24, PAIRS), F32) for _ in range(COMBOS)]
        for j in range(PROJ):
            part = jnp.concatenate(
                [
                    jnp.concatenate(
                        [d_slot[lanes, pl.ds(q * N + j, 8, stride=PROJ), :] for lanes in range(2)],
                        axis=1,
                    )
                    for q in range(3)
                ],
                axis=0,
            )
            for combo in range(COMBOS):
                row = j * COMBOS + combo
                values[combo] += part * summed[row : row + 1, :]
        for combo in range(COMBOS):
            applied[combo] = values[combo]

        depth = 32

        def spread_back(step, carry):
            first = pl.multiple_of(step * depth, depth)
            totals = [jnp.zeros((depth, PAIRS), F32) for _ in range(COMBOS)]
            for i in range(PROJ):
                values = proj_t[i, pl.ds(first, depth), :]
                for combo in range(COMBOS):
                    totals[combo] += values * applied[combo, 8 * (i // 7) + i % 7 : 8 * (i // 7) + i % 7 + 1, :]
            for combo in range(COMBOS):
                added[pl.ds(pl.multiple_of(combo * N + first, depth), depth), :] = totals[combo]
            return carry

        lax.fori_loop(0, N // depth, spread_back, 0)
        a_hi, a_lo = halves(added[...])
        projected = mm(a_hi, row_pick[...], NT) + mm(a_lo, row_pick[...], NT)
        for combo in range(COMBOS):
            here = slice(combo * N, (combo + 1) * N)
            h_ref[here, :] = vloc_t[...] * field[here, :] + projected[here]

        spectra = []
        for plane in range(PLANES):
            lanes = slice(plane * N, (plane + 1) * N)
            value = jnp.concatenate(
                [
                    jnp.concatenate(
                        [
                            h_ref[(part * BANDS + member) * N : (part * BANDS + member + 1) * N, lanes]
                            for member in range(BANDS)
                        ],
                        axis=1,
                    )
                    for part in range(2)
                ],
                axis=0,
            )
            v_hi, v_lo = halves(value)
            spectra.append(mm(zb_ref[0], v_hi) + mm(zb_ref[1], v_hi) + mm(zb_ref[0], v_lo))
        turned = jnp.concatenate(
            [spectra[plane][part * BOX : (part + 1) * BOX] for part in range(2) for plane in range(PLANES)],
            axis=0,
        )
        t_hi, t_lo = halves(turned)
        turned = mm(t_hi, yb_ref[0]) + mm(t_lo, yb_ref[0]) + mm(t_hi, yb_ref[1])
        end = BANDS * BOX
        final = jnp.concatenate(
            [turned[:mid, :end] + turned[mid:, end:], turned[mid:, :end] - turned[:mid, end:]], axis=0
        )
        q_hi, q_lo = halves(final)
        both = jnp.concatenate([q_hi, q_lo], axis=1)

        if band_count > 1:

            @pl.when(middle)
            def _():
                add_parts()

        batch = 16

        def take(targets):
            for first in range(0, batch, 2):
                two = targets[first : first + 2]
                pick = jnp.concatenate([oh_y[target] for target in two], axis=1)
                found = mm(both, jnp.concatenate([pick, pick], axis=0))
                for k, target in enumerate(two):
                    at = z_id == code_z[target]
                    msg2[target] = jnp.concatenate(
                        [
                            jnp.sum(
                                jnp.where(
                                    at, found[r * BOX : (r + 1) * BOX, k * N : (k + 1) * N], 0.0
                                ),
                                axis=0,
                                keepdims=True,
                            )
                            for r in range(4)
                        ],
                        axis=0,
                    )

        def partners(step):
            return [
                wrap(me + offset)
                for pair in range(batch // 2)
                for offset in far(batch // 2 * step + pair)
            ]

        def send2(target):
            to_grid(msg2.at[target], got2.at[me], s2, r2, target).start()

        def take_and_send(step, carry):
            targets = partners(step)
            take(targets)
            for target in targets:
                send2(target)
            return carry

        batches = grid_count // batch
        lax.fori_loop(0, batches // 2, take_and_send, 0)
        if band_count > 1:

            @pl.when(foremost)
            def _():
                add_parts()

        lax.fori_loop(batches // 2, batches - 1, take_and_send, 0)
        targets = partners(batches - 1)
        take(targets)
        for target in targets[:-1]:
            send2(target)
        own_back = pltpu.make_async_copy(msg2.at[me], got2.at[me], out_sem)
        own_back.start()

        if band_count > 1:

            settle(dens_full.at[pl.ds(0, ROWS - share)], rf)
        dens_out = pltpu.make_async_copy(dens_full, dens_hbm, in_sem.at[0])
        dens_out.start()
        settle(got2.at[pl.ds(0, peers)], r2)
        own_back.wait()

        dens_out.wait()
        settle(msg1.at[pl.ds(0, peers)], s1)
        settle(msg2.at[pl.ds(0, peers)], s2)
        settle(d_own.at[pl.ds(0, height - 1)], sd)
        settle(d_rest.at[pl.ds(0, width - 1)], se)
        settle(d_rest.at[pl.ds(0, half - width)], sg)
        rest_copy.wait_send()
        for i in range(3):
            settle(d_own.at[pl.ds(0, height)], sx.at[i])
        settle(d_mate, sm)
        for copies in [atom_copies] + coeff_copies:
            for copy in copies:
                copy.wait_send()
        if band_count > 1:
            settle(dens_part.at[pl.ds(0, band_count - 1)], sp)
            settle(dens_full.at[pl.ds(0, ROWS - share)], sf)
    return kernel


def finish(psi_ref, col_ref, table_ref, got_ref, dens_in, out_ref, dens_ref, work):
    back = got_ref[...].reshape(got_ref.shape[0] * 4, N).T
    b_hi, b_lo = halves(back)
    result = mm(b_hi, table_ref[0]) + mm(b_lo, table_ref[0]) + mm(b_hi, table_ref[1])
    dens_ref[...] = dens_in[...]
    work[...] = jnp.zeros_like(work)
    work[0:1, 0:COLS] = col_ref[...].astype(F32)
    codes = jnp.broadcast_to(work[0:1, :], (N, N)).T.astype(jnp.int32)[0:COLS]

    def signed(index):
        return jnp.where(index >= N // 2, index - N, index)

    fy, fz, fx = signed(codes // N), signed(codes % N), signed(iota((COLS, N), 1))
    kinetic = KINETIC * (fx * fx + fy * fy + fz * fz).astype(F32)
    for part in range(2):
        for member in range(BANDS):
            out_ref[part, member] = (
                result[member * SLOT : member * SLOT + COLS, part * N : (part + 1) * N]
                + kinetic * psi_ref[part, member]
            )


def solution(mesh):
    grid_count = mesh.shape["grid"]
    band_count = mesh.shape["band"]
    half = grid_count // 2
    constants = tables(grid_count)

    def step(psi_g, col_index, v_local, proj_values, pair_atom, pair_row, d_matrices, occupations):
        x_table, y_table, y_back, z_table, z_back = [jnp.asarray(t) for t in constants]
        hbm = pl.BlockSpec(memory_space=pl.ANY)
        dma = pltpu.SemaphoreType.DMA
        col_row = col_index.reshape(1, COLS)
        got, dens = pl.pallas_call(
            make_kernel(grid_count, band_count),
            out_shape=(
                jax.ShapeDtypeStruct((grid_count, 4, N), F32),
                jax.ShapeDtypeStruct((ROWS, N), F32),
            ),
            in_specs=[hbm] * 12 + [pl.BlockSpec(memory_space=pltpu.SMEM)],
            out_specs=(hbm, hbm),
            scratch_shapes=[
                pltpu.VMEM((2, BANDS, COLS, N), F32),
                pltpu.VMEM((1, COLS), jnp.int32),
                pltpu.VMEM((2, 2 * N, 2 * N), BF16),
                pltpu.VMEM((PROJ, ATOMS, PROJ), F32),
                pltpu.VMEM((1, PAIRS), jnp.int32),
                pltpu.VMEM((PLANES, N, N), F32),
                pltpu.VMEM((PROJ, PAIRS, N), F32),
                pltpu.VMEM((1, PAIRS), jnp.int32),
                pltpu.VMEM((2, BANDS * BOX, 2 * BANDS * N), BF16),
                pltpu.VMEM((2, 2 * N, 2 * BOX), BF16),
                pltpu.VMEM((2, 2 * BOX, 2 * N), BF16),
                pltpu.VMEM((2, BANDS * N, 2 * BANDS * BOX), BF16),
                pltpu.VMEM((PROJ, N, PAIRS), F32),
                pltpu.VMEM((BANDS * SLOT, 2 * N), F32),
                pltpu.VMEM((grid_count, 4, N), F32),
                pltpu.VMEM((grid_count, 4, N), F32),
                pltpu.VMEM((grid_count, 4, N), F32),
                pltpu.VMEM((grid_count, 1, N), jnp.int32),
                pltpu.VMEM((grid_count, BANDS * BOX, N), BF16),
                pltpu.VMEM((BANDS * BOX, 2 * PLANES * BOX), F32),
                pltpu.VMEM((COMBOS * N, ROWS), F32),
                pltpu.VMEM((COMBOS * N, PAIRS), F32),
                pltpu.VMEM((PROJ * COMBOS, PAIRS), F32),
                pltpu.VMEM((4, PROJ * COMBOS, PAIRS), F32),
                pltpu.VMEM((4, 1, PAIRS), jnp.int32),
                pltpu.VMEM((PAIRS, N), F32),
                pltpu.VMEM((N, ROWS), F32),
                pltpu.VMEM((half, 2, ATOMS, N), F32),
                pltpu.VMEM((half, 2, ATOMS, N), F32),
                pltpu.VMEM((half, ATOMS, N), F32),
                pltpu.VMEM((half, ATOMS, N), F32),
                pltpu.VMEM((2, 3 * N + 24, N), F32),
                pltpu.VMEM((3, ATOMS, N), F32),
                pltpu.VMEM((PROJ * COMBOS, PAIRS), F32),
                pltpu.VMEM((COMBOS, 24, PAIRS), F32),
                pltpu.VMEM((COMBOS * N, PAIRS), F32),
                pltpu.VMEM((COMBOS * N, ROWS), F32),
                pltpu.VMEM((ROWS, N), F32),
                pltpu.VMEM((band_count, ROWS // band_count, N), F32),
                pltpu.VMEM((ROWS, N), F32),
                pltpu.VMEM((8, N), F32),
                pltpu.VMEM((ROWS, PAIRS), BF16),
                pltpu.VMEM((2, 2, half * ATOMS, PAIRS), BF16),
                pltpu.VMEM((5, PAIRS, PAIRS), BF16),
                pltpu.SemaphoreType.REGULAR((grid_count // 16,)), pltpu.SemaphoreType.REGULAR,
                dma((12,)), dma, dma, dma((grid_count // 16,)), dma, dma, dma, dma, dma((3,)), dma((3,)), dma, dma, dma, dma, dma, dma, dma, dma,
                dma((4,)), dma((4,)), dma((4, 3)), dma((4, 3)), dma, dma, dma, dma,
            ],
            compiler_params=pltpu.CompilerParams(
                collective_id=0, has_side_effects=True, vmem_limit_bytes=60 << 20
            ),
        )(
            psi_g,
            col_row,
            x_table,
            d_matrices.transpose(1, 0, 2),
            pair_atom.reshape(1, PAIRS),
            v_local,
            proj_values.transpose(1, 0, 2),
            pair_row.reshape(1, PAIRS),
            y_table,
            z_table,
            z_back,
            y_back,
            occupations.reshape(1, BANDS),
        )
        out, dens = pl.pallas_call(
            finish,
            out_shape=(
                jax.ShapeDtypeStruct(psi_g.shape, F32),
                jax.ShapeDtypeStruct((ROWS, N), F32),
            ),
            in_specs=[pl.BlockSpec(memory_space=pltpu.VMEM)] * 5,
            out_specs=(pl.BlockSpec(memory_space=pltpu.VMEM),) * 2,
            scratch_shapes=[pltpu.VMEM((8, N), F32)],
            compiler_params=pltpu.CompilerParams(vmem_limit_bytes=60 << 20),
        )(psi_g, col_row, x_table, got, dens)
        return out, dens.reshape(PLANES, N, N)

    return jax.shard_map(
        step,
        mesh=mesh,
        in_specs=(
            P(None, "band", "grid", None),
            P("grid"),
            P("grid", None, None),
            P("grid", None, None),
            P("grid"),
            P("grid"),
            P("grid", None, None),
            P("band"),
        ),
        out_specs=(P(None, "band", "grid", None), P("grid", None, None)),
        check_vma=False,
    )
```
